512 devices in a mesh: dp: 16 (over y, core), expert: 32 (over z, x).
Axes of the slice: x: 4, y: 8, z: 8, core: 2. Of those that a mesh axis runs over, the one named last changes fastest.
Arguments:
- tokens: bfloat16 [1024, 4096], P('expert', 'dp'), may hold values from -6 to 6
- out_grad: bfloat16 [1024, 4096], P('expert', 'dp'), may hold values from -6 to 6
- routes: int32 [1024, 8], P('expert'), may hold values from 0 to 31, all different within a row; in each aligned block of 32 rows (0 to 31, 32 to 63, ...) at most 12 rows name the same one
- route_weights: float32 [1024, 8], P('expert'), may hold values from 0.1 to 0.5
- gate_weight: bfloat16 [32, 4096, 768], P('expert', 'dp'), may hold values from -0.09375 to 0.09375
- up_weight: bfloat16 [32, 4096, 768], P('expert', 'dp'), may hold values from -0.09375 to 0.09375
- down_weight: bfloat16 [32, 768, 4096], P('expert', None, 'dp'), may hold values from -0.21875 to 0.21875
- sign_bits: int32 [32, 128], replicated, may hold values from 0 to 1
- partner: int32 [32], replicated, may hold values from 0 to 31, as said below
Outputs:
- gate_grad: bfloat16 [32, 4096, 768], P('expert', 'dp')
- up_grad: bfloat16 [32, 4096, 768], P('expert', 'dp')
- down_grad: bfloat16 [32, 768, 4096], P('expert', None, 'dp')
- input_grad: bfloat16 [1024, 4096], P('expert', 'dp')
The draws below stay inside these ranges and needn't reach their ends.
Inputs may be any that keep to these rules, and one draw needn't show every extreme that they name: `routes`: each row names 8 different experts; among the 32 rows of one expert-axis index no expert is named by more than 12 rows, a bound that some block reaches. partner[partner[e]] = e; partner[e] is e or differs from e in exactly one bit; every bit position of the expert number is used by some pair.
All inputs are finite; a program needn't handle non-finite values.
Results may differ from the reference program's by a relative error of at most 0.04.
Values may be sent and summed in bfloat16 or wider, within the bound.
No kernel may reach another device: no remote copies, remote signals or barrier semaphores. Data moves between devices by JAX's collectives and lax.ppermute only.
A program may use at most 64 MiB of HBM per device.

```python
import math
import jax
import jax.numpy as jnp
import numpy as np
from jax import lax

D = 4096
FF = 768
TOPK = 8
HBLOCK = 128
TOK_DEV = 32
EXPERTS = 32
CAP = 12
TOKENS = 1024
N_DP = 16
N_EXPERT = 32


def draw_partner(key, part):
    key = jax.random.fold_in(key, 7)
    expert_total = EXPERTS
    bit_count = expert_total.bit_length() - 1
    experts_iota = jnp.arange(expert_total, dtype=jnp.int32)
    offset_key, coin_key = jax.random.split(key)
    offset = jax.random.randint(offset_key, (), 0, expert_total, dtype=jnp.int32)
    partner = experts_iota
    paired = jnp.zeros((expert_total,), jnp.bool_)
    for bit_pos in range(bit_count):
        base_pair = 1 << bit_pos + 1 if bit_pos < bit_count - 1 else 1
        first_one = offset ^ base_pair
        second = first_one ^ 1 << bit_pos
        partner = jnp.where(experts_iota == first_one, second, partner)
        partner = jnp.where(experts_iota == second, first_one, partner)
        paired = paired | (experts_iota == first_one) | (experts_iota == second)
    for bit_pos in range(bit_count):
        flipped = experts_iota ^ 1 << bit_pos
        coin_flip = jax.random.randint(jax.random.fold_in(coin_key, bit_pos), (expert_total,), 0, 3) == 0
        vacant = jnp.logical_not(paired)
        low_side = experts_iota & 1 << bit_pos == 0
        chosen = vacant & vacant[flipped] & low_side & coin_flip
        take_now = chosen | chosen[flipped]
        partner = jnp.where(take_now, flipped, partner)
        paired = paired | take_now
    return partner.astype(jnp.int32)


def with_ends(array, own_key, least, top_value):
    place = [jax.random.randint(jax.random.fold_in(own_key, axis), (), 0, length) for axis, length in enumerate(array.shape)]
    longest = array.shape.index(max(array.shape))
    next_to = place[:longest] + [(place[longest] + 1) % array.shape[longest]] + place[longest + 1:]
    return array.at[tuple(place)].set(least).at[tuple(next_to)].set(top_value)


def block_levels(stream_key, dims, cuts, least, high):
    def one(position, shards_of):
        heights = jax.random.uniform(jax.random.fold_in(jax.random.fold_in(stream_key, 6), position), (shards_of,), jnp.float32, least / len(cuts), high / len(cuts))
        return jnp.repeat(jnp.exp(heights), dims[position] // shards_of).reshape((-1,) + (1,) * (len(dims) - position - 1))

    level = one(*cuts[0])
    for cut in cuts[1:]:
        level = level * one(*cut)
    return level


def routed_block(rng, own, number, rows, number_of, top, limit, slope):
    sequence = jax.random.permutation(rng, number_of)
    heavy_load, ordinary = load_shares(number_of, rows * top, limit, slope, True), load_shares(number_of, rows * top, limit, slope, False)
    places = jnp.arange(number_of)

    def named(lengths, turn):
        used = int((lengths > 0).sum())
        fixed = max(1, used // 4)
        passed = fixed + (places - fixed + turn * (used - fixed)) % max(1, number_of - fixed)
        return jnp.zeros((number_of,), jnp.int32).at[sequence[jnp.where(places < fixed, places, passed)]].set(jnp.asarray(lengths, jnp.int32))

    lengths = jnp.where(number % 4 == 0, named(heavy_load, number // 4), named(ordinary, number - number // 4 - 1))
    mixed = jax.random.permutation(jax.random.fold_in(own, 3), number_of)
    giver, receiver = mixed[0:number_of // 2 * 2:2], mixed[1:number_of // 2 * 2:2]
    slack = jnp.minimum(lengths[giver] - 1, limit - lengths[receiver]) // 2
    slack = jnp.where((giver == sequence[0]) | (receiver == sequence[0]) | (lengths[receiver] == 0), 0, jnp.maximum(slack, 0))
    passed = jax.random.randint(jax.random.fold_in(own, 4), (number_of // 2,), 0, 1 << 20) % (slack + 1)
    lengths = lengths.at[giver].add(-passed).at[receiver].add(passed)
    labels = jnp.searchsorted(jnp.cumsum(lengths), jnp.arange(rows * top), side="right").astype(jnp.int32)
    table = labels.reshape(top, rows).T
    table = table[jax.random.permutation(jax.random.fold_in(own, 1), rows)]
    turn = jax.random.randint(jax.random.fold_in(own, 2), (rows, 1), 0, top)
    return jnp.take_along_axis(table, (jnp.arange(top)[None, :] + turn) % top, axis=1)


def load_shares(count, total, most, lean, full):
    portions = [(1 << 20) // math.isqrt(grade ** lean) + 1 for grade in range(1, count + 1)]
    largest = most if full else min(most, max(-(-total // count), total * portions[0] // sum(portions)))
    least = 1 if total - largest >= count - 1 else 0
    holding, spare = [largest] + [least] * (count - 1), total - largest - least * (count - 1)
    while spare > 0:
        free = [i for i in range(1, count) if holding[i] < largest] or [i for i in range(1, count) if holding[i] < most]
        mass, left = sum([portions[i] for i in free]), spare
        for i in free:
            more = min(most - holding[i], max(1, left * portions[i] // mass), spare)
            holding[i] = holding[i] + more
            spare = spare - more
    return np.array(holding)


def bell_draw(own_key, shape, spread, bound, cuts=(), kind=jnp.bfloat16):
    entries = jax.random.normal(own_key, shape, jnp.float32) * spread
    if len(cuts) > 0:
        entries = block_levels(own_key, shape, cuts, -0.22, 0.18) * entries
    return jnp.clip(entries, min=-bound, max=bound).astype(kind)


def setup_inputs(seed: int = 0) -> dict:
    streams_of = jax.random.split(jax.random.key(seed), 10)
    tokens = bell_draw(streams_of[0], (TOKENS, D), 1.0, 6.0, ((0, 32), (1, 16)))
    out_grad = bell_draw(streams_of[1], (TOKENS, D), 1.0, 6.0, ((0, 32), (1, 16)))
    routes_keys = jax.random.split(jax.random.fold_in(streams_of[2], 1), TOKENS // TOK_DEV)
    routes_turns = jax.random.permutation(jax.random.fold_in(streams_of[2], 3), TOKENS // TOK_DEV)
    routes = jax.vmap(lambda own, number: routed_block(jax.random.fold_in(streams_of[2], 2), own, number, TOK_DEV, EXPERTS, TOPK, CAP, 2))(routes_keys, routes_turns).reshape((TOKENS, TOPK))
    route_weights = jnp.clip(0.1 + 0.4 * jax.random.uniform(streams_of[3], (TOKENS, TOPK), jnp.float32) ** block_levels(streams_of[3], (TOKENS, TOPK), ((0, 32),), -0.2, 0.2), 0.1, 0.5)
    gate_weight = bell_draw(streams_of[4], (EXPERTS, D, FF), D ** -0.5, 0.09375, ((0, 32), (1, 16)))
    up_weight = bell_draw(streams_of[5], (EXPERTS, D, FF), D ** -0.5, 0.09375, ((0, 32), (1, 16)))
    down_weight = bell_draw(streams_of[6], (EXPERTS, FF, D), FF ** -0.5, 0.21875, ((0, 32), (2, 16)))
    sign_bits = with_ends(jax.random.randint(streams_of[7], (EXPERTS, HBLOCK), 0, 2), jax.random.fold_in(streams_of[7], 1), 0, 1).astype(jnp.int32)
    partner = draw_partner(jax.random.fold_in(streams_of[9], 71), 0)
    return dict(tokens=tokens, out_grad=out_grad, routes=routes, route_weights=route_weights, gate_weight=gate_weight, up_weight=up_weight, down_weight=down_weight, sign_bits=sign_bits, partner=partner)


EPS = 1e-06
QSTEP = 2.0
TWO_PI = 2.0 * math.pi

def sylvester(block_len):
    positions = jnp.arange(block_len, dtype=jnp.int32)
    common_bits = positions[:, None] & positions[None, :]
    parity = jnp.zeros((block_len, block_len), jnp.int32)
    for bit_pos in range(block_len.bit_length() - 1):
        parity = parity ^ common_bits >> bit_pos & 1
    return (1 - 2 * parity).astype(jnp.float32)

def slot_tables(routes, weights, expert_count, capacity):
    experts_iota = jnp.arange(expert_count, dtype=jnp.int32)
    hit_table = (routes[:, :, None] == experts_iota[None, None, :]).astype(jnp.int32)
    member = lax.optimization_barrier(jnp.sum(hit_table, axis=1)).astype(jnp.int32)
    weight_sum = lax.optimization_barrier(jnp.sum(hit_table.astype(jnp.float32) * weights[:, :, None], axis=1))
    rank_table = (jnp.cumsum(member, axis=0) - member).astype(jnp.int32)
    cap_iota = jnp.arange(capacity, dtype=jnp.int32)
    placed = ((rank_table[:, :, None] == cap_iota[None, None, :]) & (member[:, :, None] == 1)).astype(jnp.float32)
    placed = jnp.transpose(placed, (1, 2, 0))
    slot_weight = jnp.einsum('ect,te->ec', placed, weight_sum, precision=lax.Precision.HIGHEST)
    return (placed, slot_weight)

def activation_grads(gate_sum, up_sum, hid_grad):
    sigmoid_val = jax.nn.sigmoid(gate_sum)
    silu_val = gate_sum * sigmoid_val
    hidden = (silu_val * up_sum).astype(jnp.bfloat16)
    gate_rows = (hid_grad * up_sum * sigmoid_val * (1.0 + gate_sum * (1.0 - sigmoid_val))).astype(jnp.bfloat16)
    up_rows = (hid_grad * silu_val).astype(jnp.bfloat16)
    return (hidden, gate_rows, up_rows)

def rotate_quant(operand, flip_signs, hadamard):
    row_count, col_count = operand.shape
    block_len = hadamard.shape[0]
    blocks = operand.astype(jnp.float32).reshape(row_count // block_len, block_len, col_count)
    signed = blocks * flip_signs[None, :, None]
    rotated = jnp.einsum('ij,bjc->bic', hadamard, signed, precision=lax.Precision.HIGHEST)
    meansq = lax.optimization_barrier(jnp.mean(rotated * rotated, axis=1, keepdims=True))
    scale_val = jnp.sqrt(meansq + EPS)
    steps_t = QSTEP * rotated / scale_val
    softened = (steps_t - jnp.sin(TWO_PI * steps_t) / TWO_PI) * scale_val / QSTEP
    return softened.astype(jnp.bfloat16).reshape(row_count, col_count)

def source_tables(src_routes, src_weights):
    return slot_tables(src_routes, src_weights, EXPERTS, CAP)

def partial_sum(split_rows, split_weight, form):
    parts = jnp.einsum(form, split_rows, split_weight, precision=lax.Precision.HIGHEST).astype(jnp.bfloat16)
    parts = lax.optimization_barrier(parts)
    return lax.optimization_barrier(jnp.sum(parts.astype(jnp.float32), axis=0))

def reference(tokens, out_grad, routes, route_weights, gate_weight, up_weight, down_weight, sign_bits, partner):
    row_total = N_EXPERT * CAP
    width_part = D // N_DP
    src_tokens = tokens.astype(jnp.float32).reshape(N_EXPERT, TOK_DEV, D)
    src_grads = out_grad.astype(jnp.float32).reshape(N_EXPERT, TOK_DEV, D)
    placed_all, weight_all = jax.vmap(source_tables)(routes.reshape(N_EXPERT, TOK_DEV, TOPK), route_weights.reshape(N_EXPERT, TOK_DEV, TOPK))
    hadamard = sylvester(HBLOCK)

    def per_expert(acc_grad, expert_id):
        place_e = lax.dynamic_index_in_dim(placed_all, expert_id, 1, keepdims=False)
        weight_e = lax.dynamic_index_in_dim(weight_all, expert_id, 1, keepdims=False)
        gate_e = lax.dynamic_index_in_dim(gate_weight, expert_id, 0, keepdims=False)
        up_e = lax.dynamic_index_in_dim(up_weight, expert_id, 0, keepdims=False)
        down_e = lax.dynamic_index_in_dim(down_weight, expert_id, 0, keepdims=False)
        sign_row = lax.dynamic_index_in_dim(sign_bits, expert_id, 0, keepdims=False)
        rows_in = jnp.einsum('sct,std->scd', place_e, src_tokens, precision=lax.Precision.HIGHEST)
        rows_in = rows_in.astype(jnp.bfloat16).reshape(row_total, D)
        rows_grad = jnp.einsum('sct,std->scd', place_e, src_grads, precision=lax.Precision.HIGHEST) * weight_e[:, :, None]
        rows_grad = rows_grad.astype(jnp.bfloat16).reshape(row_total, D)
        split_in = rows_in.astype(jnp.float32).reshape(row_total, N_DP, width_part)
        split_grad = rows_grad.astype(jnp.float32).reshape(row_total, N_DP, width_part)
        gate_sum = partial_sum(split_in, gate_e.astype(jnp.float32).reshape(N_DP, width_part, FF), 'rsd,sdf->srf')
        up_sum = partial_sum(split_in, up_e.astype(jnp.float32).reshape(N_DP, width_part, FF), 'rsd,sdf->srf')
        hid_grad = partial_sum(split_grad, down_e.astype(jnp.float32).reshape(FF, N_DP, width_part), 'rsd,fsd->srf')
        hidden, gate_rows, up_rows = activation_grads(gate_sum, up_sum, hid_grad)
        slot_back = jnp.dot(gate_rows, gate_e.T, preferred_element_type=jnp.float32) + jnp.dot(up_rows, up_e.T, preferred_element_type=jnp.float32)
        slot_back = slot_back.astype(jnp.bfloat16)
        flip_signs = (1 - 2 * sign_row).astype(jnp.float32)
        quant_in = rotate_quant(rows_in, flip_signs, hadamard)
        gate_new = (jnp.dot(quant_in.T, rotate_quant(gate_rows, flip_signs, hadamard), preferred_element_type=jnp.float32) * (1.0 / HBLOCK)).astype(jnp.bfloat16)
        up_new = (jnp.dot(quant_in.T, rotate_quant(up_rows, flip_signs, hadamard), preferred_element_type=jnp.float32) * (1.0 / HBLOCK)).astype(jnp.bfloat16)
        down_new = (jnp.dot(rotate_quant(hidden, flip_signs, hadamard).T, rotate_quant(rows_grad, flip_signs, hadamard), preferred_element_type=jnp.float32) * (1.0 / HBLOCK)).astype(jnp.bfloat16)
        returned_rows = slot_back.astype(jnp.float32).reshape(N_EXPERT, CAP, D)
        acc_grad = acc_grad + jnp.einsum('sct,scd->std', place_e, returned_rows, precision=lax.Precision.HIGHEST)
        return (acc_grad, (gate_new, up_new, down_new))
    start_grad = jnp.zeros((N_EXPERT, TOK_DEV, D), jnp.float32)
    summed_in, (gate_all, up_all, down_all) = lax.scan(per_expert, start_grad, jnp.arange(EXPERTS, dtype=jnp.int32))
    input_grad = summed_in.reshape(TOKENS, D).astype(jnp.bfloat16)
    return (jnp.take(gate_all, partner, axis=0), jnp.take(up_all, partner, axis=0), jnp.take(down_all, partner, axis=0), input_grad)
```

```python
import math

import jax
import jax.numpy as jnp
from jax import lax
from jax.sharding import Mesh
from jax.sharding import PartitionSpec as P

HBLOCK = 128
EPS = 1e-06
QSTEP = 2.0
TWO_PI = 2.0 * math.pi
BF16 = jnp.bfloat16
F32 = jnp.float32


def dot(left, right, left_dim, right_dim):
    return lax.dot_general(
        left, right, (((left_dim,), (right_dim,)), ((), ())), preferred_element_type=F32
    )


def sylvester(block_len):
    positions = jnp.arange(block_len, dtype=jnp.int32)
    common_bits = positions[:, None] & positions[None, :]
    parity = jnp.zeros((block_len, block_len), jnp.int32)
    for bit_pos in range(block_len.bit_length() - 1):
        parity = parity ^ common_bits >> bit_pos & 1
    return (1 - 2 * parity).astype(BF16)


def slot_tables(routes, weights, expert_count, capacity):
    experts_iota = jnp.arange(expert_count, dtype=jnp.int32)
    hit_table = (routes[:, :, None] == experts_iota[None, None, :]).astype(jnp.int32)
    member = jnp.sum(hit_table, axis=1)
    weight_sum = jnp.sum(hit_table.astype(F32) * weights[:, :, None], axis=1)
    rank_table = jnp.cumsum(member, axis=0) - member
    cap_iota = jnp.arange(capacity, dtype=jnp.int32)
    placed = (rank_table[:, :, None] == cap_iota[None, None, :]) & (member[:, :, None] == 1)
    placed = jnp.transpose(placed.astype(F32), (1, 2, 0))
    slot_weight = jnp.einsum("ect,te->ec", placed, weight_sum, precision=lax.Precision.HIGHEST)
    return placed, slot_weight


def rotate_quant_t(operand, rotation):
    cols, rows = operand.shape
    rotated = lax.dot_general(
        operand.reshape(cols, rows // HBLOCK, HBLOCK),
        rotation,
        (((2,), (0,)), ((), ())),
        preferred_element_type=F32,
    )
    scale = jnp.sqrt(jnp.mean(rotated * rotated, axis=2, keepdims=True) + EPS)
    steps = QSTEP * rotated / scale
    soft = (steps - jnp.sin(TWO_PI * steps) / TWO_PI) * scale / QSTEP
    return soft.astype(BF16).reshape(cols, rows)


def exchange(x, axis, apart):
    return lax.ppermute(x, axis, [(i, i ^ apart) for i in range(lax.axis_size(axis))])


def partner_swap(x, partner):
    count = lax.axis_size("expert")
    me = lax.axis_index("expert")
    apart = me ^ partner[me]
    bits = [1 << k for k in range(count.bit_length() - 1)]
    which = sum((apart == bit).astype(jnp.int32) * (k + 1) for k, bit in enumerate(bits))
    branches = [lambda v: v] + [lambda v, bit=bit: exchange(v, "expert", bit) for bit in bits]
    return lax.switch(which, branches, x)


def gather_y(x):
    count = lax.axis_size("y")
    copies = jnp.broadcast_to(x[None], (count,) + x.shape)
    return lax.all_to_all(copies, "y", 0, 0, tiled=True)


def shards(
    tokens, out_grad, routes, route_weights, gate_weight, up_weight, down_weight, sign_bits, partner
):
    experts = lax.axis_size("expert")
    n_y = lax.axis_size("y")
    core = lax.axis_index("core")
    tok_count, width = tokens.shape
    capacity = min(tok_count, tok_count * routes.shape[1] * 3 // (2 * experts))
    rows = experts * capacity
    gate_w, up_w, down_w = gate_weight[0], up_weight[0], down_weight[0]
    ff = gate_w.shape[1]
    half = ff // 2
    part = half // n_y

    placed, slot_weight = slot_tables(routes, route_weights, experts, capacity)
    picker = placed.astype(BF16)
    nothing = jnp.zeros_like(picker)
    pick_both = jnp.concatenate(
        [jnp.concatenate([picker, nothing], 2), jnp.concatenate([nothing, picker], 2)], 1
    )
    factor = jnp.concatenate([jnp.ones_like(slot_weight), slot_weight], 1)
    both = jnp.concatenate([tokens, out_grad], 0)
    send = jnp.einsum("ect,td->ecd", pick_both, both, preferred_element_type=F32)
    send = (send * factor[:, :, None]).astype(BF16)
    recv = lax.all_to_all(send, "expert", 0, 0, tiled=True)
    rows_in = recv[:, :capacity].reshape(rows, width)
    rows_grad = recv[:, capacity:].reshape(rows, width)

    def partials(which):
        start = which * half
        gate_part = dot(lax.dynamic_slice_in_dim(gate_w, start, half, 1), rows_in, 0, 1)
        up_part = dot(lax.dynamic_slice_in_dim(up_w, start, half, 1), rows_in, 0, 1)
        hid_part = dot(lax.dynamic_slice_in_dim(down_w, start, half, 0), rows_grad, 1, 1)
        return jnp.concatenate(
            [v.reshape(n_y, part, rows) for v in (gate_part, up_part, hid_part)], 1
        )

    away = partials(1 - core).astype(BF16)
    arrived = exchange(away, "core", 1)
    chip_sum = (partials(core) + arrived.astype(F32)).astype(BF16)
    blocks = lax.all_to_all(chip_sum, "y", 0, 0, tiled=True)
    sums = jnp.sum(blocks.astype(F32), axis=0)
    gate_sum, up_sum, hid_grad = sums[:part], sums[part : 2 * part], sums[2 * part :]

    me = lax.axis_index("expert")
    flip_signs = (1 - 2 * lax.dynamic_index_in_dim(sign_bits, me, 0, keepdims=False)).astype(BF16)
    rotation = sylvester(HBLOCK) * flip_signs[:, None]
    quant_rows = rotate_quant_t(jnp.concatenate([rows_in.T, rows_grad.T], 0), rotation)
    mate_rows = partner_swap(quant_rows, partner)
    mate_in, mate_grad = mate_rows[:width], mate_rows[width:]

    sig = jax.nn.sigmoid(gate_sum)
    silu = gate_sum * sig
    hidden = (silu * up_sum).astype(BF16)
    gate_rows = (hid_grad * up_sum * sig * (1.0 + gate_sum * (1.0 - sig))).astype(BF16)
    up_rows = (hid_grad * silu).astype(BF16)

    own = jnp.concatenate([gate_rows, up_rows], 0)
    own_half = gather_y(own)
    quant = rotate_quant_t(jnp.concatenate([gate_rows, up_rows, hidden], 0), rotation)
    mate_half = gather_y(partner_swap(quant, partner))

    def back(half_rows, which):
        start = which * half
        gate_t = half_rows[:, :part].reshape(half, rows)
        up_t = half_rows[:, part:].reshape(half, rows)
        return dot(gate_t, lax.dynamic_slice_in_dim(gate_w, start, half, 1), 0, 1) + dot(
            up_t, lax.dynamic_slice_in_dim(up_w, start, half, 1), 0, 1
        )

    own_other = exchange(own_half, "core", 1)
    slot_back = (back(own_half, core) + back(own_other, 1 - core)).astype(BF16)
    returned = lax.all_to_all(
        slot_back.reshape(experts, capacity, width), "expert", 0, 0, tiled=True
    )
    input_grad = jnp.einsum("ect,ecd->td", picker, returned, preferred_element_type=F32)

    mate_other = exchange(mate_half, "core", 1)
    low = jnp.where(core == 0, mate_half, mate_other)
    high = jnp.where(core == 0, mate_other, mate_half)

    def whole(k):
        cut = slice(k * part, (k + 1) * part)
        return jnp.concatenate([low[:, cut].reshape(half, rows), high[:, cut].reshape(half, rows)], 0)

    scale = 1.0 / HBLOCK
    gate_new = (dot(mate_in, whole(0), 1, 1) * scale).astype(BF16)
    up_new = (dot(mate_in, whole(1), 1, 1) * scale).astype(BF16)
    down_new = (dot(whole(2), mate_grad, 1, 1) * scale).astype(BF16)
    return gate_new[None], up_new[None], down_new[None], input_grad.astype(BF16)


def solution(mesh):
    n_dp, n_expert = mesh.shape["dp"], mesh.shape["expert"]
    split = Mesh(mesh.devices.reshape(n_dp // 2, 2, n_expert), ("y", "core", "expert"))
    dp = ("y", "core")
    return jax.shard_map(
        shards,
        mesh=split,
        in_specs=(
            P("expert", dp),
            P("expert", dp),
            P("expert", None),
            P("expert", None),
            P("expert", dp, None),
            P("expert", dp, None),
            P("expert", None, dp),
            P(),
            P(),
        ),
        out_specs=(
            P("expert", dp, None),
            P("expert", dp, None),
            P("expert", None, dp),
            P("expert", dp),
        ),
        check_vma=False,
    )
```

```python
import math

import jax
import jax.numpy as jnp
from jax import lax
from jax.sharding import Mesh
from jax.sharding import PartitionSpec as P

HBLOCK = 128
EPS = 1e-06
QSTEP = 2.0
TWO_PI = 2.0 * math.pi
BF16 = jnp.bfloat16
F32 = jnp.float32


def dot(left, right, left_dim, right_dim):
    return lax.dot_general(
        left, right, (((left_dim,), (right_dim,)), ((), ())), preferred_element_type=F32
    )


def sylvester(block_len):
    positions = jnp.arange(block_len, dtype=jnp.int32)
    common_bits = positions[:, None] & positions[None, :]
    parity = jnp.zeros((block_len, block_len), jnp.int32)
    for bit_pos in range(block_len.bit_length() - 1):
        parity = parity ^ common_bits >> bit_pos & 1
    return (1 - 2 * parity).astype(BF16)


def slot_tables(routes, weights, expert_count, capacity):
    experts_iota = jnp.arange(expert_count, dtype=jnp.int32)
    hit_table = (routes[:, :, None] == experts_iota[None, None, :]).astype(jnp.int32)
    member = jnp.sum(hit_table, axis=1)
    weight_sum = jnp.sum(hit_table.astype(F32) * weights[:, :, None], axis=1)
    rank_table = jnp.cumsum(member, axis=0) - member
    cap_iota = jnp.arange(capacity, dtype=jnp.int32)
    placed = (rank_table[:, :, None] == cap_iota[None, None, :]) & (member[:, :, None] == 1)
    placed = jnp.transpose(placed.astype(F32), (1, 2, 0))
    slot_weight = jnp.einsum("ect,te->ec", placed, weight_sum, precision=lax.Precision.HIGHEST)
    return placed, slot_weight


def rotate_quant_t(operand, rotation):
    cols, rows = operand.shape
    rotated = lax.dot_general(
        operand.reshape(cols, rows // HBLOCK, HBLOCK),
        rotation,
        (((2,), (0,)), ((), ())),
        preferred_element_type=F32,
    )
    scale = jnp.sqrt(jnp.mean(rotated * rotated, axis=2, keepdims=True) + EPS)
    steps = QSTEP * rotated / scale
    soft = (steps - jnp.sin(TWO_PI * steps) / TWO_PI) * scale / QSTEP
    return soft.astype(BF16).reshape(cols, rows)


def exchange(x, axis, apart):
    return lax.ppermute(x, axis, [(i, i ^ apart) for i in range(lax.axis_size(axis))])


def partner_swap(x, partner):
    count = lax.axis_size("expert")
    me = lax.axis_index("expert")
    apart = me ^ partner[me]
    bits = [1 << k for k in range(count.bit_length() - 1)]
    which = sum((apart == bit).astype(jnp.int32) * (k + 1) for k, bit in enumerate(bits))
    branches = [lambda v: v] + [lambda v, bit=bit: exchange(v, "expert", bit) for bit in bits]
    return lax.switch(which, branches, x)


def gather_y(x):
    count = lax.axis_size("y")
    copies = jnp.broadcast_to(x[None], (count,) + x.shape)
    return lax.all_to_all(copies, "y", 0, 0, tiled=True)


def gather_y_shifts(x):
    count = lax.axis_size("y")
    me = lax.axis_index("y")
    out = jnp.zeros((count,) + x.shape, x.dtype)
    out = lax.dynamic_update_index_in_dim(out, x, me, 0)
    for apart in sorted(range(1, count), key=lambda k: -min(k, count - k)):
        piece = lax.ppermute(x, "y", [(i, (i + apart) % count) for i in range(count)])
        out = lax.dynamic_update_index_in_dim(out, piece, (me - apart) % count, 0)
    return out


def shards(
    tokens, out_grad, routes, route_weights, gate_weight, up_weight, down_weight, sign_bits, partner
):
    experts = lax.axis_size("expert")
    n_y = lax.axis_size("y")
    core = lax.axis_index("core")
    tok_count, width = tokens.shape
    capacity = min(tok_count, tok_count * routes.shape[1] * 3 // (2 * experts))
    rows = experts * capacity
    gate_w, up_w, down_w = gate_weight[0], up_weight[0], down_weight[0]
    ff = gate_w.shape[1]
    half = ff // 2
    part = half // n_y

    placed, slot_weight = slot_tables(routes, route_weights, experts, capacity)
    picker = placed.astype(BF16)
    nothing = jnp.zeros_like(picker)
    pick_both = jnp.concatenate(
        [jnp.concatenate([picker, nothing], 2), jnp.concatenate([nothing, picker], 2)], 1
    )
    factor = jnp.concatenate([jnp.ones_like(slot_weight), slot_weight], 1)
    both = jnp.concatenate([tokens, out_grad], 0)
    send = jnp.einsum("ect,td->ecd", pick_both, both, preferred_element_type=F32)
    send = (send * factor[:, :, None]).astype(BF16)
    recv = lax.all_to_all(send, "expert", 0, 0, tiled=True)
    rows_in = recv[:, :capacity].reshape(rows, width)
    rows_grad = recv[:, capacity:].reshape(rows, width)

    def partials(which):
        start = which * half
        gate_part = dot(lax.dynamic_slice_in_dim(gate_w, start, half, 1), rows_in, 0, 1)
        up_part = dot(lax.dynamic_slice_in_dim(up_w, start, half, 1), rows_in, 0, 1)
        hid_part = dot(lax.dynamic_slice_in_dim(down_w, start, half, 0), rows_grad, 1, 1)
        return jnp.concatenate(
            [v.reshape(n_y, part, rows) for v in (gate_part, up_part, hid_part)], 1
        )

    away = partials(1 - core).astype(BF16)
    arrived = exchange(away, "core", 1)
    chip_sum = (partials(core) + arrived.astype(F32)).astype(BF16)
    blocks = lax.all_to_all(chip_sum, "y", 0, 0, tiled=True)

    me = lax.axis_index("expert")
    flip_signs = (1 - 2 * lax.dynamic_index_in_dim(sign_bits, me, 0, keepdims=False)).astype(BF16)
    rotation = sylvester(HBLOCK) * flip_signs[:, None]
    quant_rows = rotate_quant_t(jnp.concatenate([rows_in.T, rows_grad.T], 0), rotation)
    mate_rows = partner_swap(quant_rows, partner)

    blocks, mate_rows = lax.optimization_barrier((blocks, mate_rows))
    mate_in, mate_grad = mate_rows[:width], mate_rows[width:]
    sums = jnp.sum(blocks.astype(F32), axis=0)
    gate_sum, up_sum, hid_grad = sums[:part], sums[part : 2 * part], sums[2 * part :]

    sig = jax.nn.sigmoid(gate_sum)
    silu = gate_sum * sig
    hidden = (silu * up_sum).astype(BF16)
    gate_rows = (hid_grad * up_sum * sig * (1.0 + gate_sum * (1.0 - sig))).astype(BF16)
    up_rows = (hid_grad * silu).astype(BF16)

    own = jnp.concatenate([gate_rows, up_rows], 0)
    own_half = gather_y(own)
    quant = rotate_quant_t(jnp.concatenate([gate_rows, up_rows, hidden], 0), rotation)
    mate_half = gather_y_shifts(partner_swap(quant, partner))

    def back(half_rows, which):
        start = which * half
        gate_t = half_rows[:, :part].reshape(half, rows)
        up_t = half_rows[:, part:].reshape(half, rows)
        return dot(gate_t, lax.dynamic_slice_in_dim(gate_w, start, half, 1), 0, 1) + dot(
            up_t, lax.dynamic_slice_in_dim(up_w, start, half, 1), 0, 1
        )

    own_other = exchange(own_half, "core", 1)
    slot_back = (back(own_half, core) + back(own_other, 1 - core)).astype(BF16)
    returned = lax.all_to_all(
        slot_back.reshape(experts, capacity, width), "expert", 0, 0, tiled=True
    )
    input_grad = jnp.einsum("ect,ecd->td", picker, returned, preferred_element_type=F32)

    mate_other = exchange(mate_half, "core", 1)
    low = jnp.where(core == 0, mate_half, mate_other)
    high = jnp.where(core == 0, mate_other, mate_half)

    def whole(k):
        cut = slice(k * part, (k + 1) * part)
        return jnp.concatenate([low[:, cut].reshape(half, rows), high[:, cut].reshape(half, rows)], 0)

    scale = 1.0 / HBLOCK
    gate_new = (dot(mate_in, whole(0), 1, 1) * scale).astype(BF16)
    up_new = (dot(mate_in, whole(1), 1, 1) * scale).astype(BF16)
    down_new = (dot(whole(2), mate_grad, 1, 1) * scale).astype(BF16)
    return gate_new[None], up_new[None], down_new[None], input_grad.astype(BF16)


def solution(mesh):
    n_dp, n_expert = mesh.shape["dp"], mesh.shape["expert"]
    split = Mesh(mesh.devices.reshape(n_dp // 2, 2, n_expert), ("y", "core", "expert"))
    dp = ("y", "core")
    return jax.shard_map(
        shards,
        mesh=split,
        in_specs=(
            P("expert", dp),
            P("expert", dp),
            P("expert", None),
            P("expert", None),
            P("expert", dp, None),
            P("expert", dp, None),
            P("expert", None, dp),
            P(),
            P(),
        ),
        out_specs=(
            P("expert", dp, None),
            P("expert", dp, None),
            P("expert", None, dp),
            P("expert", dp),
        ),
        check_vma=False,
    )
```

```python
import math

import jax
import jax.numpy as jnp
from jax import lax
from jax.sharding import Mesh
from jax.sharding import PartitionSpec as P

HBLOCK = 128
EPS = 1e-06
QSTEP = 2.0
TWO_PI = 2.0 * math.pi
BF16 = jnp.bfloat16
F32 = jnp.float32


def dot(left, right, left_dim, right_dim):
    return lax.dot_general(
        left, right, (((left_dim,), (right_dim,)), ((), ())), preferred_element_type=F32
    )


def sylvester(block_len):
    positions = jnp.arange(block_len, dtype=jnp.int32)
    common_bits = positions[:, None] & positions[None, :]
    parity = jnp.zeros((block_len, block_len), jnp.int32)
    for bit_pos in range(block_len.bit_length() - 1):
        parity = parity ^ common_bits >> bit_pos & 1
    return (1 - 2 * parity).astype(BF16)


def slot_tables(routes, weights, expert_count, capacity):
    experts_iota = jnp.arange(expert_count, dtype=jnp.int32)
    hit_table = (routes[:, :, None] == experts_iota[None, None, :]).astype(jnp.int32)
    member = jnp.sum(hit_table, axis=1)
    weight_sum = jnp.sum(hit_table.astype(F32) * weights[:, :, None], axis=1)
    rank_table = jnp.cumsum(member, axis=0) - member
    cap_iota = jnp.arange(capacity, dtype=jnp.int32)
    placed = (rank_table[:, :, None] == cap_iota[None, None, :]) & (member[:, :, None] == 1)
    placed = jnp.transpose(placed.astype(F32), (1, 2, 0))
    slot_weight = jnp.einsum("ect,te->ec", placed, weight_sum, precision=lax.Precision.HIGHEST)
    return placed, slot_weight


def rotate_quant_t(operand, rotation):
    cols, rows = operand.shape
    rotated = lax.dot_general(
        operand.reshape(cols, rows // HBLOCK, HBLOCK),
        rotation,
        (((2,), (0,)), ((), ())),
        preferred_element_type=F32,
    )
    scale = jnp.sqrt(jnp.mean(rotated * rotated, axis=2, keepdims=True) + EPS)
    steps = QSTEP * rotated / scale
    soft = (steps - jnp.sin(TWO_PI * steps) / TWO_PI) * scale / QSTEP
    return soft.astype(BF16).reshape(cols, rows)


def exchange(x, axis, apart):
    return lax.ppermute(x, axis, [(i, i ^ apart) for i in range(lax.axis_size(axis))])


def partner_swap(x, partner):
    count = lax.axis_size("expert")
    me = lax.axis_index("expert")
    apart = me ^ partner[me]
    bits = [1 << k for k in range(count.bit_length() - 1)]
    which = sum((apart == bit).astype(jnp.int32) * (k + 1) for k, bit in enumerate(bits))
    branches = [lambda v: v] + [lambda v, bit=bit: exchange(v, "expert", bit) for bit in bits]
    return lax.switch(which, branches, x)


def gather_y(x):
    count = lax.axis_size("y")
    copies = jnp.broadcast_to(x[None], (count,) + x.shape)
    return lax.all_to_all(copies, "y", 0, 0, tiled=True)


def shards(
    tokens, out_grad, routes, route_weights, gate_weight, up_weight, down_weight, sign_bits, partner
):
    experts = lax.axis_size("expert")
    n_y = lax.axis_size("y")
    core = lax.axis_index("core")
    tok_count, width = tokens.shape
    capacity = min(tok_count, tok_count * routes.shape[1] * 3 // (2 * experts))
    rows = experts * capacity
    gate_w, up_w, down_w = gate_weight[0], up_weight[0], down_weight[0]
    ff = gate_w.shape[1]
    half = ff // 2
    part = half // n_y

    placed, slot_weight = slot_tables(routes, route_weights, experts, capacity)
    picker = placed.astype(BF16)
    nothing = jnp.zeros_like(picker)
    pick_both = jnp.concatenate(
        [jnp.concatenate([picker, nothing], 2), jnp.concatenate([nothing, picker], 2)], 1
    )
    factor = jnp.concatenate([jnp.ones_like(slot_weight), slot_weight], 1)
    both = jnp.concatenate([tokens, out_grad], 0)
    send = jnp.einsum("ect,td->ecd", pick_both, both, preferred_element_type=F32)
    send = (send * factor[:, :, None]).astype(BF16)
    recv = lax.all_to_all(send, "expert", 0, 0, tiled=True)
    rows_in = recv[:, :capacity].reshape(rows, width)
    rows_grad = recv[:, capacity:].reshape(rows, width)

    def partials(which):
        start = which * half
        gate_part = dot(lax.dynamic_slice_in_dim(gate_w, start, half, 1), rows_in, 0, 1)
        up_part = dot(lax.dynamic_slice_in_dim(up_w, start, half, 1), rows_in, 0, 1)
        hid_part = dot(lax.dynamic_slice_in_dim(down_w, start, half, 0), rows_grad, 1, 1)
        return jnp.concatenate(
            [v.reshape(n_y, part, rows) for v in (gate_part, up_part, hid_part)], 1
        )

    away = partials(1 - core).astype(BF16)
    arrived = exchange(away, "core", 1)
    chip_sum = (partials(core) + arrived.astype(F32)).astype(BF16)
    blocks = lax.all_to_all(chip_sum, "y", 0, 0, tiled=True)

    me = lax.axis_index("expert")
    flip_signs = (1 - 2 * lax.dynamic_index_in_dim(sign_bits, me, 0, keepdims=False)).astype(BF16)
    rotation = sylvester(HBLOCK) * flip_signs[:, None]
    quant_rows = rotate_quant_t(jnp.concatenate([rows_in.T, rows_grad.T], 0), rotation)
    mate_rows = partner_swap(quant_rows, partner)

    blocks, mate_rows = lax.optimization_barrier((blocks, mate_rows))
    mate_in, mate_grad = mate_rows[:width], mate_rows[width:]
    sums = jnp.sum(blocks.astype(F32), axis=0)
    gate_sum, up_sum, hid_grad = sums[:part], sums[part : 2 * part], sums[2 * part :]

    sig = jax.nn.sigmoid(gate_sum)
    silu = gate_sum * sig
    hidden = (silu * up_sum).astype(BF16)
    gate_rows = (hid_grad * up_sum * sig * (1.0 + gate_sum * (1.0 - sig))).astype(BF16)
    up_rows = (hid_grad * silu).astype(BF16)

    own = jnp.concatenate([gate_rows, up_rows], 0)
    own_half = gather_y(own)
    quant = rotate_quant_t(jnp.concatenate([gate_rows, up_rows, hidden], 0), rotation)
    mate_all = lax.all_gather(partner_swap(quant, partner), ("y", "core"))

    def back(half_rows, which):
        start = which * half
        gate_t = half_rows[:, :part].reshape(half, rows)
        up_t = half_rows[:, part:].reshape(half, rows)
        return dot(gate_t, lax.dynamic_slice_in_dim(gate_w, start, half, 1), 0, 1) + dot(
            up_t, lax.dynamic_slice_in_dim(up_w, start, half, 1), 0, 1
        )

    own_other = exchange(own_half, "core", 1)
    slot_back = (back(own_half, core) + back(own_other, 1 - core)).astype(BF16)
    returned = lax.all_to_all(
        slot_back.reshape(experts, capacity, width), "expert", 0, 0, tiled=True
    )
    input_grad = jnp.einsum("ect,ecd->td", picker, returned, preferred_element_type=F32)

    mate_all = mate_all.reshape(n_y, 2, 3, part, rows)

    def whole(k):
        return jnp.swapaxes(mate_all[:, :, k], 0, 1).reshape(ff, rows)

    scale = 1.0 / HBLOCK
    gate_new = (dot(mate_in, whole(0), 1, 1) * scale).astype(BF16)
    up_new = (dot(mate_in, whole(1), 1, 1) * scale).astype(BF16)
    down_new = (dot(whole(2), mate_grad, 1, 1) * scale).astype(BF16)
    return gate_new[None], up_new[None], down_new[None], input_grad.astype(BF16)


def solution(mesh):
    n_dp, n_expert = mesh.shape["dp"], mesh.shape["expert"]
    split = Mesh(mesh.devices.reshape(n_dp // 2, 2, n_expert), ("y", "core", "expert"))
    dp = ("y", "core")
    return jax.shard_map(
        shards,
        mesh=split,
        in_specs=(
            P("expert", dp),
            P("expert", dp),
            P("expert", None),
            P("expert", None),
            P("expert", dp, None),
            P("expert", dp, None),
            P("expert", None, dp),
            P(),
            P(),
        ),
        out_specs=(
            P("expert", dp, None),
            P("expert", dp, None),
            P("expert", None, dp),
            P("expert", dp),
        ),
        check_vma=False,
    )
```

```python
import jax
import jax.numpy as jnp
from jax import lax
from jax.sharding import Mesh
from jax.sharding import PartitionSpec as P

HBLOCK = 128
EPS = 1e-06
QSTEP = 2.0
SINE = (
    0.9999995827674866,
    -6.579691410064697,
    12.986429214477539,
    -12.18803596496582,
    6.557779312133789,
    -1.952649712562561,
)
BF16 = jnp.bfloat16
F32 = jnp.float32


def dot(left, right, left_dim, right_dim):
    return lax.dot_general(
        left, right, (((left_dim,), (right_dim,)), ((), ())), preferred_element_type=F32
    )


def sylvester(block_len):
    positions = jnp.arange(block_len, dtype=jnp.int32)
    common_bits = positions[:, None] & positions[None, :]
    parity = jnp.zeros((block_len, block_len), jnp.int32)
    for bit_pos in range(block_len.bit_length() - 1):
        parity = parity ^ common_bits >> bit_pos & 1
    return (1 - 2 * parity).astype(BF16)


def slot_tables(routes, weights, expert_count, capacity):
    experts_iota = jnp.arange(expert_count, dtype=jnp.int32)
    hit_table = (routes[:, :, None] == experts_iota[None, None, :]).astype(jnp.int32)
    member = jnp.sum(hit_table, axis=1)
    weight_sum = jnp.sum(hit_table.astype(F32) * weights[:, :, None], axis=1)
    rank_table = jnp.cumsum(member, axis=0) - member
    cap_iota = jnp.arange(capacity, dtype=jnp.int32)
    placed = (rank_table[:, :, None] == cap_iota[None, None, :]) & (member[:, :, None] == 1)
    placed = jnp.transpose(placed.astype(F32), (1, 2, 0))
    slot_weight = jnp.einsum("ect,te->ec", placed, weight_sum, precision=lax.Precision.HIGHEST)
    return placed, slot_weight


def soft_steps(rotated, meansq):
    scale = jnp.sqrt(meansq + EPS)
    steps = QSTEP * rotated / scale
    near = steps - jnp.round(steps)
    square = near * near
    series = jnp.full_like(near, SINE[-1])
    for term in SINE[-2::-1]:
        series = series * square + term
    return ((steps - near * series) * (scale / QSTEP)).astype(BF16)


def rotate_quant_t(operand, rotation):
    cols, rows = operand.shape
    rotated = lax.dot_general(
        operand.reshape(cols, rows // HBLOCK, HBLOCK),
        rotation,
        (((2,), (0,)), ((), ())),
        preferred_element_type=F32,
    )
    meansq = jnp.mean(rotated * rotated, axis=2, keepdims=True)
    return soft_steps(rotated, meansq).reshape(cols, rows)


def exchange(x, axis, apart):
    return lax.ppermute(x, axis, [(i, i ^ apart) for i in range(lax.axis_size(axis))])


def partner_swap(x, partner):
    count = lax.axis_size("expert")
    me = lax.axis_index("expert")
    apart = me ^ partner[me]
    bits = [1 << k for k in range(count.bit_length() - 1)]
    which = sum((apart == bit).astype(jnp.int32) * (k + 1) for k, bit in enumerate(bits))
    branches = [lambda v: v] + [lambda v, bit=bit: exchange(v, "expert", bit) for bit in bits]
    return lax.switch(which, branches, x)


def gather_y(x):
    count = lax.axis_size("y")
    copies = jnp.broadcast_to(x[None], (count,) + x.shape)
    return lax.all_to_all(copies, "y", 0, 0, tiled=True)


def shards(
    tokens, out_grad, routes, route_weights, gate_weight, up_weight, down_weight, sign_bits, partner
):
    experts = lax.axis_size("expert")
    n_y = lax.axis_size("y")
    core = lax.axis_index("core")
    tok_count, width = tokens.shape
    capacity = min(tok_count, tok_count * routes.shape[1] * 3 // (2 * experts))
    rows = experts * capacity
    gate_w, up_w, down_w = gate_weight[0], up_weight[0], down_weight[0]
    ff = gate_w.shape[1]
    half = ff // 2
    part = half // n_y

    placed, slot_weight = slot_tables(routes, route_weights, experts, capacity)
    picker = placed.astype(BF16)
    nothing = jnp.zeros_like(picker)
    pick_both = jnp.concatenate(
        [jnp.concatenate([picker, nothing], 2), jnp.concatenate([nothing, picker], 2)], 1
    )
    factor = jnp.concatenate([jnp.ones_like(slot_weight), slot_weight], 1)
    both = jnp.concatenate([tokens, out_grad], 0)
    send = jnp.einsum("ect,td->ecd", pick_both, both, preferred_element_type=F32)
    send = (send * factor[:, :, None]).astype(BF16)
    recv = lax.all_to_all(send, "expert", 0, 0, tiled=True)
    rows_in = recv[:, :capacity].reshape(rows, width)
    rows_grad = recv[:, capacity:].reshape(rows, width)

    def partials(which):
        start = which * half
        gate_part = dot(lax.dynamic_slice_in_dim(gate_w, start, half, 1), rows_in, 0, 1)
        up_part = dot(lax.dynamic_slice_in_dim(up_w, start, half, 1), rows_in, 0, 1)
        hid_part = dot(lax.dynamic_slice_in_dim(down_w, start, half, 0), rows_grad, 1, 1)
        return jnp.concatenate(
            [v.reshape(n_y, part, rows) for v in (gate_part, up_part, hid_part)], 1
        )

    away = partials(1 - core).astype(BF16)
    arrived = exchange(away, "core", 1)
    chip_sum = (partials(core) + arrived.astype(F32)).astype(BF16)
    blocks = lax.all_to_all(chip_sum, "y", 0, 0, tiled=True)
    mate_w = partner_swap(jnp.concatenate([gate_w, up_w], 0), partner)
    blocks, mate_w = lax.optimization_barrier((blocks, mate_w))
    sums = jnp.sum(blocks.astype(F32), axis=0)
    gate_sum, up_sum, hid_grad = sums[:part], sums[part : 2 * part], sums[2 * part :]

    sig = jax.nn.sigmoid(gate_sum)
    silu = gate_sum * sig
    hidden = silu * up_sum
    gate_rows = hid_grad * up_sum * sig * (1.0 + gate_sum * (1.0 - sig))
    up_rows = hid_grad * silu
    acts = jnp.concatenate([gate_rows, up_rows, hidden], 0).astype(BF16)
    mine = gather_y(partner_swap(acts, partner))
    mate_recv = partner_swap(recv, partner)
    mine, mate_recv = lax.optimization_barrier((mine, mate_recv))

    theirs = exchange(mine, "core", 1)
    low = jnp.where(core == 0, mine, theirs)
    high = jnp.where(core == 0, theirs, mine)

    def whole(k):
        cut = slice(k * part, (k + 1) * part)
        return jnp.concatenate([low[:, cut].reshape(half, rows), high[:, cut].reshape(half, rows)], 0)

    gate_t, up_t, hidden_t = whole(0), whole(1), whole(2)
    slot_back = (dot(gate_t, mate_w[:width], 0, 1) + dot(up_t, mate_w[width:], 0, 1)).astype(BF16)
    returned = lax.all_to_all(
        slot_back.reshape(experts, capacity, width), "expert", 0, 0, tiled=True
    )
    input_grad = jnp.einsum(
        "ect,ecd->td", jnp.take(picker, partner, axis=0), returned, preferred_element_type=F32
    )

    mate = partner[lax.axis_index("expert")]
    flip_signs = (1 - 2 * lax.dynamic_index_in_dim(sign_bits, mate, 0, keepdims=False)).astype(BF16)
    rotation = sylvester(HBLOCK) * flip_signs[:, None]
    mate_in = rotate_quant_t(mate_recv[:, :capacity].reshape(rows, width).T, rotation)
    mate_grad = rotate_quant_t(mate_recv[:, capacity:].reshape(rows, width).T, rotation)
    scale = 1.0 / HBLOCK
    gate_new = (dot(mate_in, rotate_quant_t(gate_t, rotation), 1, 1) * scale).astype(BF16)
    up_new = (dot(mate_in, rotate_quant_t(up_t, rotation), 1, 1) * scale).astype(BF16)
    down_new = (dot(rotate_quant_t(hidden_t, rotation), mate_grad, 1, 1) * scale).astype(BF16)
    return gate_new[None], up_new[None], down_new[None], input_grad.astype(BF16)


def solution(mesh):
    n_dp, n_expert = mesh.shape["dp"], mesh.shape["expert"]
    split = Mesh(mesh.devices.reshape(n_dp // 2, 2, n_expert), ("y", "core", "expert"))
    dp = ("y", "core")
    return jax.shard_map(
        shards,
        mesh=split,
        in_specs=(
            P("expert", dp),
            P("expert", dp),
            P("expert", None),
            P("expert", None),
            P("expert", dp, None),
            P("expert", dp, None),
            P("expert", None, dp),
            P(),
            P(),
        ),
        out_specs=(
            P("expert", dp, None),
            P("expert", dp, None),
            P("expert", None, dp),
            P("expert", dp),
        ),
        check_vma=False,
    )
```

```python
import functools

import jax
import jax.numpy as jnp
from jax import lax
from jax.experimental import pallas as pl
from jax.experimental.pallas import tpu as pltpu
from jax.sharding import Mesh
from jax.sharding import PartitionSpec as P

HBLOCK = 128
EPS = 1e-06
QSTEP = 2.0
SINE = (
    0.9999995827674866,
    -6.579691410064697,
    12.986429214477539,
    -12.18803596496582,
    6.557779312133789,
    -1.952649712562561,
)
BF16 = jnp.bfloat16
F32 = jnp.float32
BITS = ("b4", "b3", "b2", "b1", "b0")
VMEM_BYTES = 16 * 2**20


def dot(left, right, left_dim, right_dim):
    return lax.dot_general(
        left, right, (((left_dim,), (right_dim,)), ((), ())), preferred_element_type=F32
    )


def sylvester(block_len):
    positions = jnp.arange(block_len, dtype=jnp.int32)
    common_bits = positions[:, None] & positions[None, :]
    parity = jnp.zeros((block_len, block_len), jnp.int32)
    for bit_pos in range(block_len.bit_length() - 1):
        parity = parity ^ common_bits >> bit_pos & 1
    return (1 - 2 * parity).astype(BF16)


def pick_kernel(capacity, routes_ref, weights_ref, tok_ref, grad_ref, out_ref):
    choices, tok_count = routes_ref.shape
    block = 2 * capacity
    out_rows = out_ref.shape[0]
    experts = out_rows // block
    expert_ids = lax.broadcasted_iota(jnp.int32, (experts, tok_count), 0)
    member = jnp.zeros((experts, tok_count), F32)
    weight = jnp.zeros((experts, tok_count), F32)
    for k in range(choices):
        hit = routes_ref[k : k + 1, :] == expert_ids
        member = member + jnp.where(hit, 1.0, 0.0)
        weight = weight + jnp.where(hit, weights_ref[k : k + 1, :], 0.0)
    square = (tok_count, tok_count)
    earlier = lax.broadcasted_iota(jnp.int32, square, 0) < lax.broadcasted_iota(jnp.int32, square, 1)
    rank = dot(member.astype(BF16), jnp.where(earlier, 1.0, 0.0).astype(BF16), 1, 0)
    rank = jnp.where(member > 0.0, rank, -1.0).astype(BF16)
    weight_hi = weight.astype(BF16)
    weight_lo = (weight - weight_hi.astype(F32)).astype(BF16)

    row = lax.broadcasted_iota(jnp.int32, (out_rows, experts), 0)
    start = lax.broadcasted_iota(jnp.int32, (out_rows, experts), 1) * block
    owns = (row >= start) & (row < start + block)
    spread = jnp.where(owns, 1.0, 0.0).astype(BF16)
    place = jnp.sum(jnp.where(owns, row - start, 0).astype(F32), axis=1, keepdims=True)
    rank_of = dot(spread, rank, 1, 0)
    is_tok = place < capacity
    tok_pick = jnp.where(is_tok & (rank_of == place), 1.0, 0.0)
    grad_pick = jnp.where(jnp.logical_not(is_tok) & (rank_of == place - capacity), 1.0, 0.0)
    hi = (grad_pick * dot(spread, weight_hi, 1, 0)).astype(BF16)
    lo = (grad_pick * dot(spread, weight_lo, 1, 0)).astype(BF16)
    out = dot(tok_pick.astype(BF16), tok_ref[...], 1, 0)
    out = out + dot(hi, grad_ref[...], 1, 0) + dot(lo, grad_ref[...], 1, 0)
    out_ref[...] = out.astype(BF16)


def pick_rows(routes, weights, tokens, out_grad, experts, capacity):
    out_rows = 2 * capacity * experts
    out = pl.pallas_call(
        functools.partial(pick_kernel, capacity),
        out_shape=jax.ShapeDtypeStruct((out_rows, tokens.shape[1]), BF16),
        compiler_params=pltpu.CompilerParams(vmem_limit_bytes=VMEM_BYTES),
        name="pick_rows",
    )(routes.T, weights.T, tokens, out_grad)
    return out.reshape(experts, 2 * capacity, tokens.shape[1])


def partial_kernel(gate_up_ref, down_ref, in_ref, grad_ref, out_ref):
    cut = gate_up_ref.shape[0]
    out_ref[:cut, :] = dot(gate_up_ref[...], in_ref[...], 1, 1).astype(BF16)
    out_ref[cut:, :] = dot(down_ref[...], grad_ref[...], 1, 1).astype(BF16)


def partials_out(gate_up, down, rows_in, rows_grad):
    total = gate_up.shape[0] + down.shape[0]
    return pl.pallas_call(
        partial_kernel,
        out_shape=jax.ShapeDtypeStruct((total, rows_in.shape[0]), BF16),
        compiler_params=pltpu.CompilerParams(vmem_limit_bytes=VMEM_BYTES),
        name="partials_out",
    )(gate_up, down, rows_in, rows_grad)


def slot_picker(routes, expert_count, capacity):
    experts_iota = jnp.arange(expert_count, dtype=jnp.int32)
    member = jnp.sum((routes[:, :, None] == experts_iota[None, None, :]).astype(jnp.int32), axis=1)
    rank_table = jnp.cumsum(member, axis=0) - member
    cap_iota = jnp.arange(capacity, dtype=jnp.int32)
    placed = (rank_table[:, :, None] == cap_iota[None, None, :]) & (member[:, :, None] == 1)
    return jnp.transpose(placed.astype(BF16), (1, 2, 0))


def soft_steps(rotated, meansq):
    scale = jnp.sqrt(meansq + EPS)
    steps = QSTEP * rotated / scale
    near = steps - jnp.round(steps)
    square = near * near
    series = jnp.full_like(near, SINE[-1])
    for term in SINE[-2::-1]:
        series = series * square + term
    return ((steps - near * series) * (scale / QSTEP)).astype(BF16)


def rotate_quant_t(operand, rotation):
    cols, rows = operand.shape
    rotated = lax.dot_general(
        operand.reshape(cols, rows // HBLOCK, HBLOCK),
        rotation,
        (((2,), (0,)), ((), ())),
        preferred_element_type=F32,
    )
    meansq = jnp.mean(rotated * rotated, axis=2, keepdims=True)
    return soft_steps(rotated, meansq).reshape(cols, rows)


def pair_permute(x, axis):
    return lax.ppermute(x, axis, [(0, 1), (1, 0)])


def by_pair(which, alone, paired, *operands):
    branches = [alone] + [functools.partial(paired, axis) for axis in BITS[::-1]]
    return lax.switch(which, branches, *operands)


def swap(which, x):
    return by_pair(which, lambda v: v, lambda axis, v: pair_permute(v, axis), x)


def shards(
    tokens, out_grad, routes, route_weights, gate_weight, up_weight, down_weight, sign_bits, partner
):
    experts = lax.axis_size(BITS)
    n_y = lax.axis_size("y")
    core = lax.axis_index("core")
    me = lax.axis_index(BITS)
    mate = partner[me]
    apart = me ^ mate
    which = sum((apart == 1 << k).astype(jnp.int32) * (k + 1) for k in range(len(BITS)))
    tok_count, width = tokens.shape
    capacity = min(tok_count, tok_count * routes.shape[1] * 3 // (2 * experts))
    rows = experts * capacity
    ff = gate_weight.shape[2]
    half = ff // 2
    pieces = 2 * n_y
    unit = half // pieces

    send = pick_rows(routes, route_weights, tokens, out_grad, experts, capacity)
    recv = lax.all_to_all(send, BITS, 0, 0, tiled=True)

    gate_t = gate_weight[0].T.reshape(2, pieces, unit, width)
    up_t = up_weight[0].T.reshape(2, pieces, unit, width)
    gate_up = jnp.concatenate([gate_t, up_t], 2).reshape(2, ff, width)
    down = down_weight[0].reshape(2, half, width)
    gu_keep = lax.dynamic_index_in_dim(gate_up, core, 0, keepdims=False)
    gu_away = lax.dynamic_index_in_dim(gate_up, 1 - core, 0, keepdims=False)
    down_keep = lax.dynamic_index_in_dim(down, core, 0, keepdims=False)
    down_away = lax.dynamic_index_in_dim(down, 1 - core, 0, keepdims=False)
    mate_keep = swap(which, gu_keep)
    recv, mate_keep = lax.optimization_barrier((recv, mate_keep))
    rows_in = recv[:, :capacity].reshape(rows, width)
    rows_grad = recv[:, capacity:].reshape(rows, width)

    arrived = pair_permute(partials_out(gu_away, down_away, rows_in, rows_grad), "core")
    sum_gu = dot(gu_keep, rows_in, 1, 1) + arrived[:ff].astype(F32)
    sum_down = dot(down_keep, rows_grad, 1, 1) + arrived[ff:].astype(F32)
    chip_sum = jnp.concatenate(
        [sum_gu.reshape(pieces, 2 * unit, rows), sum_down.reshape(pieces, unit, rows)], 1
    ).astype(BF16)

    def spread_alone(x, w):
        merged = x.reshape(n_y, 2 * x.shape[1], rows)
        return lax.all_to_all(merged, "y", 0, 0, tiled=True).reshape(x.shape), w

    def spread_paired(axis, x, w):
        return lax.all_to_all(x, ("y", axis), 0, 0, tiled=True), pair_permute(w, axis)

    blocks, mate_away = by_pair(which, spread_alone, spread_paired, chip_sum, gu_away)
    sums = jnp.sum(blocks.reshape(n_y, 2, 3 * unit, rows).astype(F32), axis=0)
    gate_sum, up_sum, hid_grad = sums[:, :unit], sums[:, unit : 2 * unit], sums[:, 2 * unit :]
    sig = jax.nn.sigmoid(gate_sum)
    silu = gate_sum * sig
    hidden = silu * up_sum
    gate_rows = hid_grad * up_sum * sig * (1.0 + gate_sum * (1.0 - sig))
    up_rows = hid_grad * silu
    acts = jnp.concatenate([gate_rows, up_rows, hidden], 1).astype(BF16)

    def copies(x):
        return jnp.broadcast_to(x[None], (n_y,) + x.shape)

    def gather_alone(x, r):
        merged = copies(x).reshape(n_y, 2 * x.shape[1], rows)
        out = lax.all_to_all(merged, "y", 0, 0, tiled=True)
        return out.reshape(pieces, x.shape[1], rows), r

    def gather_paired(axis, x, r):
        out = copies(x[::-1]).reshape(pieces, x.shape[1], rows)
        return lax.all_to_all(out, ("y", axis), 0, 0, tiled=True), pair_permute(r, axis)

    mine, mate_recv = by_pair(which, gather_alone, gather_paired, acts, recv)

    theirs = pair_permute(mine, "core")

    def gate_up_rows(x):
        return x[:, : 2 * unit].reshape(ff, rows)

    slot_back = dot(gate_up_rows(mine), mate_keep, 0, 0) + dot(gate_up_rows(theirs), mate_away, 0, 0)
    returned = lax.all_to_all(
        slot_back.astype(BF16).reshape(experts, capacity, width), BITS, 0, 0, tiled=True
    )
    picker = jnp.take(slot_picker(routes, experts, capacity), partner, axis=0)
    input_grad = jnp.einsum("ect,ecd->td", picker, returned, preferred_element_type=F32)

    low = jnp.where(core == 0, mine, theirs)
    high = jnp.where(core == 0, theirs, mine)

    def whole(k):
        cut = slice(k * unit, (k + 1) * unit)
        return jnp.concatenate([low[:, cut].reshape(half, rows), high[:, cut].reshape(half, rows)], 0)

    flip_signs = (1 - 2 * lax.dynamic_index_in_dim(sign_bits, mate, 0, keepdims=False)).astype(BF16)
    rotation = sylvester(HBLOCK) * flip_signs[:, None]
    mate_in = rotate_quant_t(mate_recv[:, :capacity].reshape(rows, width).T, rotation)
    mate_grad = rotate_quant_t(mate_recv[:, capacity:].reshape(rows, width).T, rotation)
    scale = 1.0 / HBLOCK
    gate_new = (dot(mate_in, rotate_quant_t(whole(0), rotation), 1, 1) * scale).astype(BF16)
    up_new = (dot(mate_in, rotate_quant_t(whole(1), rotation), 1, 1) * scale).astype(BF16)
    down_new = (dot(rotate_quant_t(whole(2), rotation), mate_grad, 1, 1) * scale).astype(BF16)
    return gate_new[None], up_new[None], down_new[None], input_grad.astype(BF16)


def solution(mesh):
    n_dp = mesh.shape["dp"]
    split = Mesh(mesh.devices.reshape((n_dp // 2, 2) + (2,) * len(BITS)), ("y", "core") + BITS)
    dp = ("y", "core")
    return jax.shard_map(
        shards,
        mesh=split,
        in_specs=(
            P(BITS, dp),
            P(BITS, dp),
            P(BITS, None),
            P(BITS, None),
            P(BITS, dp, None),
            P(BITS, dp, None),
            P(BITS, None, dp),
            P(),
            P(),
        ),
        out_specs=(
            P(BITS, dp, None),
            P(BITS, dp, None),
            P(BITS, None, dp),
            P(BITS, dp),
        ),
        check_vma=False,
    )
```

```python
import functools

import jax
import jax.numpy as jnp
from jax import lax
from jax.experimental import pallas as pl
from jax.experimental.pallas import tpu as pltpu
from jax.sharding import Mesh
from jax.sharding import PartitionSpec as P

HBLOCK = 128
EPS = 1e-06
QSTEP = 2.0
SINE = (
    0.9999995827674866,
    -6.579691410064697,
    12.986429214477539,
    -12.18803596496582,
    6.557779312133789,
    -1.952649712562561,
)
BF16 = jnp.bfloat16
F32 = jnp.float32
BITS = ("b4", "b3", "b2", "b1", "b0")
VMEM_BYTES = 16 * 2**20


def dot(left, right, left_dim, right_dim):
    return lax.dot_general(
        left, right, (((left_dim,), (right_dim,)), ((), ())), preferred_element_type=F32
    )


def sylvester(block_len):
    positions = jnp.arange(block_len, dtype=jnp.int32)
    common_bits = positions[:, None] & positions[None, :]
    parity = jnp.zeros((block_len, block_len), jnp.int32)
    for bit_pos in range(block_len.bit_length() - 1):
        parity = parity ^ common_bits >> bit_pos & 1
    return (1 - 2 * parity).astype(BF16)


def pick_kernel(
    capacity, routes_in, weights_in, tok_in, grad_in, out_ref, routes_ref, weights_ref, tok_ref, grad_ref, sems
):
    loads = [
        pltpu.make_async_copy(src, dst, sems.at[k])
        for k, (src, dst) in enumerate(
            ((routes_in, routes_ref), (weights_in, weights_ref), (tok_in, tok_ref), (grad_in, grad_ref))
        )
    ]
    for load in loads:
        load.start()
    choices, tok_count = routes_ref.shape
    block = 2 * capacity
    out_rows = out_ref.shape[0]
    experts = out_rows // block

    row = lax.broadcasted_iota(jnp.int32, (out_rows, experts), 0)
    start = lax.broadcasted_iota(jnp.int32, (out_rows, experts), 1) * block
    owns = (row >= start) & (row < start + block)
    spread = jnp.where(owns, 1.0, 0.0).astype(BF16)
    place = jnp.sum(jnp.where(owns, row - start, 0).astype(F32), axis=1, keepdims=True)
    is_tok = place < capacity
    tok_place = jnp.where(is_tok, place, -2.0)
    grad_place = jnp.where(is_tok, -2.0, place - capacity)
    square = (tok_count, tok_count)
    earlier = lax.broadcasted_iota(jnp.int32, square, 0) < lax.broadcasted_iota(jnp.int32, square, 1)
    earlier = jnp.where(earlier, 1.0, 0.0).astype(BF16)
    expert_ids = lax.broadcasted_iota(jnp.int32, (experts, tok_count), 0)

    for load in loads:
        load.wait()
    member = jnp.zeros((experts, tok_count), F32)
    weight = jnp.zeros((experts, tok_count), F32)
    for k in range(choices):
        hit = routes_ref[k : k + 1, :] == expert_ids
        member = member + jnp.where(hit, 1.0, 0.0)
        weight = weight + jnp.where(hit, weights_ref[k : k + 1, :], 0.0)
    rank = dot(member.astype(BF16), earlier, 1, 0)
    rank = jnp.where(member > 0.0, rank, -1.0).astype(BF16)
    weight_hi = weight.astype(BF16)
    weight_lo = (weight - weight_hi.astype(F32)).astype(BF16)
    rank_of = dot(spread, rank, 1, 0)
    tok_pick = jnp.where(rank_of == tok_place, 1.0, 0.0).astype(BF16)
    grad_here = rank_of == grad_place
    hi = jnp.where(grad_here, dot(spread, weight_hi, 1, 0), 0.0).astype(BF16)
    lo = jnp.where(grad_here, dot(spread, weight_lo, 1, 0), 0.0).astype(BF16)
    out = dot(tok_pick, tok_ref[...], 1, 0)
    out = out + dot(hi, grad_ref[...], 1, 0) + dot(lo, grad_ref[...], 1, 0)
    out_ref[...] = out.astype(BF16)


def call(kernel, name, out_shapes, operands, scalars=0, in_hbm=False, scratch=()):
    smem = pl.BlockSpec(memory_space=pltpu.SMEM)
    rest = pl.BlockSpec(memory_space=pltpu.HBM) if in_hbm else pl.BlockSpec(memory_space=pltpu.VMEM)
    outs = [jax.ShapeDtypeStruct(shape, BF16) for shape in out_shapes]
    flops = 2 * 384 * 768 * 768
    moved = sum(v.size * 2 for v in list(operands) + outs)
    return pl.pallas_call(
        kernel,
        out_shape=outs,
        in_specs=[smem] * scalars + [rest] * (len(operands) - scalars),
        out_specs=[pl.BlockSpec(memory_space=pltpu.VMEM)] * len(outs),
        scratch_shapes=list(scratch),
        compiler_params=pltpu.CompilerParams(vmem_limit_bytes=VMEM_BYTES),
        cost_estimate=pl.CostEstimate(flops=flops, bytes_accessed=moved, transcendentals=0),
        name=name,
    )(*operands)


def pick_rows(routes, weights, tokens, out_grad, experts, capacity):
    operands = (routes.T, weights.T, tokens, out_grad)
    out = call(
        functools.partial(pick_kernel, capacity),
        "pick_rows",
        [(2 * capacity * experts, tokens.shape[1])],
        operands,
        in_hbm=True,
        scratch=[pltpu.VMEM(v.shape, v.dtype) for v in operands] + [pltpu.SemaphoreType.DMA((4,))],
    )[0]
    return out.reshape(experts, 2 * capacity, tokens.shape[1])


def side(which, size):
    return pl.ds(pl.multiple_of(which * size, size), size)


def away_kernel(core_ref, gate_ref, up_ref, down_ref, in_ref, grad_ref, out_ref):
    units, rows = out_ref.shape[0], in_ref.shape[0]
    cut = side(1 - core_ref[0], units)
    out_ref[:, :rows] = dot(gate_ref[cut, :], in_ref[...], 1, 1).astype(BF16)
    out_ref[:, rows : 2 * rows] = dot(up_ref[cut, :], in_ref[...], 1, 1).astype(BF16)
    out_ref[:, 2 * rows :] = dot(down_ref[cut, :], grad_ref[...], 1, 1).astype(BF16)


def keep_kernel(core_ref, gate_ref, up_ref, down_ref, in_ref, grad_ref, add_ref, out_ref):
    units, rows = out_ref.shape[0], in_ref.shape[0]
    cut = side(core_ref[0], units)

    def put(k, part):
        lanes = slice(k * rows, (k + 1) * rows)
        out_ref[:, lanes] = (part + add_ref[:, lanes].astype(F32)).astype(BF16)

    put(0, dot(gate_ref[cut, :], in_ref[...], 1, 1))
    put(1, dot(up_ref[cut, :], in_ref[...], 1, 1))
    put(2, dot(down_ref[cut, :], grad_ref[...], 1, 1))


def act_kernel(n_y, cross_ref, blocks_ref, out_ref):
    both = blocks_ref.shape[0] // n_y
    rows = blocks_ref.shape[1] // 3
    total = blocks_ref[:both, :].astype(F32)
    for k in range(1, n_y):
        total = total + blocks_ref[k * both : (k + 1) * both, :].astype(F32)
    gate_sum, up_sum, hid_grad = total[:, :rows], total[:, rows : 2 * rows], total[:, 2 * rows :]
    sig = 1.0 / (1.0 + jnp.exp(-gate_sum))
    silu = gate_sum * sig
    gate_rows = hid_grad * up_sum * sig * (1.0 + gate_sum * (1.0 - sig))
    acts = jnp.concatenate([gate_rows, hid_grad * silu, silu * up_sum], 1)
    turned = jnp.concatenate([acts[both // 2 :], acts[: both // 2]], 0)
    acts = jnp.where(cross_ref[0] > 0, turned, acts).astype(BF16)
    for k in range(n_y):
        out_ref[k * both : (k + 1) * both, :] = acts


def back_kernel(capacity, core_ref, mine_ref, theirs_ref, gate_ref, up_ref, out_ref):
    units, rows = mine_ref.shape[0], mine_ref.shape[1] // 3
    core = core_ref[0]
    total = jnp.zeros((gate_ref.shape[0], rows), F32)
    for ref, which in ((mine_ref, core), (theirs_ref, 1 - core)):
        cut = side(which, units)
        total = total + dot(gate_ref[:, cut], ref[:, :rows], 1, 0)
        total = total + dot(up_ref[:, cut], ref[:, rows : 2 * rows], 1, 0)
    padded = out_ref.shape[0] * capacity // rows
    shape = (out_ref.shape[0], rows)
    groups = rows // capacity
    row = lax.broadcasted_iota(jnp.int32, (out_ref.shape[0], groups), 0)
    start = lax.broadcasted_iota(jnp.int32, (out_ref.shape[0], groups), 1) * padded
    inside = (row >= start) & (row < start + capacity)
    shift = lax.broadcasted_iota(jnp.int32, (out_ref.shape[0], groups), 1) * (padded - capacity)
    source = jnp.sum(jnp.where(inside, row - shift + 1, 0).astype(F32), axis=1, keepdims=True) - 1.0
    column = lax.broadcasted_iota(jnp.int32, shape, 1).astype(F32)
    place = jnp.where(column == source, 1.0, 0.0).astype(BF16)
    out_ref[...] = dot(place, total.astype(BF16), 1, 1).astype(BF16)


def soft_rotate(block, rotation):
    rotated = dot(block, rotation, 1, 0)
    meansq = jnp.sum(rotated * rotated, axis=1, keepdims=True) * (1.0 / HBLOCK) + EPS
    steps = rotated * (QSTEP * lax.rsqrt(meansq))
    near = steps - jnp.round(steps)
    square = near * near
    series = square * SINE[-1] + SINE[-2]
    for term in SINE[-3::-1]:
        series = series * square + term
    return ((steps - near * series) * (jnp.sqrt(meansq) / QSTEP)).astype(BF16)


def grads_kernel(
    core_ref, mine_ref, theirs_ref, rows_ref, rotation_ref, gate_ref, up_ref, down_ref, in_q, grad_q, gate_q, up_q, hid_q
):
    units, rows = mine_ref.shape[0], mine_ref.shape[1] // 3
    width = in_q.shape[0]
    rotation = rotation_ref[...]
    core = core_ref[0]
    scale = 1.0 / HBLOCK
    for b in range(rows // HBLOCK):
        cut = slice(b * HBLOCK, (b + 1) * HBLOCK)
        in_q[:, cut] = soft_rotate(rows_ref[:width, cut], rotation)
        grad_q[:, cut] = soft_rotate(rows_ref[width:, cut], rotation)
    for ref, which in ((mine_ref, core), (theirs_ref, 1 - core)):
        place = side(which, units)
        for k, dst in enumerate((gate_q, up_q, hid_q)):
            for b in range(rows // HBLOCK):
                cut = slice(b * HBLOCK, (b + 1) * HBLOCK)
                lanes = slice(k * rows + b * HBLOCK, k * rows + (b + 1) * HBLOCK)
                dst[:, cut] = soft_rotate(ref[:, lanes], rotation)
        gate_ref[:, place] = (dot(in_q[...], gate_q[...], 1, 1) * scale).astype(BF16)
        up_ref[:, place] = (dot(in_q[...], up_q[...], 1, 1) * scale).astype(BF16)
        down_ref[place, :] = (dot(hid_q[...], grad_q[...], 1, 1) * scale).astype(BF16)


def slot_picker(routes, expert_count, capacity):
    experts_iota = jnp.arange(expert_count, dtype=jnp.int32)
    member = jnp.sum((routes[:, :, None] == experts_iota[None, None, :]).astype(jnp.int32), axis=1)
    rank_table = jnp.cumsum(member, axis=0) - member
    cap_iota = jnp.arange(capacity, dtype=jnp.int32)
    placed = (rank_table[:, :, None] == cap_iota[None, None, :]) & (member[:, :, None] == 1)
    return jnp.transpose(placed.astype(BF16), (1, 2, 0))


def pair_permute(x, axis):
    return lax.ppermute(x, axis, [(0, 1), (1, 0)])


def by_pair(which, alone, paired, *operands):
    branches = [alone] + [functools.partial(paired, axis) for axis in BITS[::-1]]
    return lax.switch(which, branches, *operands)


def swap(which, x):
    return by_pair(which, lambda v: v, lambda axis, v: pair_permute(v, axis), x)


def shards(
    tokens, out_grad, routes, route_weights, gate_weight, up_weight, down_weight, sign_bits, partner
):
    experts = lax.axis_size(BITS)
    n_y = lax.axis_size("y")
    core = lax.axis_index("core")
    me = lax.axis_index(BITS)
    mate = partner[me]
    apart = me ^ mate
    which = sum((apart == 1 << k).astype(jnp.int32) * (k + 1) for k in range(len(BITS)))
    tok_count, width = tokens.shape
    capacity = min(tok_count, tok_count * routes.shape[1] * 3 // (2 * experts))
    rows = experts * capacity
    ff = gate_weight.shape[2]
    half = ff // 2
    core_arg = core.astype(jnp.int32)[None]
    cross_arg = (which > 0).astype(jnp.int32)[None]

    gate_w, up_w, down_w = gate_weight[0], up_weight[0], down_weight[0]
    send = pick_rows(routes, route_weights, tokens, out_grad, experts, capacity)
    recv = lax.all_to_all(send, BITS, 0, 0, tiled=True)
    mate_gate = swap(which, gate_w)
    recv, mate_gate = lax.optimization_barrier((recv, mate_gate))
    rows_in = recv[:, :capacity].reshape(rows, width)
    rows_grad = recv[:, capacity:].reshape(rows, width)

    feeds = (core_arg, gate_w.T, up_w.T, down_w, rows_in, rows_grad)
    wide = (half, 3 * rows)
    away = call(away_kernel, "away_partials", [wide], feeds, 1)[0]
    arrived = pair_permute(away, "core")
    chip_sum = call(keep_kernel, "keep_partials", [wide], feeds + (arrived,), 1)[0]

    def over_y(x):
        return lax.all_to_all(x.reshape(n_y, half // n_y, 3 * rows), "y", 0, 0, tiled=True).reshape(wide)

    def over_pair(axis, x):
        cut = x.reshape(2 * n_y, half // (2 * n_y), 3 * rows)
        return lax.all_to_all(cut, ("y", axis), 0, 0, tiled=True).reshape(wide)

    def with_swap(x, v):
        return by_pair(
            which,
            lambda x, v: (over_y(x), v),
            lambda axis, x, v: (over_pair(axis, x), pair_permute(v, axis)),
            x,
            v,
        )

    blocks, mate_up = with_swap(chip_sum, up_w)

    acts = call(functools.partial(act_kernel, n_y), "activation", [wide], (cross_arg, blocks), 1)[0]
    mine, mate_recv = with_swap(acts, recv)
    theirs = pair_permute(mine, "core")

    padded = -(-capacity // 16) * 16
    slot_back = call(
        functools.partial(back_kernel, capacity),
        "slot_back",
        [(experts * padded, width)],
        (core_arg, mine, theirs, mate_gate, mate_up),
        1,
    )[0]
    returned = lax.all_to_all(slot_back.reshape(experts, padded, width), BITS, 0, 0, tiled=True)
    picker = jnp.take(slot_picker(routes, experts, capacity), partner, axis=0)
    picker = jnp.pad(picker, ((0, 0), (0, padded - capacity), (0, 0))).reshape(experts * padded, tok_count)
    input_grad = dot(picker, returned.reshape(experts * padded, width), 0, 0).astype(BF16)

    flip_signs = (1 - 2 * lax.dynamic_index_in_dim(sign_bits, mate, 0, keepdims=False)).astype(BF16)
    rotation = sylvester(HBLOCK) * flip_signs[:, None]
    mate_rows = jnp.concatenate(
        [mate_recv[:, :capacity].reshape(rows, width).T, mate_recv[:, capacity:].reshape(rows, width).T], 0
    )
    gate_new, up_new, down_new = call(
        grads_kernel,
        "weight_grads",
        [(width, ff), (width, ff), (ff, width)],
        (core_arg, mine, theirs, mate_rows, rotation),
        1,
        scratch=[pltpu.VMEM((n, rows), BF16) for n in (width, width, half, half, half)],
    )
    return gate_new[None], up_new[None], down_new[None], input_grad


def solution(mesh):
    n_dp = mesh.shape["dp"]
    split = Mesh(mesh.devices.reshape((n_dp // 2, 2) + (2,) * len(BITS)), ("y", "core") + BITS)
    dp = ("y", "core")
    return jax.shard_map(
        shards,
        mesh=split,
        in_specs=(
            P(BITS, dp),
            P(BITS, dp),
            P(BITS, None),
            P(BITS, None),
            P(BITS, dp, None),
            P(BITS, dp, None),
            P(BITS, None, dp),
            P(),
            P(),
        ),
        out_specs=(
            P(BITS, dp, None),
            P(BITS, dp, None),
            P(BITS, None, dp),
            P(BITS, dp),
        ),
        check_vma=False,
    )
```

```python
import functools

import jax
import jax.numpy as jnp
from jax import lax
from jax.experimental import pallas as pl
from jax.experimental.pallas import tpu as pltpu
from jax.sharding import Mesh
from jax.sharding import PartitionSpec as P

HBLOCK = 128
EPS = 1e-06
QSTEP = 2.0
SINE = (
    0.9999995827674866,
    -6.579691410064697,
    12.986429214477539,
    -12.18803596496582,
    6.557779312133789,
    -1.952649712562561,
)
BF16 = jnp.bfloat16
F32 = jnp.float32
BITS = ("b4", "b3", "b2", "b1", "b0")
VMEM_BYTES = 16 * 2**20
ALL_VMEM = 60 * 2**20


def dot(left, right, left_dim, right_dim):
    return lax.dot_general(
        left, right, (((left_dim,), (right_dim,)), ((), ())), preferred_element_type=F32
    )


def sylvester(block_len):
    positions = jnp.arange(block_len, dtype=jnp.int32)
    common_bits = positions[:, None] & positions[None, :]
    parity = jnp.zeros((block_len, block_len), jnp.int32)
    for bit_pos in range(block_len.bit_length() - 1):
        parity = parity ^ common_bits >> bit_pos & 1
    return (1 - 2 * parity).astype(BF16)


def pick_kernel(
    capacity, routes_in, weights_in, tok_in, grad_in, out_ref, routes_ref, weights_ref, tok_ref, grad_ref, sems
):
    loads = [
        pltpu.make_async_copy(src, dst, sems.at[k])
        for k, (src, dst) in enumerate(
            ((routes_in, routes_ref), (weights_in, weights_ref), (tok_in, tok_ref), (grad_in, grad_ref))
        )
    ]
    for load in loads:
        load.start()
    choices, tok_count = routes_ref.shape
    block = 2 * capacity
    out_rows = out_ref.shape[0]
    experts = out_rows // block

    row = lax.broadcasted_iota(jnp.int32, (out_rows, experts), 0)
    start = lax.broadcasted_iota(jnp.int32, (out_rows, experts), 1) * block
    owns = (row >= start) & (row < start + block)
    spread = jnp.where(owns, 1.0, 0.0).astype(BF16)
    place = jnp.sum(jnp.where(owns, row - start, 0).astype(F32), axis=1, keepdims=True)
    is_tok = place < capacity
    tok_place = jnp.where(is_tok, place, -2.0)
    grad_place = jnp.where(is_tok, -2.0, place - capacity)
    square = (tok_count, tok_count)
    earlier = lax.broadcasted_iota(jnp.int32, square, 0) < lax.broadcasted_iota(jnp.int32, square, 1)
    earlier = jnp.where(earlier, 1.0, 0.0).astype(BF16)
    expert_ids = lax.broadcasted_iota(jnp.int32, (experts, tok_count), 0)

    for load in loads:
        load.wait()
    member = jnp.zeros((experts, tok_count), F32)
    weight = jnp.zeros((experts, tok_count), F32)
    for k in range(choices):
        hit = routes_ref[k : k + 1, :] == expert_ids
        member = member + jnp.where(hit, 1.0, 0.0)
        weight = weight + jnp.where(hit, weights_ref[k : k + 1, :], 0.0)
    rank = dot(member.astype(BF16), earlier, 1, 0)
    rank = jnp.where(member > 0.0, rank, -1.0).astype(BF16)
    weight_hi = weight.astype(BF16)
    weight_lo = (weight - weight_hi.astype(F32)).astype(BF16)
    rank_of = dot(spread, rank, 1, 0)
    tok_pick = jnp.where(rank_of == tok_place, 1.0, 0.0).astype(BF16)
    grad_here = rank_of == grad_place
    hi = jnp.where(grad_here, dot(spread, weight_hi, 1, 0), 0.0).astype(BF16)
    lo = jnp.where(grad_here, dot(spread, weight_lo, 1, 0), 0.0).astype(BF16)
    out = dot(tok_pick, tok_ref[...], 1, 0)
    out = out + dot(hi, grad_ref[...], 1, 0) + dot(lo, grad_ref[...], 1, 0)
    out_ref[...] = out.astype(BF16)


def call(kernel, name, out_shapes, operands, scalars=0, in_hbm=False, scratch=(), dtype=BF16):
    smem = pl.BlockSpec(memory_space=pltpu.SMEM)
    rest = pl.BlockSpec(memory_space=pltpu.HBM) if in_hbm else pl.BlockSpec(memory_space=pltpu.VMEM)
    outs = [jax.ShapeDtypeStruct(shape, dtype) for shape in out_shapes]
    flops = 2 * 384 * 768 * 768
    moved = sum(v.size * 2 for v in list(operands) + outs)
    return pl.pallas_call(
        kernel,
        out_shape=outs,
        in_specs=[smem] * scalars + [rest] * (len(operands) - scalars),
        out_specs=[pl.BlockSpec(memory_space=pltpu.VMEM)] * len(outs),
        scratch_shapes=list(scratch),
        compiler_params=pltpu.CompilerParams(vmem_limit_bytes=ALL_VMEM if in_hbm else VMEM_BYTES),
        cost_estimate=pl.CostEstimate(flops=flops, bytes_accessed=moved, transcendentals=0),
        name=name,
    )(*operands)


def pick_rows(routes, weights, tokens, out_grad, experts, capacity):
    operands = (routes.T, weights.T, tokens, out_grad)
    out = call(
        functools.partial(pick_kernel, capacity),
        "pick_rows",
        [(2 * capacity * experts, tokens.shape[1])],
        operands,
        in_hbm=True,
        scratch=[pltpu.VMEM(v.shape, v.dtype) for v in operands] + [pltpu.SemaphoreType.DMA((4,))],
    )[0]
    return out.reshape(experts, 2 * capacity, tokens.shape[1])


def side(which, size):
    return pl.ds(pl.multiple_of(which * size, size), size)


def away_kernel(core_ref, gate_ref, up_ref, down_ref, in_ref, grad_ref, out_ref):
    units, rows = out_ref.shape[0], in_ref.shape[0]
    cut = side(1 - core_ref[0], units)
    out_ref[:, :rows] = dot(gate_ref[cut, :], in_ref[...], 1, 1).astype(BF16)
    out_ref[:, rows : 2 * rows] = dot(up_ref[cut, :], in_ref[...], 1, 1).astype(BF16)
    out_ref[:, 2 * rows :] = dot(down_ref[cut, :], grad_ref[...], 1, 1).astype(BF16)


def keep_kernel(core_ref, gate_ref, up_ref, down_ref, in_ref, grad_ref, out_ref):
    units, rows = out_ref.shape[0], in_ref.shape[0]
    cut = side(core_ref[0], units)
    out_ref[:, :rows] = dot(gate_ref[cut, :], in_ref[...], 1, 1)
    out_ref[:, rows : 2 * rows] = dot(up_ref[cut, :], in_ref[...], 1, 1)
    out_ref[:, 2 * rows :] = dot(down_ref[cut, :], grad_ref[...], 1, 1)


def half_back(units_ref, first_ref, rest_ref, cut, rows):
    split = first_ref.shape[0]
    gate, up = units_ref[:, :rows], units_ref[:, rows : 2 * rows]
    upper = dot(first_ref[:, cut], gate, 1, 0)
    lower = dot(rest_ref[: rest_ref.shape[0] - 2 * split, cut], gate, 1, 0)
    return jnp.concatenate([upper, lower], 0) + dot(rest_ref[split:, cut], up, 1, 0)


def mine_back_kernel(core_ref, mine_ref, first_ref, rest_ref, out_ref):
    units, rows = mine_ref.shape[0], out_ref.shape[1]
    out_ref[...] = half_back(mine_ref, first_ref, rest_ref, side(core_ref[0], units), rows)


def back_kernel(capacity, core_ref, theirs_ref, first_ref, rest_ref, total_ref, out_ref):
    units, rows = theirs_ref.shape[0], total_ref.shape[1]
    out_rows = out_ref.shape[0]
    total = total_ref[...] + half_back(theirs_ref, first_ref, rest_ref, side(1 - core_ref[0], units), rows)
    groups = rows // capacity
    padded = out_rows // groups
    row = lax.broadcasted_iota(jnp.int32, (out_rows, groups), 0)
    group = lax.broadcasted_iota(jnp.int32, (out_rows, groups), 1)
    inside = (row >= group * padded) & (row < group * padded + capacity)
    source = jnp.where(inside, row - group * (padded - capacity) + 1, 0).astype(F32)
    source = jnp.sum(source, axis=1, keepdims=True) - 1.0
    column = lax.broadcasted_iota(jnp.int32, (out_rows, rows), 1).astype(F32)
    place = jnp.where(column == source, 1.0, 0.0).astype(BF16)
    out_ref[...] = dot(place, total.astype(BF16), 1, 1).astype(BF16)


def soft_rotate(block, rotation):
    rotated = dot(block, rotation, 1, 0)
    meansq = jnp.sum(rotated * rotated, axis=1, keepdims=True) * (1.0 / HBLOCK) + EPS
    steps = rotated * (QSTEP * lax.rsqrt(meansq))
    near = steps - jnp.round(steps)
    square = near * near
    series = square * SINE[-1] + SINE[-2]
    for term in SINE[-3::-1]:
        series = series * square + term
    return ((steps - near * series) * (jnp.sqrt(meansq) / QSTEP)).astype(BF16)


def grads_kernel(
    core_ref, mine_ref, theirs_ref, rows_ref, rotation_ref, gate_ref, up_ref, down_ref, in_q, grad_q, gate_q, up_q, hid_q
):
    units, rows = mine_ref.shape[0], mine_ref.shape[1] // 3
    width = in_q.shape[0]
    rotation = rotation_ref[...]
    core = core_ref[0]
    scale = 1.0 / HBLOCK
    for b in range(rows // HBLOCK):
        cut = slice(b * HBLOCK, (b + 1) * HBLOCK)
        in_q[:, cut] = soft_rotate(rows_ref[:width, cut], rotation)
        grad_q[:, cut] = soft_rotate(rows_ref[width:, cut], rotation)
    for ref, which in ((mine_ref, core), (theirs_ref, 1 - core)):
        place = side(which, units)
        for k, dst in enumerate((gate_q, up_q, hid_q)):
            for b in range(rows // HBLOCK):
                cut = slice(b * HBLOCK, (b + 1) * HBLOCK)
                lanes = slice(k * rows + b * HBLOCK, k * rows + (b + 1) * HBLOCK)
                dst[:, cut] = soft_rotate(ref[:, lanes], rotation)
        gate_ref[:, place] = (dot(in_q[...], gate_q[...], 1, 1) * scale).astype(BF16)
        up_ref[:, place] = (dot(in_q[...], up_q[...], 1, 1) * scale).astype(BF16)
        down_ref[place, :] = (dot(hid_q[...], grad_q[...], 1, 1) * scale).astype(BF16)


def slot_picker(routes, expert_count, capacity):
    experts_iota = jnp.arange(expert_count, dtype=jnp.int32)
    member = jnp.sum((routes[:, :, None] == experts_iota[None, None, :]).astype(jnp.int32), axis=1)
    rank_table = jnp.cumsum(member, axis=0) - member
    cap_iota = jnp.arange(capacity, dtype=jnp.int32)
    placed = (rank_table[:, :, None] == cap_iota[None, None, :]) & (member[:, :, None] == 1)
    return jnp.transpose(placed.astype(BF16), (1, 2, 0))


def pair_permute(x, axis):
    return lax.ppermute(x, axis, [(0, 1), (1, 0)])


def by_pair(which, alone, paired, *operands):
    branches = [alone] + [functools.partial(paired, axis) for axis in BITS[::-1]]
    return lax.switch(which, branches, *operands)


def swap(which, x):
    def paired(axis, v):
        return jax.tree.map(lambda leaf: pair_permute(leaf, axis), v)

    return by_pair(which, lambda v: v, paired, x)


def shards(
    tokens, out_grad, routes, route_weights, gate_weight, up_weight, down_weight, sign_bits, partner
):
    experts = lax.axis_size(BITS)
    n_y = lax.axis_size("y")
    core = lax.axis_index("core")
    me = lax.axis_index(BITS)
    mate = partner[me]
    apart = me ^ mate
    which = sum((apart == 1 << k).astype(jnp.int32) * (k + 1) for k in range(len(BITS)))
    tok_count, width = tokens.shape
    capacity = min(tok_count, tok_count * routes.shape[1] * 3 // (2 * experts))
    rows = experts * capacity
    ff = gate_weight.shape[2]
    half = ff // 2
    core_arg = core.astype(jnp.int32)[None]

    gate_w, up_w, down_w = gate_weight[0], up_weight[0], down_weight[0]
    send = pick_rows(routes, route_weights, tokens, out_grad, experts, capacity)
    recv = lax.all_to_all(send, BITS, 0, 0, tiled=True)
    gate_first = gate_w[: width // 2]
    weight_rest = jnp.concatenate([gate_w[width // 2 :], up_w], 0)
    gate_t, up_t = gate_w.T, up_w.T
    recv, weight_rest, gate_t, up_t = lax.optimization_barrier((recv, weight_rest, gate_t, up_t))
    rows_in = recv[:, :capacity].reshape(rows, width)
    rows_grad = recv[:, capacity:].reshape(rows, width)

    feeds = (core_arg, gate_t, up_t, down_w, rows_in, rows_grad)
    wide = (half, 3 * rows)
    away = call(away_kernel, "away_partials", [wide], feeds, 1)[0]
    arrived = pair_permute(away, "core")
    kept = call(keep_kernel, "keep_partials", [wide], feeds, 1, dtype=F32)[0]
    chip_sum = (kept + arrived.astype(F32)).astype(BF16)

    chip_sum, recv, gate_first = lax.optimization_barrier((chip_sum, recv, gate_first))

    piece = (half // n_y, 3 * rows)
    blocks = lax.all_to_all(chip_sum.reshape((n_y,) + piece), "y", 0, 0, tiled=True)
    mate_recv, gate_first = swap(which, (recv, gate_first))
    blocks, mate_recv, gate_first = lax.optimization_barrier((blocks, mate_recv, gate_first))
    sums = jnp.sum(blocks.astype(F32), axis=0)
    gate_sum, up_sum, hid_grad = sums[:, :rows], sums[:, rows : 2 * rows], sums[:, 2 * rows :]
    sig = jax.nn.sigmoid(gate_sum)
    silu = gate_sum * sig
    gate_rows = hid_grad * up_sum * sig * (1.0 + gate_sum * (1.0 - sig))
    acts = jnp.concatenate([gate_rows, hid_grad * silu, silu * up_sum], 1).astype(BF16)

    acts, weight_rest = lax.optimization_barrier((swap(which, acts), weight_rest))
    acts = jnp.broadcast_to(acts[None], (n_y,) + piece)
    mine = lax.all_to_all(acts, "y", 0, 0, tiled=True).reshape(wide)
    weight_rest = swap(which, weight_rest)
    mate_rows = jnp.concatenate(
        [mate_recv[:, :capacity].reshape(rows, width).T, mate_recv[:, capacity:].reshape(rows, width).T], 0
    )
    mine, weight_rest, mate_rows = lax.optimization_barrier((mine, weight_rest, mate_rows))
    theirs = pair_permute(mine, "core")

    padded = -(-capacity // 16) * 16
    weights = (gate_first, weight_rest)
    mine_back = call(
        mine_back_kernel, "mine_back", [(width, rows)], (core_arg, mine) + weights, 1, dtype=F32
    )[0]
    slot_back = call(
        functools.partial(back_kernel, capacity),
        "slot_back",
        [(experts * padded, width)],
        (core_arg, theirs) + weights + (mine_back,),
        1,
    )[0]
    returned = lax.all_to_all(slot_back.reshape(experts, padded, width), BITS, 0, 0, tiled=True)
    picker = jnp.take(slot_picker(routes, experts, capacity), partner, axis=0)
    picker = jnp.pad(picker, ((0, 0), (0, padded - capacity), (0, 0))).reshape(experts * padded, tok_count)
    input_grad = dot(picker, returned.reshape(experts * padded, width), 0, 0).astype(BF16)

    flip_signs = (1 - 2 * lax.dynamic_index_in_dim(sign_bits, mate, 0, keepdims=False)).astype(BF16)
    rotation = sylvester(HBLOCK) * flip_signs[:, None]
    gate_new, up_new, down_new = call(
        grads_kernel,
        "weight_grads",
        [(width, ff), (width, ff), (ff, width)],
        (core_arg, mine, theirs, mate_rows, rotation),
        1,
        scratch=[pltpu.VMEM((n, rows), BF16) for n in (width, width, half, half, half)],
    )
    return gate_new[None], up_new[None], down_new[None], input_grad


def solution(mesh):
    n_dp = mesh.shape["dp"]
    split = Mesh(mesh.devices.reshape((n_dp // 2, 2) + (2,) * len(BITS)), ("y", "core") + BITS)
    dp = ("y", "core")
    return jax.shard_map(
        shards,
        mesh=split,
        in_specs=(
            P(BITS, dp),
            P(BITS, dp),
            P(BITS, None),
            P(BITS, None),
            P(BITS, dp, None),
            P(BITS, dp, None),
            P(BITS, None, dp),
            P(),
            P(),
        ),
        out_specs=(
            P(BITS, dp, None),
            P(BITS, dp, None),
            P(BITS, None, dp),
            P(BITS, dp),
        ),
        check_vma=False,
    )
```

```python
import functools

import jax
import jax.numpy as jnp
from jax import lax
from jax.experimental import pallas as pl
from jax.experimental.pallas import tpu as pltpu
from jax.sharding import Mesh
from jax.sharding import PartitionSpec as P

HBLOCK = 128
EPS = 1e-06
QSTEP = 2.0
SINE = (
    0.9999995827674866,
    -6.579691410064697,
    12.986429214477539,
    -12.18803596496582,
    6.557779312133789,
    -1.952649712562561,
)
BF16 = jnp.bfloat16
F32 = jnp.float32
BITS = ("b4", "b3", "b2", "b1", "b0")
VMEM_BYTES = 16 * 2**20
ALL_VMEM = 60 * 2**20


def dot(left, right, left_dim, right_dim):
    return lax.dot_general(
        left, right, (((left_dim,), (right_dim,)), ((), ())), preferred_element_type=F32
    )


def sylvester(block_len):
    positions = jnp.arange(block_len, dtype=jnp.int32)
    common_bits = positions[:, None] & positions[None, :]
    parity = jnp.zeros((block_len, block_len), jnp.int32)
    for bit_pos in range(block_len.bit_length() - 1):
        parity = parity ^ common_bits >> bit_pos & 1
    return (1 - 2 * parity).astype(BF16)


def pick_kernel(
    capacity, routes_in, weights_in, tok_in, grad_in, out_ref, routes_ref, weights_ref, tok_ref, grad_ref, sems
):
    loads = [
        pltpu.make_async_copy(src, dst, sems.at[k])
        for k, (src, dst) in enumerate(
            ((routes_in, routes_ref), (weights_in, weights_ref), (tok_in, tok_ref), (grad_in, grad_ref))
        )
    ]
    for load in loads:
        load.start()
    choices, tok_count = routes_ref.shape
    block = 2 * capacity
    out_rows = out_ref.shape[0]
    experts = out_rows // block

    row = lax.broadcasted_iota(jnp.int32, (out_rows, experts), 0)
    start = lax.broadcasted_iota(jnp.int32, (out_rows, experts), 1) * block
    owns = (row >= start) & (row < start + block)
    spread = jnp.where(owns, 1.0, 0.0).astype(BF16)
    place = jnp.sum(jnp.where(owns, row - start, 0).astype(F32), axis=1, keepdims=True)
    is_tok = place < capacity
    tok_place = jnp.where(is_tok, place, -2.0)
    grad_place = jnp.where(is_tok, -2.0, place - capacity)
    square = (tok_count, tok_count)
    earlier = lax.broadcasted_iota(jnp.int32, square, 0) < lax.broadcasted_iota(jnp.int32, square, 1)
    earlier = jnp.where(earlier, 1.0, 0.0).astype(BF16)
    expert_ids = lax.broadcasted_iota(jnp.int32, (experts, tok_count), 0)

    for load in loads:
        load.wait()
    member = jnp.zeros((experts, tok_count), F32)
    weight = jnp.zeros((experts, tok_count), F32)
    for k in range(choices):
        hit = routes_ref[k : k + 1, :] == expert_ids
        member = member + jnp.where(hit, 1.0, 0.0)
        weight = weight + jnp.where(hit, weights_ref[k : k + 1, :], 0.0)
    rank = dot(member.astype(BF16), earlier, 1, 0)
    rank = jnp.where(member > 0.0, rank, -1.0).astype(BF16)
    weight_hi = weight.astype(BF16)
    weight_lo = (weight - weight_hi.astype(F32)).astype(BF16)
    rank_of = dot(spread, rank, 1, 0)
    tok_pick = jnp.where(rank_of == tok_place, 1.0, 0.0).astype(BF16)
    grad_here = rank_of == grad_place
    hi = jnp.where(grad_here, dot(spread, weight_hi, 1, 0), 0.0).astype(BF16)
    lo = jnp.where(grad_here, dot(spread, weight_lo, 1, 0), 0.0).astype(BF16)
    out = dot(tok_pick, tok_ref[...], 1, 0)
    out = out + dot(hi, grad_ref[...], 1, 0) + dot(lo, grad_ref[...], 1, 0)
    out_ref[...] = out.astype(BF16)


def call(kernel, name, out_shapes, operands, scalars=0, in_hbm=False, scratch=(), dtype=BF16):
    smem = pl.BlockSpec(memory_space=pltpu.SMEM)
    rest = pl.BlockSpec(memory_space=pltpu.HBM) if in_hbm else pl.BlockSpec(memory_space=pltpu.VMEM)
    outs = [jax.ShapeDtypeStruct(shape, dtype) for shape in out_shapes]
    flops = 2 * 384 * 768 * 768
    moved = sum(v.size * 2 for v in list(operands) + outs)
    return pl.pallas_call(
        kernel,
        out_shape=outs,
        in_specs=[smem] * scalars + [rest] * (len(operands) - scalars),
        out_specs=[pl.BlockSpec(memory_space=pltpu.VMEM)] * len(outs),
        scratch_shapes=list(scratch),
        compiler_params=pltpu.CompilerParams(vmem_limit_bytes=ALL_VMEM if in_hbm else VMEM_BYTES),
        cost_estimate=pl.CostEstimate(flops=flops, bytes_accessed=moved, transcendentals=0),
        name=name,
    )(*operands)


def pick_rows(routes, weights, tokens, out_grad, experts, capacity):
    operands = (routes.T, weights.T, tokens, out_grad)
    out = call(
        functools.partial(pick_kernel, capacity),
        "pick_rows",
        [(2 * capacity * experts, tokens.shape[1])],
        operands,
        in_hbm=True,
        scratch=[pltpu.VMEM(v.shape, v.dtype) for v in operands] + [pltpu.SemaphoreType.DMA((4,))],
    )[0]
    return out.reshape(experts, 2 * capacity, tokens.shape[1])


def side(which, size):
    return pl.ds(pl.multiple_of(which * size, size), size)


def away_kernel(core_ref, gate_ref, up_ref, down_ref, in_ref, grad_ref, out_ref):
    units, rows = out_ref.shape[0], in_ref.shape[0]
    cut = side(1 - core_ref[0], units)
    out_ref[:, :rows] = dot(gate_ref[cut, :], in_ref[...], 1, 1).astype(BF16)
    out_ref[:, rows : 2 * rows] = dot(up_ref[cut, :], in_ref[...], 1, 1).astype(BF16)
    out_ref[:, 2 * rows :] = dot(down_ref[cut, :], grad_ref[...], 1, 1).astype(BF16)


def keep_kernel(core_ref, gate_ref, up_ref, down_ref, in_ref, grad_ref, out_ref):
    units, rows = out_ref.shape[0], in_ref.shape[0]
    cut = side(core_ref[0], units)
    out_ref[:, :rows] = dot(gate_ref[cut, :], in_ref[...], 1, 1)
    out_ref[:, rows : 2 * rows] = dot(up_ref[cut, :], in_ref[...], 1, 1)
    out_ref[:, 2 * rows :] = dot(down_ref[cut, :], grad_ref[...], 1, 1)


def half_back(units_ref, gate_ref, up_ref, cut, rows):
    part = dot(gate_ref[:, cut], units_ref[:, :rows], 1, 0)
    return part + dot(up_ref[:, cut], units_ref[:, rows:], 1, 0)


def mine_back_kernel(core_ref, mine_ref, gate_ref, up_ref, out_ref):
    units, rows = mine_ref.shape[0], out_ref.shape[1]
    out_ref[...] = half_back(mine_ref, gate_ref, up_ref, side(core_ref[0], units), rows)


def back_kernel(capacity, core_ref, theirs_ref, gate_ref, up_ref, total_ref, out_ref):
    units, rows = theirs_ref.shape[0], total_ref.shape[1]
    out_rows = out_ref.shape[0]
    total = total_ref[...] + half_back(theirs_ref, gate_ref, up_ref, side(1 - core_ref[0], units), rows)
    groups = rows // capacity
    padded = out_rows // groups
    row = lax.broadcasted_iota(jnp.int32, (out_rows, groups), 0)
    group = lax.broadcasted_iota(jnp.int32, (out_rows, groups), 1)
    inside = (row >= group * padded) & (row < group * padded + capacity)
    source = jnp.where(inside, row - group * (padded - capacity) + 1, 0).astype(F32)
    source = jnp.sum(source, axis=1, keepdims=True) - 1.0
    column = lax.broadcasted_iota(jnp.int32, (out_rows, rows), 1).astype(F32)
    place = jnp.where(column == source, 1.0, 0.0).astype(BF16)
    out_ref[...] = dot(place, total.astype(BF16), 1, 1).astype(BF16)


def soft_rotate(block, rotation):
    rotated = dot(block, rotation, 1, 0)
    meansq = jnp.sum(rotated * rotated, axis=1, keepdims=True) * (1.0 / HBLOCK) + EPS
    steps = rotated * (QSTEP * lax.rsqrt(meansq))
    near = steps - jnp.round(steps)
    square = near * near
    series = square * SINE[-1] + SINE[-2]
    for term in SINE[-3::-1]:
        series = series * square + term
    return ((steps - near * series) * (jnp.sqrt(meansq) / QSTEP)).astype(BF16)


def quant_kernel(rows_ref, rotation_ref, out_ref):
    rotation = rotation_ref[...]
    for b in range(rows_ref.shape[1] // HBLOCK):
        cut = slice(b * HBLOCK, (b + 1) * HBLOCK)
        out_ref[:, cut] = soft_rotate(rows_ref[:, cut], rotation)


def grads_kernel(core_ref, mine_ref, theirs_ref, rows_ref, gate_ref, up_ref, down_ref):
    units, rows = mine_ref.shape[0], rows_ref.shape[1]
    width = gate_ref.shape[0]
    core = core_ref[0]
    scale = 1.0 / HBLOCK
    for ref, which in ((mine_ref, core), (theirs_ref, 1 - core)):
        place = side(which, units)
        gate_ref[:, place] = (dot(rows_ref[:width, :], ref[:, :rows], 1, 1) * scale).astype(BF16)
        up_ref[:, place] = (dot(rows_ref[:width, :], ref[:, rows : 2 * rows], 1, 1) * scale).astype(BF16)
        down_ref[place, :] = (dot(ref[:, 2 * rows :], rows_ref[width:, :], 1, 1) * scale).astype(BF16)


def slot_picker(routes, expert_count, capacity):
    experts_iota = jnp.arange(expert_count, dtype=jnp.int32)
    member = jnp.sum((routes[:, :, None] == experts_iota[None, None, :]).astype(jnp.int32), axis=1)
    rank_table = jnp.cumsum(member, axis=0) - member
    cap_iota = jnp.arange(capacity, dtype=jnp.int32)
    placed = (rank_table[:, :, None] == cap_iota[None, None, :]) & (member[:, :, None] == 1)
    return jnp.transpose(placed.astype(BF16), (1, 2, 0))


def pair_permute(x, axis):
    return lax.ppermute(x, axis, [(0, 1), (1, 0)])


def by_pair(which, alone, paired, *operands):
    branches = [alone] + [functools.partial(paired, axis) for axis in BITS[::-1]]
    return lax.switch(which, branches, *operands)


def swap(which, x):
    def paired(axis, v):
        return jax.tree.map(lambda leaf: pair_permute(leaf, axis), v)

    return by_pair(which, lambda v: v, paired, x)


def shards(
    tokens, out_grad, routes, route_weights, gate_weight, up_weight, down_weight, sign_bits, partner
):
    experts = lax.axis_size(BITS)
    n_y = lax.axis_size("y")
    core = lax.axis_index("core")
    me = lax.axis_index(BITS)
    mate = partner[me]
    apart = me ^ mate
    which = sum((apart == 1 << k).astype(jnp.int32) * (k + 1) for k in range(len(BITS)))
    tok_count, width = tokens.shape
    capacity = min(tok_count, tok_count * routes.shape[1] * 3 // (2 * experts))
    rows = experts * capacity
    ff = gate_weight.shape[2]
    half = ff // 2
    core_arg = core.astype(jnp.int32)[None]

    gate_w, up_w, down_w = gate_weight[0], up_weight[0], down_weight[0]
    send = pick_rows(routes, route_weights, tokens, out_grad, experts, capacity)
    recv = lax.all_to_all(send, BITS, 0, 0, tiled=True)
    gate_t, up_t = gate_w.T, up_w.T
    recv, gate_t, up_t = lax.optimization_barrier((recv, gate_t, up_t))
    rows_in = recv[:, :capacity].reshape(rows, width)
    rows_grad = recv[:, capacity:].reshape(rows, width)

    feeds = (core_arg, gate_t, up_t, down_w, rows_in, rows_grad)
    wide = (half, 3 * rows)
    away = call(away_kernel, "away_partials", [wide], feeds, 1)[0]
    arrived = pair_permute(away, "core")
    kept = call(keep_kernel, "keep_partials", [wide], feeds, 1, dtype=F32)[0]
    chip_sum = (kept + arrived.astype(F32)).astype(BF16)

    chip_sum, recv = lax.optimization_barrier((chip_sum, recv))

    def copies(x):
        return jnp.broadcast_to(x[None], (n_y,) + x.shape)

    def over_y(x):
        return lax.all_to_all(x, "y", 0, 0, tiled=True)

    blocks = over_y(chip_sum.reshape(n_y, half // n_y, 3 * rows))
    mate_recv = swap(which, recv)
    blocks, mate_recv = lax.optimization_barrier((blocks, mate_recv))
    sums = jnp.sum(blocks.astype(F32), axis=0)
    gate_sum, up_sum, hid_grad = sums[:, :rows], sums[:, rows : 2 * rows], sums[:, 2 * rows :]
    sig = jax.nn.sigmoid(gate_sum)
    silu = gate_sum * sig
    gate_rows = hid_grad * up_sum * sig * (1.0 + gate_sum * (1.0 - sig))
    acts = jnp.concatenate([gate_rows, hid_grad * silu, silu * up_sum], 1).astype(BF16)

    own = over_y(copies(acts[:, : 2 * rows])).reshape(half, 2 * rows)

    def rotation_of(expert):
        bits = lax.dynamic_index_in_dim(sign_bits, expert, 0, keepdims=False)
        return sylvester(HBLOCK) * (1 - 2 * bits).astype(BF16)[:, None]

    def quantized(x, expert, name):
        return call(quant_kernel, name, [x.shape], (x, rotation_of(expert)))[0]

    mate_units = swap(which, quantized(acts, me, "quant_units"))
    own, mate_units = lax.optimization_barrier((own, mate_units))

    mine = over_y(copies(mate_units)).reshape(half, 3 * rows)
    own_other = pair_permute(own, "core")
    mine_back = call(
        mine_back_kernel, "mine_back", [(width, rows)], (core_arg, own, gate_w, up_w), 1, dtype=F32
    )[0]
    padded = -(-capacity // 16) * 16
    slot_back = call(
        functools.partial(back_kernel, capacity),
        "slot_back",
        [(experts * padded, width)],
        (core_arg, own_other, gate_w, up_w, mine_back),
        1,
    )[0]
    mate_rows = jnp.concatenate(
        [mate_recv[:, :capacity].reshape(rows, width).T, mate_recv[:, capacity:].reshape(rows, width).T], 0
    )
    mate_rows = quantized(mate_rows, mate, "quant_rows")
    mine, slot_back, mate_rows = lax.optimization_barrier((mine, slot_back, mate_rows))

    returned = lax.all_to_all(slot_back.reshape(experts, padded, width), BITS, 0, 0, tiled=True)
    picker = jnp.pad(slot_picker(routes, experts, capacity), ((0, 0), (0, padded - capacity), (0, 0)))
    picker = picker.reshape(experts * padded, tok_count)
    input_grad = dot(picker, returned.reshape(experts * padded, width), 0, 0).astype(BF16)
    theirs = pair_permute(mine, "core")
    gate_new, up_new, down_new = call(
        grads_kernel,
        "weight_grads",
        [(width, ff), (width, ff), (ff, width)],
        (core_arg, mine, theirs, mate_rows),
        1,
    )
    return gate_new[None], up_new[None], down_new[None], input_grad


def solution(mesh):
    n_dp = mesh.shape["dp"]
    split = Mesh(mesh.devices.reshape((n_dp // 2, 2) + (2,) * len(BITS)), ("y", "core") + BITS)
    dp = ("y", "core")
    return jax.shard_map(
        shards,
        mesh=split,
        in_specs=(
            P(BITS, dp),
            P(BITS, dp),
            P(BITS, None),
            P(BITS, None),
            P(BITS, dp, None),
            P(BITS, dp, None),
            P(BITS, None, dp),
            P(),
            P(),
        ),
        out_specs=(
            P(BITS, dp, None),
            P(BITS, dp, None),
            P(BITS, None, dp),
            P(BITS, dp),
        ),
        check_vma=False,
    )
```

```python
import functools

import jax
import jax.numpy as jnp
from jax import lax
from jax.experimental import pallas as pl
from jax.experimental.pallas import tpu as pltpu
from jax.sharding import Mesh
from jax.sharding import PartitionSpec as P

HBLOCK = 128
EPS = 1e-06
QSTEP = 2.0
SINE = (
    0.9999995827674866,
    -6.579691410064697,
    12.986429214477539,
    -12.18803596496582,
    6.557779312133789,
    -1.952649712562561,
)
BF16 = jnp.bfloat16
F32 = jnp.float32
BITS = ("b4", "b3", "b2", "b1", "b0")
VMEM_BYTES = 16 * 2**20
ALL_VMEM = 60 * 2**20


def dot(left, right, left_dim, right_dim):
    return lax.dot_general(
        left, right, (((left_dim,), (right_dim,)), ((), ())), preferred_element_type=F32
    )


def sylvester(block_len):
    positions = jnp.arange(block_len, dtype=jnp.int32)
    common_bits = positions[:, None] & positions[None, :]
    parity = jnp.zeros((block_len, block_len), jnp.int32)
    for bit_pos in range(block_len.bit_length() - 1):
        parity = parity ^ common_bits >> bit_pos & 1
    return (1 - 2 * parity).astype(BF16)


def pick_kernel(
    capacity, routes_in, weights_in, tok_in, grad_in, out_ref, routes_ref, weights_ref, tok_ref, grad_ref, sems
):
    loads = [
        pltpu.make_async_copy(src, dst, sems.at[k])
        for k, (src, dst) in enumerate(
            ((routes_in, routes_ref), (weights_in, weights_ref), (tok_in, tok_ref), (grad_in, grad_ref))
        )
    ]
    for load in loads:
        load.start()
    choices, tok_count = routes_ref.shape
    block = 2 * capacity
    out_rows = out_ref.shape[0]
    experts = out_rows // block

    row = lax.broadcasted_iota(jnp.int32, (out_rows, experts), 0)
    start = lax.broadcasted_iota(jnp.int32, (out_rows, experts), 1) * block
    owns = (row >= start) & (row < start + block)
    spread = jnp.where(owns, 1.0, 0.0).astype(BF16)
    place = jnp.sum(jnp.where(owns, row - start, 0).astype(F32), axis=1, keepdims=True)
    is_tok = place < capacity
    tok_place = jnp.where(is_tok, place, -2.0)
    grad_place = jnp.where(is_tok, -2.0, place - capacity)
    square = (tok_count, tok_count)
    earlier = lax.broadcasted_iota(jnp.int32, square, 0) < lax.broadcasted_iota(jnp.int32, square, 1)
    earlier = jnp.where(earlier, 1.0, 0.0).astype(BF16)
    expert_ids = lax.broadcasted_iota(jnp.int32, (experts, tok_count), 0)

    for load in loads:
        load.wait()
    member = jnp.zeros((experts, tok_count), F32)
    weight = jnp.zeros((experts, tok_count), F32)
    for k in range(choices):
        hit = routes_ref[k : k + 1, :] == expert_ids
        member = member + jnp.where(hit, 1.0, 0.0)
        weight = weight + jnp.where(hit, weights_ref[k : k + 1, :], 0.0)
    rank = dot(member.astype(BF16), earlier, 1, 0)
    rank = jnp.where(member > 0.0, rank, -1.0).astype(BF16)
    weight_hi = weight.astype(BF16)
    weight_lo = (weight - weight_hi.astype(F32)).astype(BF16)
    rank_of = dot(spread, rank, 1, 0)
    tok_pick = jnp.where(rank_of == tok_place, 1.0, 0.0).astype(BF16)
    grad_here = rank_of == grad_place
    hi = jnp.where(grad_here, dot(spread, weight_hi, 1, 0), 0.0).astype(BF16)
    lo = jnp.where(grad_here, dot(spread, weight_lo, 1, 0), 0.0).astype(BF16)
    out = dot(tok_pick, tok_ref[...], 1, 0)
    out = out + dot(hi, grad_ref[...], 1, 0) + dot(lo, grad_ref[...], 1, 0)
    out_ref[...] = out.astype(BF16)


def call(kernel, name, out_shapes, operands, scalars=0, in_hbm=False, scratch=(), dtype=BF16):
    smem = pl.BlockSpec(memory_space=pltpu.SMEM)
    rest = pl.BlockSpec(memory_space=pltpu.HBM) if in_hbm else pl.BlockSpec(memory_space=pltpu.VMEM)
    outs = [jax.ShapeDtypeStruct(shape, dtype) for shape in out_shapes]
    flops = 2 * 384 * 768 * 768
    moved = sum(v.size * 2 for v in list(operands) + outs)
    return pl.pallas_call(
        kernel,
        out_shape=outs,
        in_specs=[smem] * scalars + [rest] * (len(operands) - scalars),
        out_specs=[pl.BlockSpec(memory_space=pltpu.VMEM)] * len(outs),
        scratch_shapes=list(scratch),
        compiler_params=pltpu.CompilerParams(vmem_limit_bytes=ALL_VMEM if in_hbm else VMEM_BYTES),
        cost_estimate=pl.CostEstimate(flops=flops, bytes_accessed=moved, transcendentals=0),
        name=name,
    )(*operands)


def pick_rows(routes, weights, tokens, out_grad, experts, capacity):
    operands = (routes.T, weights.T, tokens, out_grad)
    out = call(
        functools.partial(pick_kernel, capacity),
        "pick_rows",
        [(2 * capacity * experts, tokens.shape[1])],
        operands,
        in_hbm=True,
        scratch=[pltpu.VMEM(v.shape, v.dtype) for v in operands] + [pltpu.SemaphoreType.DMA((4,))],
    )[0]
    return out.reshape(experts, 2 * capacity, tokens.shape[1])


def copies_kernel(in_ref, out_ref, sems):
    stores = [pltpu.make_async_copy(in_ref, out_ref.at[k], sems.at[k]) for k in range(out_ref.shape[0])]
    for store in stores:
        store.start()
    for store in stores:
        store.wait()


def copies(x, count):
    return pl.pallas_call(
        copies_kernel,
        out_shape=jax.ShapeDtypeStruct((count,) + x.shape, x.dtype),
        in_specs=[pl.BlockSpec(memory_space=pltpu.VMEM)],
        out_specs=pl.BlockSpec(memory_space=pl.ANY),
        scratch_shapes=[pltpu.SemaphoreType.DMA((count,))],
        compiler_params=pltpu.CompilerParams(vmem_limit_bytes=VMEM_BYTES),
        name="copies",
    )(x)


def side(which, size):
    return pl.ds(pl.multiple_of(which * size, size), size)


def away_kernel(core_ref, gate_ref, up_ref, down_ref, in_ref, grad_ref, out_ref):
    units, rows = out_ref.shape[0], in_ref.shape[0]
    cut = side(1 - core_ref[0], units)
    out_ref[:, :rows] = dot(gate_ref[cut, :], in_ref[...], 1, 1).astype(BF16)
    out_ref[:, rows : 2 * rows] = dot(up_ref[cut, :], in_ref[...], 1, 1).astype(BF16)
    out_ref[:, 2 * rows :] = dot(down_ref[cut, :], grad_ref[...], 1, 1).astype(BF16)


def keep_kernel(core_ref, gate_ref, up_ref, down_ref, in_ref, grad_ref, out_ref):
    units, rows = out_ref.shape[0], in_ref.shape[0]
    cut = side(core_ref[0], units)
    out_ref[:, :rows] = dot(gate_ref[cut, :], in_ref[...], 1, 1)
    out_ref[:, rows : 2 * rows] = dot(up_ref[cut, :], in_ref[...], 1, 1)
    out_ref[:, 2 * rows :] = dot(down_ref[cut, :], grad_ref[...], 1, 1)


def half_back(units_ref, weight_refs, cut, rows):
    gate, up = units_ref[:, :rows], units_ref[:, rows : 2 * rows]
    width = sum(ref.shape[0] for ref in weight_refs) // 2
    parts = []
    done = 0
    for ref in weight_refs:
        for_gate = min(max(width - done, 0), ref.shape[0])
        if for_gate > 0:
            parts.append(dot(ref[:for_gate, cut], gate, 1, 0))
        if for_gate < ref.shape[0]:
            upper = dot(ref[for_gate:, cut], up, 1, 0)
        done += ref.shape[0]
    return jnp.concatenate(parts, 0) + upper


def mine_back_kernel(core_ref, mine_ref, *refs):
    weight_refs, out_ref = refs[:-1], refs[-1]
    units, rows = mine_ref.shape[0], out_ref.shape[1]
    out_ref[...] = half_back(mine_ref, weight_refs, side(core_ref[0], units), rows)


def back_kernel(capacity, core_ref, theirs_ref, *refs):
    weight_refs, (total_ref, out_ref) = refs[:-2], refs[-2:]
    units, rows = theirs_ref.shape[0], total_ref.shape[1]
    out_rows = out_ref.shape[0]
    total = total_ref[...] + half_back(theirs_ref, weight_refs, side(1 - core_ref[0], units), rows)
    groups = rows // capacity
    padded = out_rows // groups
    row = lax.broadcasted_iota(jnp.int32, (out_rows, groups), 0)
    group = lax.broadcasted_iota(jnp.int32, (out_rows, groups), 1)
    inside = (row >= group * padded) & (row < group * padded + capacity)
    source = jnp.where(inside, row - group * (padded - capacity) + 1, 0).astype(F32)
    source = jnp.sum(source, axis=1, keepdims=True) - 1.0
    column = lax.broadcasted_iota(jnp.int32, (out_rows, rows), 1).astype(F32)
    place = jnp.where(column == source, 1.0, 0.0).astype(BF16)
    out_ref[...] = dot(place, total.astype(BF16), 1, 1).astype(BF16)


def soft_rotate(block, rotation):
    rotated = dot(block, rotation, 1, 0)
    meansq = jnp.sum(rotated * rotated, axis=1, keepdims=True) * (1.0 / HBLOCK) + EPS
    steps = rotated * (QSTEP * lax.rsqrt(meansq))
    near = steps - jnp.round(steps)
    square = near * near
    series = square * SINE[-1] + SINE[-2]
    for term in SINE[-3::-1]:
        series = series * square + term
    return ((steps - near * series) * (jnp.sqrt(meansq) / QSTEP)).astype(BF16)


def grads_kernel(
    core_ref, mine_ref, theirs_ref, rows_ref, rotation_ref, gate_ref, up_ref, down_ref, in_q, grad_q, gate_q, up_q, hid_q
):
    units, rows = mine_ref.shape[0], mine_ref.shape[1] // 3
    width = in_q.shape[0]
    rotation = rotation_ref[...]
    core = core_ref[0]
    scale = 1.0 / HBLOCK
    for b in range(rows // HBLOCK):
        cut = slice(b * HBLOCK, (b + 1) * HBLOCK)
        in_q[:, cut] = soft_rotate(rows_ref[:width, cut], rotation)
        grad_q[:, cut] = soft_rotate(rows_ref[width:, cut], rotation)
    for ref, which in ((mine_ref, core), (theirs_ref, 1 - core)):
        place = side(which, units)
        for k, dst in enumerate((gate_q, up_q, hid_q)):
            for b in range(rows // HBLOCK):
                cut = slice(b * HBLOCK, (b + 1) * HBLOCK)
                lanes = slice(k * rows + b * HBLOCK, k * rows + (b + 1) * HBLOCK)
                dst[:, cut] = soft_rotate(ref[:, lanes], rotation)
        gate_ref[:, place] = (dot(in_q[...], gate_q[...], 1, 1) * scale).astype(BF16)
        up_ref[:, place] = (dot(in_q[...], up_q[...], 1, 1) * scale).astype(BF16)
        down_ref[place, :] = (dot(hid_q[...], grad_q[...], 1, 1) * scale).astype(BF16)


def slot_picker(routes, expert_count, capacity):
    experts_iota = jnp.arange(expert_count, dtype=jnp.int32)
    member = jnp.sum((routes[:, :, None] == experts_iota[None, None, :]).astype(jnp.int32), axis=1)
    rank_table = jnp.cumsum(member, axis=0) - member
    cap_iota = jnp.arange(capacity, dtype=jnp.int32)
    placed = (rank_table[:, :, None] == cap_iota[None, None, :]) & (member[:, :, None] == 1)
    return jnp.transpose(placed.astype(BF16), (1, 2, 0))


def pair_permute(x, axis):
    return lax.ppermute(x, axis, [(0, 1), (1, 0)])


def by_pair(which, alone, paired, *operands):
    branches = [alone] + [functools.partial(paired, axis) for axis in BITS[::-1]]
    return lax.switch(which, branches, *operands)


def swap(which, x):
    def paired(axis, v):
        return jax.tree.map(lambda leaf: pair_permute(leaf, axis), v)

    return by_pair(which, lambda v: v, paired, x)


def shards(
    tokens, out_grad, routes, route_weights, gate_weight, up_weight, down_weight, sign_bits, partner
):
    experts = lax.axis_size(BITS)
    n_y = lax.axis_size("y")
    core = lax.axis_index("core")
    me = lax.axis_index(BITS)
    mate = partner[me]
    apart = me ^ mate
    which = sum((apart == 1 << k).astype(jnp.int32) * (k + 1) for k in range(len(BITS)))
    tok_count, width = tokens.shape
    capacity = min(tok_count, tok_count * routes.shape[1] * 3 // (2 * experts))
    rows = experts * capacity
    ff = gate_weight.shape[2]
    half = ff // 2
    core_arg = core.astype(jnp.int32)[None]

    gate_w, up_w, down_w = gate_weight[0], up_weight[0], down_weight[0]
    send = pick_rows(routes, route_weights, tokens, out_grad, experts, capacity)
    recv = lax.all_to_all(send, BITS, 0, 0, tiled=True)
    gate_t, up_t = gate_w.T, up_w.T
    cut_1, cut_2 = width // 2, width * 3 // 4
    weight_3 = jnp.concatenate([gate_w[cut_2:], up_w], 0)
    padded = -(-capacity // 16) * 16
    picker = jnp.take(slot_picker(routes, experts, capacity), partner, axis=0)
    picker = jnp.pad(picker, ((0, 0), (0, padded - capacity), (0, 0))).reshape(experts * padded, tok_count)
    weight_1 = swap(which, gate_w[:cut_1])
    recv, weight_1, weight_3, gate_t, up_t, picker = lax.optimization_barrier(
        (recv, weight_1, weight_3, gate_t, up_t, picker)
    )
    rows_in = recv[:, :capacity].reshape(rows, width)
    rows_grad = recv[:, capacity:].reshape(rows, width)

    feeds = (core_arg, gate_t, up_t, down_w, rows_in, rows_grad)
    wide = (half, 3 * rows)
    away = call(away_kernel, "away_partials", [wide], feeds, 1)[0]
    arrived = pair_permute(away, "core")
    kept = call(keep_kernel, "keep_partials", [wide], feeds, 1, dtype=F32)[0]
    chip_sum = (kept + arrived.astype(F32)).astype(BF16)

    weight_2 = gate_w[cut_1:cut_2]
    chip_sum, recv, weight_2 = lax.optimization_barrier((chip_sum, recv, weight_2))

    piece = (half // n_y, 3 * rows)
    blocks = lax.all_to_all(chip_sum.reshape((n_y,) + piece), "y", 0, 0, tiled=True)
    mate_recv, weight_2 = swap(which, (recv, weight_2))
    blocks, mate_recv, weight_2 = lax.optimization_barrier((blocks, mate_recv, weight_2))
    sums = jnp.sum(blocks.astype(F32), axis=0)
    gate_sum, up_sum, hid_grad = sums[:, :rows], sums[:, rows : 2 * rows], sums[:, 2 * rows :]
    sig = jax.nn.sigmoid(gate_sum)
    silu = gate_sum * sig
    gate_rows = hid_grad * up_sum * sig * (1.0 + gate_sum * (1.0 - sig))
    acts = jnp.concatenate([gate_rows, hid_grad * silu, silu * up_sum], 1).astype(BF16)

    acts, weight_3 = lax.optimization_barrier((swap(which, acts), weight_3))
    mine = lax.all_to_all(copies(acts, n_y), "y", 0, 0, tiled=True).reshape(wide)
    weight_3 = swap(which, weight_3)
    mate_rows = jnp.concatenate(
        [mate_recv[:, :capacity].reshape(rows, width).T, mate_recv[:, capacity:].reshape(rows, width).T], 0
    )
    flip_signs = (1 - 2 * lax.dynamic_index_in_dim(sign_bits, mate, 0, keepdims=False)).astype(BF16)
    rotation = sylvester(HBLOCK) * flip_signs[:, None]
    mine, weight_3, mate_rows, rotation = lax.optimization_barrier((mine, weight_3, mate_rows, rotation))
    theirs = pair_permute(mine, "core")

    weights = (weight_1, weight_2, weight_3)
    mine_back = call(
        mine_back_kernel, "mine_back", [(width, rows)], (core_arg, mine) + weights, 1, dtype=F32
    )[0]
    slot_back = call(
        functools.partial(back_kernel, capacity),
        "slot_back",
        [(experts * padded, width)],
        (core_arg, theirs) + weights + (mine_back,),
        1,
    )[0]
    returned = lax.all_to_all(slot_back.reshape(experts, padded, width), BITS, 0, 0, tiled=True)
    input_grad = dot(picker, returned.reshape(experts * padded, width), 0, 0).astype(BF16)

    gate_new, up_new, down_new = call(
        grads_kernel,
        "weight_grads",
        [(width, ff), (width, ff), (ff, width)],
        (core_arg, mine, theirs, mate_rows, rotation),
        1,
        scratch=[pltpu.VMEM((n, rows), BF16) for n in (width, width, half, half, half)],
    )
    return gate_new[None], up_new[None], down_new[None], input_grad


def solution(mesh):
    n_dp = mesh.shape["dp"]
    split = Mesh(mesh.devices.reshape((n_dp // 2, 2) + (2,) * len(BITS)), ("y", "core") + BITS)
    dp = ("y", "core")
    return jax.shard_map(
        shards,
        mesh=split,
        in_specs=(
            P(BITS, dp),
            P(BITS, dp),
            P(BITS, None),
            P(BITS, None),
            P(BITS, dp, None),
            P(BITS, dp, None),
            P(BITS, None, dp),
            P(),
            P(),
        ),
        out_specs=(
            P(BITS, dp, None),
            P(BITS, dp, None),
            P(BITS, None, dp),
            P(BITS, dp),
        ),
        check_vma=False,
    )
```

```python
import functools

import jax
import jax.numpy as jnp
from jax import lax
from jax.experimental import pallas as pl
from jax.experimental.pallas import tpu as pltpu
from jax.sharding import Mesh
from jax.sharding import PartitionSpec as P

HBLOCK = 128
EPS = 1e-06
QSTEP = 2.0
SINE = (
    0.9999995827674866,
    -6.579691410064697,
    12.986429214477539,
    -12.18803596496582,
    6.557779312133789,
    -1.952649712562561,
)
BF16 = jnp.bfloat16
F32 = jnp.float32
BITS = ("b4", "b3", "b2", "b1", "b0")
GROUP = 8
VMEM_BYTES = 16 * 2**20
ALL_VMEM = 60 * 2**20


def dot(left, right, left_dim, right_dim):
    return lax.dot_general(
        left, right, (((left_dim,), (right_dim,)), ((), ())), preferred_element_type=F32
    )


def sylvester(block_len):
    positions = jnp.arange(block_len, dtype=jnp.int32)
    common_bits = positions[:, None] & positions[None, :]
    parity = jnp.zeros((block_len, block_len), jnp.int32)
    for bit_pos in range(block_len.bit_length() - 1):
        parity = parity ^ common_bits >> bit_pos & 1
    return (1 - 2 * parity).astype(BF16)


def pick_kernel(
    capacity, routes_in, weights_in, tok_in, grad_in, out_ref, routes_ref, weights_ref, tok_ref, grad_ref, sems
):
    loads = [
        pltpu.make_async_copy(src, dst, sems.at[k])
        for k, (src, dst) in enumerate(
            ((routes_in, routes_ref), (weights_in, weights_ref), (tok_in, tok_ref), (grad_in, grad_ref))
        )
    ]
    for load in loads:
        load.start()
    choices, tok_count = routes_ref.shape
    block = 2 * capacity
    out_rows = out_ref.shape[0]
    experts = out_rows // block

    row = lax.broadcasted_iota(jnp.int32, (out_rows, experts), 0)
    start = lax.broadcasted_iota(jnp.int32, (out_rows, experts), 1) * block
    owns = (row >= start) & (row < start + block)
    spread = jnp.where(owns, 1.0, 0.0).astype(BF16)
    place = jnp.sum(jnp.where(owns, row - start, 0).astype(F32), axis=1, keepdims=True)
    is_tok = place < capacity
    tok_place = jnp.where(is_tok, place, -2.0)
    grad_place = jnp.where(is_tok, -2.0, place - capacity)
    square = (tok_count, tok_count)
    earlier = lax.broadcasted_iota(jnp.int32, square, 0) < lax.broadcasted_iota(jnp.int32, square, 1)
    earlier = jnp.where(earlier, 1.0, 0.0).astype(BF16)
    expert_ids = lax.broadcasted_iota(jnp.int32, (experts, tok_count), 0)

    for load in loads:
        load.wait()
    member = jnp.zeros((experts, tok_count), F32)
    weight = jnp.zeros((experts, tok_count), F32)
    for k in range(choices):
        hit = routes_ref[k : k + 1, :] == expert_ids
        member = member + jnp.where(hit, 1.0, 0.0)
        weight = weight + jnp.where(hit, weights_ref[k : k + 1, :], 0.0)
    rank = dot(member.astype(BF16), earlier, 1, 0)
    rank = jnp.where(member > 0.0, rank, -1.0).astype(BF16)
    weight_hi = weight.astype(BF16)
    weight_lo = (weight - weight_hi.astype(F32)).astype(BF16)
    rank_of = dot(spread, rank, 1, 0)
    tok_pick = jnp.where(rank_of == tok_place, 1.0, 0.0).astype(BF16)
    grad_here = rank_of == grad_place
    hi = jnp.where(grad_here, dot(spread, weight_hi, 1, 0), 0.0).astype(BF16)
    lo = jnp.where(grad_here, dot(spread, weight_lo, 1, 0), 0.0).astype(BF16)
    out = dot(tok_pick, tok_ref[...], 1, 0)
    out = out + dot(hi, grad_ref[...], 1, 0) + dot(lo, grad_ref[...], 1, 0)
    out_ref[...] = out.astype(BF16)


def call(kernel, name, out_shapes, operands, scalars=0, in_hbm=False, scratch=(), dtype=BF16):
    smem = pl.BlockSpec(memory_space=pltpu.SMEM)
    rest = pl.BlockSpec(memory_space=pltpu.HBM) if in_hbm else pl.BlockSpec(memory_space=pltpu.VMEM)
    outs = [jax.ShapeDtypeStruct(shape, dtype) for shape in out_shapes]
    flops = 2 * 384 * 768 * 768
    moved = sum(v.size * 2 for v in list(operands) + outs)
    return pl.pallas_call(
        kernel,
        out_shape=outs,
        in_specs=[smem] * scalars + [rest] * (len(operands) - scalars),
        out_specs=[pl.BlockSpec(memory_space=pltpu.VMEM)] * len(outs),
        scratch_shapes=list(scratch),
        compiler_params=pltpu.CompilerParams(vmem_limit_bytes=ALL_VMEM if in_hbm else VMEM_BYTES),
        cost_estimate=pl.CostEstimate(flops=flops, bytes_accessed=moved, transcendentals=0),
        name=name,
    )(*operands)


def pick_rows(routes, weights, tokens, out_grad, experts, capacity):
    operands = (routes.T, weights.T, tokens, out_grad)
    out = call(
        functools.partial(pick_kernel, capacity),
        "pick_rows",
        [(2 * capacity * experts, tokens.shape[1])],
        operands,
        in_hbm=True,
        scratch=[pltpu.VMEM(v.shape, v.dtype) for v in operands] + [pltpu.SemaphoreType.DMA((4,))],
    )[0]
    return out.reshape(experts, 2 * capacity, tokens.shape[1])


def copies_kernel(in_ref, out_ref, sems):
    stores = [pltpu.make_async_copy(in_ref, out_ref.at[k], sems.at[k]) for k in range(out_ref.shape[0])]
    for store in stores:
        store.start()
    for store in stores:
        store.wait()


def copies(x, count):
    return pl.pallas_call(
        copies_kernel,
        out_shape=jax.ShapeDtypeStruct((count,) + x.shape, x.dtype),
        in_specs=[pl.BlockSpec(memory_space=pltpu.VMEM)],
        out_specs=pl.BlockSpec(memory_space=pl.ANY),
        scratch_shapes=[pltpu.SemaphoreType.DMA((count,))],
        compiler_params=pltpu.CompilerParams(vmem_limit_bytes=VMEM_BYTES),
        name="copies",
    )(x)


def side(which, size):
    return pl.ds(pl.multiple_of(which * size, size), size)


def away_kernel(capacity, core_ref, gate_ref, up_ref, down_ref, recv_ref, out_ref, rows_ref):
    rows = rows_ref.shape[0] // 2
    size = GROUP * capacity
    row = lax.broadcasted_iota(jnp.int32, (size, GROUP), 0)
    start = lax.broadcasted_iota(jnp.int32, (size, GROUP), 1) * capacity
    inside = (row >= start) & (row < start + capacity)
    source = jnp.sum(jnp.where(inside, row + start, 0).astype(F32), axis=1, keepdims=True)
    column = lax.broadcasted_iota(jnp.int32, (size, 2 * size), 1).astype(F32)
    for k, place in enumerate((source, source + capacity)):
        pick = jnp.where(column == place, 1.0, 0.0).astype(BF16)
        for g in range(rows // size):
            block = recv_ref[2 * g * size : 2 * (g + 1) * size, :]
            rows_ref[k * rows + g * size : k * rows + (g + 1) * size, :] = dot(pick, block, 1, 0).astype(BF16)
    units = out_ref.shape[0]
    cut = side(1 - core_ref[0], units)
    out_ref[:, :rows] = dot(gate_ref[cut, :], rows_ref[:rows, :], 1, 1).astype(BF16)
    out_ref[:, rows : 2 * rows] = dot(up_ref[cut, :], rows_ref[:rows, :], 1, 1).astype(BF16)
    out_ref[:, 2 * rows :] = dot(down_ref[cut, :], rows_ref[rows:, :], 1, 1).astype(BF16)


def keep_kernel(core_ref, gate_ref, up_ref, down_ref, rows_ref, out_ref):
    units, rows = out_ref.shape[0], rows_ref.shape[0] // 2
    cut = side(core_ref[0], units)
    out_ref[:, :rows] = dot(gate_ref[cut, :], rows_ref[:rows, :], 1, 1)
    out_ref[:, rows : 2 * rows] = dot(up_ref[cut, :], rows_ref[:rows, :], 1, 1)
    out_ref[:, 2 * rows :] = dot(down_ref[cut, :], rows_ref[rows:, :], 1, 1)


def half_back(units_ref, weight_refs, cut, rows):
    gate, up = units_ref[:, :rows], units_ref[:, rows : 2 * rows]
    width = sum(ref.shape[0] for ref in weight_refs) // 2
    parts = []
    done = 0
    for ref in weight_refs:
        for_gate = min(max(width - done, 0), ref.shape[0])
        if for_gate > 0:
            parts.append(dot(ref[:for_gate, cut], gate, 1, 0))
        if for_gate < ref.shape[0]:
            upper = dot(ref[for_gate:, cut], up, 1, 0)
        done += ref.shape[0]
    return jnp.concatenate(parts, 0) + upper


def mine_back_kernel(core_ref, mine_ref, *refs):
    weight_refs, out_ref = refs[:-1], refs[-1]
    units, rows = mine_ref.shape[0], out_ref.shape[1]
    out_ref[...] = half_back(mine_ref, weight_refs, side(core_ref[0], units), rows)


def back_kernel(capacity, core_ref, theirs_ref, *refs):
    weight_refs, (total_ref, out_ref) = refs[:-2], refs[-2:]
    units, rows = theirs_ref.shape[0], total_ref.shape[1]
    out_rows = out_ref.shape[0]
    total = total_ref[...] + half_back(theirs_ref, weight_refs, side(1 - core_ref[0], units), rows)
    groups = rows // capacity
    padded = out_rows // groups
    row = lax.broadcasted_iota(jnp.int32, (out_rows, groups), 0)
    group = lax.broadcasted_iota(jnp.int32, (out_rows, groups), 1)
    inside = (row >= group * padded) & (row < group * padded + capacity)
    source = jnp.where(inside, row - group * (padded - capacity) + 1, 0).astype(F32)
    source = jnp.sum(source, axis=1, keepdims=True) - 1.0
    column = lax.broadcasted_iota(jnp.int32, (out_rows, rows), 1).astype(F32)
    place = jnp.where(column == source, 1.0, 0.0).astype(BF16)
    out_ref[...] = dot(place, total.astype(BF16), 1, 1).astype(BF16)


def soft_rotate(block, rotation):
    rotated = dot(block, rotation, 1, 0)
    meansq = jnp.sum(rotated * rotated, axis=1, keepdims=True) * (1.0 / HBLOCK) + EPS
    steps = rotated * (QSTEP * lax.rsqrt(meansq))
    near = steps - jnp.round(steps)
    square = near * near
    series = square * SINE[-1] + SINE[-2]
    for term in SINE[-3::-1]:
        series = series * square + term
    return ((steps - near * series) * (jnp.sqrt(meansq) / QSTEP)).astype(BF16)


def grads_kernel(
    core_ref, mine_ref, theirs_ref, rows_ref, rotation_ref, gate_ref, up_ref, down_ref, in_q, grad_q, gate_q, up_q, hid_q
):
    units, rows = mine_ref.shape[0], mine_ref.shape[1] // 3
    width = in_q.shape[0]
    rotation = rotation_ref[...]
    core = core_ref[0]
    scale = 1.0 / HBLOCK
    for b in range(rows // HBLOCK):
        cut = slice(b * HBLOCK, (b + 1) * HBLOCK)
        in_q[:, cut] = soft_rotate(rows_ref[:width, cut], rotation)
        grad_q[:, cut] = soft_rotate(rows_ref[width:, cut], rotation)
    for ref, which in ((mine_ref, core), (theirs_ref, 1 - core)):
        place = side(which, units)
        for k, dst in enumerate((gate_q, up_q, hid_q)):
            for b in range(rows // HBLOCK):
                cut = slice(b * HBLOCK, (b + 1) * HBLOCK)
                lanes = slice(k * rows + b * HBLOCK, k * rows + (b + 1) * HBLOCK)
                dst[:, cut] = soft_rotate(ref[:, lanes], rotation)
        gate_ref[:, place] = (dot(in_q[...], gate_q[...], 1, 1) * scale).astype(BF16)
        up_ref[:, place] = (dot(in_q[...], up_q[...], 1, 1) * scale).astype(BF16)
        down_ref[place, :] = (dot(hid_q[...], grad_q[...], 1, 1) * scale).astype(BF16)


def slot_picker(routes, expert_count, capacity):
    experts_iota = jnp.arange(expert_count, dtype=jnp.int32)
    member = jnp.sum((routes[:, :, None] == experts_iota[None, None, :]).astype(jnp.int32), axis=1)
    rank_table = jnp.cumsum(member, axis=0) - member
    cap_iota = jnp.arange(capacity, dtype=jnp.int32)
    placed = (rank_table[:, :, None] == cap_iota[None, None, :]) & (member[:, :, None] == 1)
    return jnp.transpose(placed.astype(BF16), (1, 2, 0))


def pair_permute(x, axis):
    return lax.ppermute(x, axis, [(0, 1), (1, 0)])


def by_pair(which, alone, paired, *operands):
    branches = [alone] + [functools.partial(paired, axis) for axis in BITS[::-1]]
    return lax.switch(which, branches, *operands)


def swap(which, x):
    def paired(axis, v):
        return jax.tree.map(lambda leaf: pair_permute(leaf, axis), v)

    return by_pair(which, lambda v: v, paired, x)


def shards(
    tokens, out_grad, routes, route_weights, gate_weight, up_weight, down_weight, sign_bits, partner
):
    experts = lax.axis_size(BITS)
    n_y = lax.axis_size("y")
    core = lax.axis_index("core")
    me = lax.axis_index(BITS)
    mate = partner[me]
    apart = me ^ mate
    which = sum((apart == 1 << k).astype(jnp.int32) * (k + 1) for k in range(len(BITS)))
    tok_count, width = tokens.shape
    capacity = min(tok_count, tok_count * routes.shape[1] * 3 // (2 * experts))
    rows = experts * capacity
    ff = gate_weight.shape[2]
    half = ff // 2
    core_arg = core.astype(jnp.int32)[None]

    gate_w, up_w, down_w = gate_weight[0], up_weight[0], down_weight[0]
    send = pick_rows(routes, route_weights, tokens, out_grad, experts, capacity)
    recv = lax.all_to_all(send, BITS, 0, 0, tiled=True)
    gate_t, up_t = gate_w.T, up_w.T
    cut_1, cut_2 = width // 4, width * 5 // 8
    weight_2 = gate_w[cut_1:cut_2]
    weight_3 = jnp.concatenate([gate_w[cut_2:], up_w], 0)
    weight_1 = swap(which, gate_w[:cut_1])
    recv, weight_1, weight_2, weight_3, gate_t, up_t = lax.optimization_barrier(
        (recv, weight_1, weight_2, weight_3, gate_t, up_t)
    )
    recv = recv.reshape(2 * rows, width)

    feeds = (core_arg, gate_t, up_t, down_w)
    wide = (half, 3 * rows)
    away, routed = call(
        functools.partial(away_kernel, capacity), "away_partials", [wide, recv.shape], feeds + (recv,), 1
    )
    arrived = pair_permute(away, "core")
    kept = call(keep_kernel, "keep_partials", [wide], feeds + (routed,), 1, dtype=F32)[0]
    chip_sum = (kept + arrived.astype(F32)).astype(BF16)

    chip_sum, routed, weight_2 = lax.optimization_barrier((chip_sum, routed, weight_2))

    piece = (half // n_y, 3 * rows)
    blocks = lax.all_to_all(chip_sum.reshape((n_y,) + piece), "y", 0, 0, tiled=True)
    mate_routed, weight_2, routes, sign_bits = lax.optimization_barrier(
        swap(which, (routed, weight_2)) + (routes, sign_bits)
    )
    padded = -(-capacity // 16) * 16
    picker = jnp.take(slot_picker(routes, experts, capacity), partner, axis=0)
    picker = jnp.pad(picker, ((0, 0), (0, padded - capacity), (0, 0))).reshape(experts * padded, tok_count)
    flip_signs = (1 - 2 * lax.dynamic_index_in_dim(sign_bits, mate, 0, keepdims=False)).astype(BF16)
    rotation = sylvester(HBLOCK) * flip_signs[:, None]
    mate_rows = jnp.concatenate([mate_routed[:rows].T, mate_routed[rows:].T], 0)
    blocks, mate_rows, weight_2, picker, rotation = lax.optimization_barrier(
        (blocks, mate_rows, weight_2, picker, rotation)
    )
    sums = jnp.sum(blocks.astype(F32), axis=0)
    gate_sum, up_sum, hid_grad = sums[:, :rows], sums[:, rows : 2 * rows], sums[:, 2 * rows :]
    sig = jax.nn.sigmoid(gate_sum)
    silu = gate_sum * sig
    gate_rows = hid_grad * up_sum * sig * (1.0 + gate_sum * (1.0 - sig))
    acts = jnp.concatenate([gate_rows, hid_grad * silu, silu * up_sum], 1).astype(BF16)

    acts, weight_3 = lax.optimization_barrier((swap(which, acts), weight_3))
    mine = lax.all_to_all(copies(acts, n_y), "y", 0, 0, tiled=True).reshape(wide)
    weight_3 = swap(which, weight_3)
    mine, weight_3 = lax.optimization_barrier((mine, weight_3))
    theirs = pair_permute(mine, "core")

    weights = (weight_1, weight_2, weight_3)
    mine_back = call(
        mine_back_kernel, "mine_back", [(width, rows)], (core_arg, mine) + weights, 1, dtype=F32
    )[0]
    slot_back = call(
        functools.partial(back_kernel, capacity),
        "slot_back",
        [(experts * padded, width)],
        (core_arg, theirs) + weights + (mine_back,),
        1,
    )[0]
    returned = lax.all_to_all(slot_back.reshape(experts, padded, width), BITS, 0, 0, tiled=True)
    input_grad = dot(picker, returned.reshape(experts * padded, width), 0, 0).astype(BF16)

    gate_new, up_new, down_new = call(
        grads_kernel,
        "weight_grads",
        [(width, ff), (width, ff), (ff, width)],
        (core_arg, mine, theirs, mate_rows, rotation),
        1,
        scratch=[pltpu.VMEM((n, rows), BF16) for n in (width, width, half, half, half)],
    )
    return gate_new[None], up_new[None], down_new[None], input_grad


def solution(mesh):
    n_dp = mesh.shape["dp"]
    split = Mesh(mesh.devices.reshape((n_dp // 2, 2) + (2,) * len(BITS)), ("y", "core") + BITS)
    dp = ("y", "core")
    return jax.shard_map(
        shards,
        mesh=split,
        in_specs=(
            P(BITS, dp),
            P(BITS, dp),
            P(BITS, None),
            P(BITS, None),
            P(BITS, dp, None),
            P(BITS, dp, None),
            P(BITS, None, dp),
            P(),
            P(),
        ),
        out_specs=(
            P(BITS, dp, None),
            P(BITS, dp, None),
            P(BITS, None, dp),
            P(BITS, dp),
        ),
        check_vma=False,
    )
```

```python
import functools

import jax
import jax.numpy as jnp
from jax import lax
from jax.experimental import pallas as pl
from jax.experimental.pallas import tpu as pltpu
from jax.sharding import Mesh
from jax.sharding import PartitionSpec as P

HBLOCK = 128
EPS = 1e-06
QSTEP = 2.0
SINE = (
    0.9999995827674866,
    -6.579691410064697,
    12.986429214477539,
    -12.18803596496582,
    6.557779312133789,
    -1.952649712562561,
)
BF16 = jnp.bfloat16
F32 = jnp.float32
BITS = ("b4", "b3", "b2", "b1", "b0")
GROUP = 8
VMEM_BYTES = 16 * 2**20
ALL_VMEM = 60 * 2**20


def dot(left, right, left_dim, right_dim):
    return lax.dot_general(
        left, right, (((left_dim,), (right_dim,)), ((), ())), preferred_element_type=F32
    )


def sylvester(block_len):
    positions = jnp.arange(block_len, dtype=jnp.int32)
    common_bits = positions[:, None] & positions[None, :]
    parity = jnp.zeros((block_len, block_len), jnp.int32)
    for bit_pos in range(block_len.bit_length() - 1):
        parity = parity ^ common_bits >> bit_pos & 1
    return (1 - 2 * parity).astype(BF16)


def pick_kernel(
    capacity, routes_in, weights_in, tok_in, grad_in, out_ref, routes_ref, weights_ref, tok_ref, grad_ref, sems
):
    loads = [
        pltpu.make_async_copy(src, dst, sems.at[k])
        for k, (src, dst) in enumerate(
            ((routes_in, routes_ref), (weights_in, weights_ref), (tok_in, tok_ref), (grad_in, grad_ref))
        )
    ]
    for load in loads:
        load.start()
    choices, tok_count = routes_ref.shape
    block = 2 * capacity
    out_rows = out_ref.shape[0]
    experts = out_rows // block

    row = lax.broadcasted_iota(jnp.int32, (out_rows, experts), 0)
    start = lax.broadcasted_iota(jnp.int32, (out_rows, experts), 1) * block
    owns = (row >= start) & (row < start + block)
    spread = jnp.where(owns, 1.0, 0.0).astype(BF16)
    place = jnp.sum(jnp.where(owns, row - start, 0).astype(F32), axis=1, keepdims=True)
    is_tok = place < capacity
    tok_place = jnp.where(is_tok, place, -2.0)
    grad_place = jnp.where(is_tok, -2.0, place - capacity)
    square = (tok_count, tok_count)
    earlier = lax.broadcasted_iota(jnp.int32, square, 0) < lax.broadcasted_iota(jnp.int32, square, 1)
    earlier = jnp.where(earlier, 1.0, 0.0).astype(BF16)
    expert_ids = lax.broadcasted_iota(jnp.int32, (experts, tok_count), 0)

    for load in loads:
        load.wait()
    member = jnp.zeros((experts, tok_count), F32)
    weight = jnp.zeros((experts, tok_count), F32)
    for k in range(choices):
        hit = routes_ref[k : k + 1, :] == expert_ids
        member = member + jnp.where(hit, 1.0, 0.0)
        weight = weight + jnp.where(hit, weights_ref[k : k + 1, :], 0.0)
    rank = dot(member.astype(BF16), earlier, 1, 0)
    rank = jnp.where(member > 0.0, rank, -1.0).astype(BF16)
    weight_hi = weight.astype(BF16)
    weight_lo = (weight - weight_hi.astype(F32)).astype(BF16)
    rank_of = dot(spread, rank, 1, 0)
    tok_pick = jnp.where(rank_of == tok_place, 1.0, 0.0).astype(BF16)
    grad_here = rank_of == grad_place
    hi = jnp.where(grad_here, dot(spread, weight_hi, 1, 0), 0.0).astype(BF16)
    lo = jnp.where(grad_here, dot(spread, weight_lo, 1, 0), 0.0).astype(BF16)
    out = dot(tok_pick, tok_ref[...], 1, 0)
    out = out + dot(hi, grad_ref[...], 1, 0) + dot(lo, grad_ref[...], 1, 0)
    out_ref[...] = out.astype(BF16)


def call(kernel, name, out_shapes, operands, scalars=0, in_hbm=False, scratch=(), dtype=BF16):
    smem = pl.BlockSpec(memory_space=pltpu.SMEM)
    rest = pl.BlockSpec(memory_space=pltpu.HBM) if in_hbm else pl.BlockSpec(memory_space=pltpu.VMEM)
    outs = [jax.ShapeDtypeStruct(shape, dtype) for shape in out_shapes]
    flops = 2 * 384 * 768 * 768
    moved = sum(v.size * 2 for v in list(operands) + outs)
    return pl.pallas_call(
        kernel,
        out_shape=outs,
        in_specs=[smem] * scalars + [rest] * (len(operands) - scalars),
        out_specs=[pl.BlockSpec(memory_space=pltpu.VMEM)] * len(outs),
        scratch_shapes=list(scratch),
        compiler_params=pltpu.CompilerParams(vmem_limit_bytes=ALL_VMEM if in_hbm else VMEM_BYTES),
        cost_estimate=pl.CostEstimate(flops=flops, bytes_accessed=moved, transcendentals=0),
        name=name,
    )(*operands)


def pick_rows(routes, weights, tokens, out_grad, experts, capacity):
    operands = (routes.T, weights.T, tokens, out_grad)
    out = call(
        functools.partial(pick_kernel, capacity),
        "pick_rows",
        [(2 * capacity * experts, tokens.shape[1])],
        operands,
        in_hbm=True,
        scratch=[pltpu.VMEM(v.shape, v.dtype) for v in operands] + [pltpu.SemaphoreType.DMA((4,))],
    )[0]
    return out.reshape(experts, 2 * capacity, tokens.shape[1])


def copies_kernel(in_ref, out_ref, sems):
    stores = [pltpu.make_async_copy(in_ref, out_ref.at[k], sems.at[k]) for k in range(out_ref.shape[0])]
    for store in stores:
        store.start()
    for store in stores:
        store.wait()


def copies(x, count):
    return pl.pallas_call(
        copies_kernel,
        out_shape=jax.ShapeDtypeStruct((count,) + x.shape, x.dtype),
        in_specs=[pl.BlockSpec(memory_space=pltpu.VMEM)],
        out_specs=pl.BlockSpec(memory_space=pl.ANY),
        scratch_shapes=[pltpu.SemaphoreType.DMA((count,))],
        compiler_params=pltpu.CompilerParams(vmem_limit_bytes=VMEM_BYTES),
        name="copies",
    )(x)


def side(which, size):
    return pl.ds(pl.multiple_of(which * size, size), size)


def away_kernel(capacity, core_ref, gate_ref, up_ref, down_ref, recv_ref, out_ref, rows_ref):
    rows = rows_ref.shape[0] // 2
    size = GROUP * capacity
    row = lax.broadcasted_iota(jnp.int32, (size, GROUP), 0)
    start = lax.broadcasted_iota(jnp.int32, (size, GROUP), 1) * capacity
    inside = (row >= start) & (row < start + capacity)
    source = jnp.sum(jnp.where(inside, row + start, 0).astype(F32), axis=1, keepdims=True)
    column = lax.broadcasted_iota(jnp.int32, (size, 2 * size), 1).astype(F32)
    for k, place in enumerate((source, source + capacity)):
        pick = jnp.where(column == place, 1.0, 0.0).astype(BF16)
        for g in range(rows // size):
            block = recv_ref[2 * g * size : 2 * (g + 1) * size, :]
            rows_ref[k * rows + g * size : k * rows + (g + 1) * size, :] = dot(pick, block, 1, 0).astype(BF16)
    units = out_ref.shape[0]
    cut = side(1 - core_ref[0], units)
    out_ref[:, :rows] = dot(gate_ref[cut, :], rows_ref[:rows, :], 1, 1).astype(BF16)
    out_ref[:, rows : 2 * rows] = dot(up_ref[cut, :], rows_ref[:rows, :], 1, 1).astype(BF16)
    out_ref[:, 2 * rows :] = dot(down_ref[cut, :], rows_ref[rows:, :], 1, 1).astype(BF16)


def keep_kernel(core_ref, gate_ref, up_ref, down_ref, rows_ref, out_ref):
    units, rows = out_ref.shape[0], rows_ref.shape[0] // 2
    cut = side(core_ref[0], units)
    out_ref[:, :rows] = dot(gate_ref[cut, :], rows_ref[:rows, :], 1, 1).astype(BF16)
    out_ref[:, rows : 2 * rows] = dot(up_ref[cut, :], rows_ref[:rows, :], 1, 1).astype(BF16)
    out_ref[:, 2 * rows :] = dot(down_ref[cut, :], rows_ref[rows:, :], 1, 1).astype(BF16)


def half_back(units_ref, weight_ref, cut, rows):
    width = weight_ref.shape[0] // 2
    part = dot(weight_ref[:width, cut], units_ref[:, :rows], 1, 0)
    return part + dot(weight_ref[width:, cut], units_ref[:, rows : 2 * rows], 1, 0)


def mine_back_kernel(core_ref, mine_ref, weight_ref, out_ref):
    units, rows = mine_ref.shape[0], out_ref.shape[1]
    out_ref[...] = half_back(mine_ref, weight_ref, side(core_ref[0], units), rows)


def back_kernel(capacity, core_ref, theirs_ref, weight_ref, total_ref, out_ref):
    units, rows = theirs_ref.shape[0], total_ref.shape[1]
    out_rows = out_ref.shape[0]
    total = total_ref[...] + half_back(theirs_ref, weight_ref, side(1 - core_ref[0], units), rows)
    groups = rows // capacity
    padded = out_rows // groups
    row = lax.broadcasted_iota(jnp.int32, (out_rows, groups), 0)
    group = lax.broadcasted_iota(jnp.int32, (out_rows, groups), 1)
    inside = (row >= group * padded) & (row < group * padded + capacity)
    source = jnp.where(inside, row - group * (padded - capacity) + 1, 0).astype(F32)
    source = jnp.sum(source, axis=1, keepdims=True) - 1.0
    column = lax.broadcasted_iota(jnp.int32, (out_rows, rows), 1).astype(F32)
    place = jnp.where(column == source, 1.0, 0.0).astype(BF16)
    out_ref[...] = dot(place, total.astype(BF16), 1, 1).astype(BF16)


def soft_rotate(block, rotation):
    rotated = dot(block, rotation, 1, 0)
    meansq = jnp.sum(rotated * rotated, axis=1, keepdims=True) * (1.0 / HBLOCK) + EPS
    steps = rotated * (QSTEP * lax.rsqrt(meansq))
    near = steps - jnp.round(steps)
    square = near * near
    series = square * SINE[-1] + SINE[-2]
    for term in SINE[-3::-1]:
        series = series * square + term
    return ((steps - near * series) * (jnp.sqrt(meansq) / QSTEP)).astype(BF16)


def grads_kernel(
    core_ref, mine_ref, theirs_ref, rows_ref, rotation_ref, gate_ref, up_ref, down_ref, in_q, grad_q, gate_q, up_q, hid_q
):
    units, rows = mine_ref.shape[0], mine_ref.shape[1] // 3
    width = in_q.shape[0]
    rotation = rotation_ref[...]
    core = core_ref[0]
    scale = 1.0 / HBLOCK
    for b in range(rows // HBLOCK):
        cut = slice(b * HBLOCK, (b + 1) * HBLOCK)
        in_q[:, cut] = soft_rotate(rows_ref[:width, cut], rotation)
        grad_q[:, cut] = soft_rotate(rows_ref[width:, cut], rotation)
    for ref, which in ((mine_ref, core), (theirs_ref, 1 - core)):
        place = side(which, units)
        for k, dst in enumerate((gate_q, up_q, hid_q)):
            for b in range(rows // HBLOCK):
                cut = slice(b * HBLOCK, (b + 1) * HBLOCK)
                lanes = slice(k * rows + b * HBLOCK, k * rows + (b + 1) * HBLOCK)
                dst[:, cut] = soft_rotate(ref[:, lanes], rotation)
        gate_ref[:, place] = (dot(in_q[...], gate_q[...], 1, 1) * scale).astype(BF16)
        up_ref[:, place] = (dot(in_q[...], up_q[...], 1, 1) * scale).astype(BF16)
        down_ref[place, :] = (dot(hid_q[...], grad_q[...], 1, 1) * scale).astype(BF16)


def slot_picker(routes, expert_count, capacity):
    experts_iota = jnp.arange(expert_count, dtype=jnp.int32)
    member = jnp.sum((routes[:, :, None] == experts_iota[None, None, :]).astype(jnp.int32), axis=1)
    rank_table = jnp.cumsum(member, axis=0) - member
    cap_iota = jnp.arange(capacity, dtype=jnp.int32)
    placed = (rank_table[:, :, None] == cap_iota[None, None, :]) & (member[:, :, None] == 1)
    return jnp.transpose(placed.astype(BF16), (1, 2, 0))


def pair_permute(x, axis):
    return lax.ppermute(x, axis, [(0, 1), (1, 0)])


def by_pair(which, alone, paired, *operands):
    branches = [alone] + [functools.partial(paired, axis) for axis in BITS[::-1]]
    return lax.switch(which, branches, *operands)


def swap(which, x):
    def paired(axis, v):
        return jax.tree.map(lambda leaf: pair_permute(leaf, axis), v)

    return by_pair(which, lambda v: v, paired, x)


def shards(
    tokens, out_grad, routes, route_weights, gate_weight, up_weight, down_weight, sign_bits, partner
):
    experts = lax.axis_size(BITS)
    n_y = lax.axis_size("y")
    core = lax.axis_index("core")
    me = lax.axis_index(BITS)
    mate = partner[me]
    apart = me ^ mate
    which = sum((apart == 1 << k).astype(jnp.int32) * (k + 1) for k in range(len(BITS)))
    tok_count, width = tokens.shape
    capacity = min(tok_count, tok_count * routes.shape[1] * 3 // (2 * experts))
    rows = experts * capacity
    ff = gate_weight.shape[2]
    half = ff // 2
    core_arg = core.astype(jnp.int32)[None]

    gate_w, up_w, down_w = gate_weight[0], up_weight[0], down_weight[0]
    send = pick_rows(routes, route_weights, tokens, out_grad, experts, capacity)
    recv = lax.all_to_all(send, BITS, 0, 0, tiled=True)
    gate_t, up_t = gate_w.T, up_w.T
    cut_1, cut_2 = width // 4, width * 5 // 8
    weight_2 = gate_w[cut_1:cut_2]
    weight_3 = jnp.concatenate([gate_w[cut_2:], up_w], 0)
    weight_1 = swap(which, gate_w[:cut_1])
    recv, weight_1, weight_2, weight_3, gate_t, up_t = lax.optimization_barrier(
        (recv, weight_1, weight_2, weight_3, gate_t, up_t)
    )
    recv = recv.reshape(2 * rows, width)

    feeds = (core_arg, gate_t, up_t, down_w)
    wide = (half, 3 * rows)
    away, routed = call(
        functools.partial(away_kernel, capacity), "away_partials", [wide, recv.shape], feeds + (recv,), 1
    )
    arrived = pair_permute(away, "core")
    kept = call(keep_kernel, "keep_partials", [wide], feeds + (routed,), 1)[0]
    chip_sum = (kept.astype(F32) + arrived.astype(F32)).astype(BF16)

    chip_sum, routed, weight_2 = lax.optimization_barrier((chip_sum, routed, weight_2))

    piece = (half // n_y, 3 * rows)
    blocks = lax.all_to_all(chip_sum.reshape((n_y,) + piece), "y", 0, 0, tiled=True)
    mate_routed, weight_2 = swap(which, (routed, weight_2))
    padded = -(-capacity // 16) * 16
    picker = jnp.take(slot_picker(routes, experts, capacity), partner, axis=0)
    picker = jnp.pad(picker, ((0, 0), (0, padded - capacity), (0, 0))).reshape(experts * padded, tok_count)
    flip_signs = (1 - 2 * lax.dynamic_index_in_dim(sign_bits, mate, 0, keepdims=False)).astype(BF16)
    rotation = sylvester(HBLOCK) * flip_signs[:, None]
    blocks, mate_routed, weight_2, picker, rotation = lax.optimization_barrier(
        (blocks, mate_routed, weight_2, picker, rotation)
    )
    sums = jnp.sum(blocks.astype(F32), axis=0)
    gate_sum, up_sum, hid_grad = sums[:, :rows], sums[:, rows : 2 * rows], sums[:, 2 * rows :]
    sig = jax.nn.sigmoid(gate_sum)
    silu = gate_sum * sig
    gate_rows = hid_grad * up_sum * sig * (1.0 + gate_sum * (1.0 - sig))
    acts = jnp.concatenate([gate_rows, hid_grad * silu, silu * up_sum], 1).astype(BF16)

    acts, weight_3 = lax.optimization_barrier((swap(which, acts), weight_3))
    mine = lax.all_to_all(copies(acts, n_y), "y", 0, 0, tiled=True).reshape(wide)
    weight_3 = swap(which, weight_3)
    mate_rows = jnp.concatenate([mate_routed[:rows].T, mate_routed[rows:].T], 0)
    weights = jnp.concatenate([weight_1, weight_2, weight_3], 0)
    mine, weights, mate_rows = lax.optimization_barrier((mine, weights, mate_rows))
    theirs = pair_permute(mine, "core")

    mine_back = call(
        mine_back_kernel, "mine_back", [(width, rows)], (core_arg, mine, weights), 1, dtype=F32
    )[0]
    slot_back = call(
        functools.partial(back_kernel, capacity),
        "slot_back",
        [(experts * padded, width)],
        (core_arg, theirs, weights, mine_back),
        1,
    )[0]
    returned = lax.all_to_all(slot_back.reshape(experts, padded, width), BITS, 0, 0, tiled=True)
    input_grad = dot(picker, returned.reshape(experts * padded, width), 0, 0).astype(BF16)

    gate_new, up_new, down_new = call(
        grads_kernel,
        "weight_grads",
        [(width, ff), (width, ff), (ff, width)],
        (core_arg, mine, theirs, mate_rows, rotation),
        1,
        scratch=[pltpu.VMEM((n, rows), BF16) for n in (width, width, half, half, half)],
    )
    return gate_new[None], up_new[None], down_new[None], input_grad


def solution(mesh):
    n_dp = mesh.shape["dp"]
    split = Mesh(mesh.devices.reshape((n_dp // 2, 2) + (2,) * len(BITS)), ("y", "core") + BITS)
    dp = ("y", "core")
    return jax.shard_map(
        shards,
        mesh=split,
        in_specs=(
            P(BITS, dp),
            P(BITS, dp),
            P(BITS, None),
            P(BITS, None),
            P(BITS, dp, None),
            P(BITS, dp, None),
            P(BITS, None, dp),
            P(),
            P(),
        ),
        out_specs=(
            P(BITS, dp, None),
            P(BITS, dp, None),
            P(BITS, None, dp),
            P(BITS, dp),
        ),
        check_vma=False,
    )
```

```python
import functools

import jax
import jax.numpy as jnp
from jax import lax
from jax.experimental import pallas as pl
from jax.experimental.pallas import tpu as pltpu
from jax.sharding import Mesh
from jax.sharding import PartitionSpec as P

HBLOCK = 128
EPS = 1e-06
QSTEP = 2.0
SINE = (
    0.9999995827674866,
    -6.579691410064697,
    12.986429214477539,
    -12.18803596496582,
    6.557779312133789,
    -1.952649712562561,
)
BF16 = jnp.bfloat16
F32 = jnp.float32
BITS = ("b4", "b3", "b2", "b1", "b0")
GROUP = 8
VMEM_BYTES = 16 * 2**20
ALL_VMEM = 60 * 2**20


def dot(left, right, left_dim, right_dim):
    return lax.dot_general(
        left, right, (((left_dim,), (right_dim,)), ((), ())), preferred_element_type=F32
    )


def sylvester(block_len):
    positions = jnp.arange(block_len, dtype=jnp.int32)
    common_bits = positions[:, None] & positions[None, :]
    parity = jnp.zeros((block_len, block_len), jnp.int32)
    for bit_pos in range(block_len.bit_length() - 1):
        parity = parity ^ common_bits >> bit_pos & 1
    return (1 - 2 * parity).astype(BF16)


def pick_kernel(
    capacity, routes_in, weights_in, tok_in, grad_in, out_ref, routes_ref, weights_ref, tok_ref, grad_ref, sems
):
    loads = [
        pltpu.make_async_copy(src, dst, sems.at[k])
        for k, (src, dst) in enumerate(
            ((routes_in, routes_ref), (weights_in, weights_ref), (tok_in, tok_ref), (grad_in, grad_ref))
        )
    ]
    for load in loads:
        load.start()
    choices, tok_count = routes_ref.shape
    block = 2 * capacity
    out_rows = out_ref.shape[0]
    experts = out_rows // block

    row = lax.broadcasted_iota(jnp.int32, (out_rows, experts), 0)
    start = lax.broadcasted_iota(jnp.int32, (out_rows, experts), 1) * block
    owns = (row >= start) & (row < start + block)
    spread = jnp.where(owns, 1.0, 0.0).astype(BF16)
    place = jnp.sum(jnp.where(owns, row - start, 0).astype(F32), axis=1, keepdims=True)
    is_tok = place < capacity
    tok_place = jnp.where(is_tok, place, -2.0)
    grad_place = jnp.where(is_tok, -2.0, place - capacity)
    square = (tok_count, tok_count)
    earlier = lax.broadcasted_iota(jnp.int32, square, 0) < lax.broadcasted_iota(jnp.int32, square, 1)
    earlier = jnp.where(earlier, 1.0, 0.0).astype(BF16)
    expert_ids = lax.broadcasted_iota(jnp.int32, (experts, tok_count), 0)

    for load in loads:
        load.wait()
    member = jnp.zeros((experts, tok_count), F32)
    weight = jnp.zeros((experts, tok_count), F32)
    for k in range(choices):
        hit = routes_ref[k : k + 1, :] == expert_ids
        member = member + jnp.where(hit, 1.0, 0.0)
        weight = weight + jnp.where(hit, weights_ref[k : k + 1, :], 0.0)
    rank = dot(member.astype(BF16), earlier, 1, 0)
    rank = jnp.where(member > 0.0, rank, -1.0).astype(BF16)
    weight_hi = weight.astype(BF16)
    weight_lo = (weight - weight_hi.astype(F32)).astype(BF16)
    rank_of = dot(spread, rank, 1, 0)
    tok_pick = jnp.where(rank_of == tok_place, 1.0, 0.0).astype(BF16)
    grad_here = rank_of == grad_place
    hi = jnp.where(grad_here, dot(spread, weight_hi, 1, 0), 0.0).astype(BF16)
    lo = jnp.where(grad_here, dot(spread, weight_lo, 1, 0), 0.0).astype(BF16)
    out = dot(tok_pick, tok_ref[...], 1, 0)
    out = out + dot(hi, grad_ref[...], 1, 0) + dot(lo, grad_ref[...], 1, 0)
    out_ref[...] = out.astype(BF16)


def call(kernel, name, out_shapes, operands, scalars=0, in_hbm=False, scratch=(), dtype=BF16):
    smem = pl.BlockSpec(memory_space=pltpu.SMEM)
    rest = pl.BlockSpec(memory_space=pltpu.HBM) if in_hbm else pl.BlockSpec(memory_space=pltpu.VMEM)
    outs = [jax.ShapeDtypeStruct(shape, dtype) for shape in out_shapes]
    flops = 2 * 384 * 768 * 768
    moved = sum(v.size * 2 for v in list(operands) + outs)
    return pl.pallas_call(
        kernel,
        out_shape=outs,
        in_specs=[smem] * scalars + [rest] * (len(operands) - scalars),
        out_specs=[pl.BlockSpec(memory_space=pltpu.VMEM)] * len(outs),
        scratch_shapes=list(scratch),
        compiler_params=pltpu.CompilerParams(vmem_limit_bytes=ALL_VMEM if in_hbm else VMEM_BYTES),
        cost_estimate=pl.CostEstimate(flops=flops, bytes_accessed=moved, transcendentals=0),
        name=name,
    )(*operands)


def pick_rows(routes, weights, tokens, out_grad, experts, capacity):
    operands = (routes.T, weights.T, tokens, out_grad)
    out = call(
        functools.partial(pick_kernel, capacity),
        "pick_rows",
        [(2 * capacity * experts, tokens.shape[1])],
        operands,
        in_hbm=True,
        scratch=[pltpu.VMEM(v.shape, v.dtype) for v in operands] + [pltpu.SemaphoreType.DMA((4,))],
    )[0]
    return out.reshape(experts, 2 * capacity, tokens.shape[1])


def copies_kernel(in_ref, out_ref, sems):
    stores = [pltpu.make_async_copy(in_ref, out_ref.at[k], sems.at[k]) for k in range(out_ref.shape[0])]
    for store in stores:
        store.start()
    for store in stores:
        store.wait()


def copies(x, count):
    return pl.pallas_call(
        copies_kernel,
        out_shape=jax.ShapeDtypeStruct((count,) + x.shape, x.dtype),
        in_specs=[pl.BlockSpec(memory_space=pltpu.VMEM)],
        out_specs=pl.BlockSpec(memory_space=pl.ANY),
        scratch_shapes=[pltpu.SemaphoreType.DMA((count,))],
        compiler_params=pltpu.CompilerParams(vmem_limit_bytes=VMEM_BYTES),
        name="copies",
    )(x)


def side(which, size):
    return pl.ds(pl.multiple_of(which * size, size), size)


def away_kernel(capacity, core_ref, gate_ref, up_ref, down_ref, recv_ref, out_ref, rows_ref):
    rows = rows_ref.shape[0] // 2
    size = GROUP * capacity
    row = lax.broadcasted_iota(jnp.int32, (size, GROUP), 0)
    start = lax.broadcasted_iota(jnp.int32, (size, GROUP), 1) * capacity
    inside = (row >= start) & (row < start + capacity)
    source = jnp.sum(jnp.where(inside, row + start, 0).astype(F32), axis=1, keepdims=True)
    column = lax.broadcasted_iota(jnp.int32, (size, 2 * size), 1).astype(F32)
    for k, place in enumerate((source, source + capacity)):
        pick = jnp.where(column == place, 1.0, 0.0).astype(BF16)
        for g in range(rows // size):
            block = recv_ref[2 * g * size : 2 * (g + 1) * size, :]
            rows_ref[k * rows + g * size : k * rows + (g + 1) * size, :] = dot(pick, block, 1, 0).astype(BF16)
    units = out_ref.shape[0]
    cut = side(1 - core_ref[0], units)
    out_ref[:, :rows] = dot(gate_ref[cut, :], rows_ref[:rows, :], 1, 1).astype(BF16)
    out_ref[:, rows : 2 * rows] = dot(up_ref[cut, :], rows_ref[:rows, :], 1, 1).astype(BF16)
    out_ref[:, 2 * rows :] = dot(down_ref[cut, :], rows_ref[rows:, :], 1, 1).astype(BF16)


def keep_kernel(core_ref, gate_ref, up_ref, down_ref, rows_ref, add_ref, out_ref):
    units, rows = out_ref.shape[0], rows_ref.shape[0] // 2
    cut = side(core_ref[0], units)

    def put(k, part):
        lanes = slice(k * rows, (k + 1) * rows)
        out_ref[:, lanes] = (part + add_ref[:, lanes].astype(F32)).astype(BF16)

    put(0, dot(gate_ref[cut, :], rows_ref[:rows, :], 1, 1))
    put(1, dot(up_ref[cut, :], rows_ref[:rows, :], 1, 1))
    put(2, dot(down_ref[cut, :], rows_ref[rows:, :], 1, 1))


def half_back(units_ref, weight_ref, cut, rows):
    width = weight_ref.shape[0] // 2
    part = dot(weight_ref[:width, cut], units_ref[:, :rows], 1, 0)
    return part + dot(weight_ref[width:, cut], units_ref[:, rows : 2 * rows], 1, 0)


def mine_back_kernel(core_ref, mine_ref, weight_ref, out_ref):
    units, rows = mine_ref.shape[0], out_ref.shape[1]
    out_ref[...] = half_back(mine_ref, weight_ref, side(core_ref[0], units), rows)


def back_kernel(capacity, core_ref, theirs_ref, weight_ref, total_ref, out_ref):
    units, rows = theirs_ref.shape[0], total_ref.shape[1]
    out_rows = out_ref.shape[0]
    total = total_ref[...] + half_back(theirs_ref, weight_ref, side(1 - core_ref[0], units), rows)
    groups = rows // capacity
    padded = out_rows // groups
    row = lax.broadcasted_iota(jnp.int32, (out_rows, groups), 0)
    group = lax.broadcasted_iota(jnp.int32, (out_rows, groups), 1)
    inside = (row >= group * padded) & (row < group * padded + capacity)
    source = jnp.where(inside, row - group * (padded - capacity) + 1, 0).astype(F32)
    source = jnp.sum(source, axis=1, keepdims=True) - 1.0
    column = lax.broadcasted_iota(jnp.int32, (out_rows, rows), 1).astype(F32)
    place = jnp.where(column == source, 1.0, 0.0).astype(BF16)
    out_ref[...] = dot(place, total.astype(BF16), 1, 1).astype(BF16)


def soft_rotate(block, rotation):
    rotated = dot(block, rotation, 1, 0)
    meansq = jnp.sum(rotated * rotated, axis=1, keepdims=True) * (1.0 / HBLOCK) + EPS
    steps = rotated * (QSTEP * lax.rsqrt(meansq))
    near = steps - jnp.round(steps)
    square = near * near
    series = square * SINE[-1] + SINE[-2]
    for term in SINE[-3::-1]:
        series = series * square + term
    return ((steps - near * series) * (jnp.sqrt(meansq) / QSTEP)).astype(BF16)


def grads_kernel(
    core_ref, mine_ref, theirs_ref, rows_ref, rotation_ref, gate_ref, up_ref, down_ref, in_q, grad_q, gate_q, up_q, hid_q
):
    units, rows = mine_ref.shape[0], mine_ref.shape[1] // 3
    width = in_q.shape[0]
    rotation = rotation_ref[...]
    core = core_ref[0]
    scale = 1.0 / HBLOCK
    for b in range(rows // HBLOCK):
        cut = slice(b * HBLOCK, (b + 1) * HBLOCK)
        in_q[:, cut] = soft_rotate(rows_ref[:width, cut], rotation)
        grad_q[:, cut] = soft_rotate(rows_ref[width:, cut], rotation)
    for ref, which in ((mine_ref, core), (theirs_ref, 1 - core)):
        place = side(which, units)
        for k, dst in enumerate((gate_q, up_q, hid_q)):
            for b in range(rows // HBLOCK):
                cut = slice(b * HBLOCK, (b + 1) * HBLOCK)
                lanes = slice(k * rows + b * HBLOCK, k * rows + (b + 1) * HBLOCK)
                dst[:, cut] = soft_rotate(ref[:, lanes], rotation)
        gate_ref[:, place] = (dot(in_q[...], gate_q[...], 1, 1) * scale).astype(BF16)
        up_ref[:, place] = (dot(in_q[...], up_q[...], 1, 1) * scale).astype(BF16)
        down_ref[place, :] = (dot(hid_q[...], grad_q[...], 1, 1) * scale).astype(BF16)


def slot_picker(routes, expert_count, capacity):
    experts_iota = jnp.arange(expert_count, dtype=jnp.int32)
    member = jnp.sum((routes[:, :, None] == experts_iota[None, None, :]).astype(jnp.int32), axis=1)
    rank_table = jnp.cumsum(member, axis=0) - member
    cap_iota = jnp.arange(capacity, dtype=jnp.int32)
    placed = (rank_table[:, :, None] == cap_iota[None, None, :]) & (member[:, :, None] == 1)
    return jnp.transpose(placed.astype(BF16), (1, 2, 0))


def pair_permute(x, axis):
    return lax.ppermute(x, axis, [(0, 1), (1, 0)])


def by_pair(which, alone, paired, *operands):
    branches = [alone] + [functools.partial(paired, axis) for axis in BITS[::-1]]
    return lax.switch(which, branches, *operands)


def swap(which, x):
    def paired(axis, v):
        return jax.tree.map(lambda leaf: pair_permute(leaf, axis), v)

    return by_pair(which, lambda v: v, paired, x)


def shards(
    tokens, out_grad, routes, route_weights, gate_weight, up_weight, down_weight, sign_bits, partner
):
    experts = lax.axis_size(BITS)
    n_y = lax.axis_size("y")
    core = lax.axis_index("core")
    me = lax.axis_index(BITS)
    mate = partner[me]
    apart = me ^ mate
    which = sum((apart == 1 << k).astype(jnp.int32) * (k + 1) for k in range(len(BITS)))
    tok_count, width = tokens.shape
    capacity = min(tok_count, tok_count * routes.shape[1] * 3 // (2 * experts))
    rows = experts * capacity
    ff = gate_weight.shape[2]
    half = ff // 2
    core_arg = core.astype(jnp.int32)[None]

    gate_w, up_w, down_w = gate_weight[0], up_weight[0], down_weight[0]
    send = pick_rows(routes, route_weights, tokens, out_grad, experts, capacity)
    recv = lax.all_to_all(send, BITS, 0, 0, tiled=True)
    gate_t, up_t = gate_w.T, up_w.T
    cut_1, cut_2 = width // 4, width * 5 // 8
    weight_2 = gate_w[cut_1:cut_2]
    weight_3 = jnp.concatenate([gate_w[cut_2:], up_w], 0)
    weight_1 = swap(which, gate_w[:cut_1])
    recv, weight_1, weight_2, weight_3, gate_t, up_t = lax.optimization_barrier(
        (recv, weight_1, weight_2, weight_3, gate_t, up_t)
    )
    recv = recv.reshape(2 * rows, width)

    feeds = (core_arg, gate_t, up_t, down_w)
    wide = (half, 3 * rows)
    away, routed = call(
        functools.partial(away_kernel, capacity), "away_partials", [wide, recv.shape], feeds + (recv,), 1
    )
    arrived = pair_permute(away, "core")
    chip_sum = call(keep_kernel, "keep_partials", [wide], feeds + (routed, arrived), 1)[0]

    chip_sum, routed, weight_2 = lax.optimization_barrier((chip_sum, routed, weight_2))

    piece = (half // n_y, 3 * rows)
    blocks = lax.all_to_all(chip_sum.reshape((n_y,) + piece), "y", 0, 0, tiled=True)
    mate_routed, weight_2 = swap(which, (routed, weight_2))
    padded = -(-capacity // 16) * 16
    blocks, mate_routed, weight_2 = lax.optimization_barrier((blocks, mate_routed, weight_2))
    sums = jnp.sum(blocks.astype(F32), axis=0)
    gate_sum, up_sum, hid_grad = sums[:, :rows], sums[:, rows : 2 * rows], sums[:, 2 * rows :]
    sig = jax.nn.sigmoid(gate_sum)
    silu = gate_sum * sig
    gate_rows = hid_grad * up_sum * sig * (1.0 + gate_sum * (1.0 - sig))
    acts = jnp.concatenate([gate_rows, hid_grad * silu, silu * up_sum], 1).astype(BF16)

    acts, weight_3 = lax.optimization_barrier((swap(which, acts), weight_3))
    mine = lax.all_to_all(copies(acts, n_y), "y", 0, 0, tiled=True).reshape(wide)
    weight_3 = swap(which, weight_3)
    mate_rows = jnp.concatenate([mate_routed[:rows].T, mate_routed[rows:].T], 0)
    weights = jnp.concatenate([weight_1, weight_2, weight_3], 0)
    mine, weights, mate_rows = lax.optimization_barrier((mine, weights, mate_rows))
    theirs = pair_permute(mine, "core")

    mine_back = call(
        mine_back_kernel, "mine_back", [(width, rows)], (core_arg, mine, weights), 1, dtype=F32
    )[0]
    slot_back = call(
        functools.partial(back_kernel, capacity),
        "slot_back",
        [(experts * padded, width)],
        (core_arg, theirs, weights, mine_back),
        1,
    )[0]
    slot_back, routes, sign_bits = lax.optimization_barrier((slot_back, routes, sign_bits))
    returned = lax.all_to_all(slot_back.reshape(experts, padded, width), BITS, 0, 0, tiled=True)
    picker = jnp.take(slot_picker(routes, experts, capacity), partner, axis=0)
    picker = jnp.pad(picker, ((0, 0), (0, padded - capacity), (0, 0))).reshape(experts * padded, tok_count)
    flip_signs = (1 - 2 * lax.dynamic_index_in_dim(sign_bits, mate, 0, keepdims=False)).astype(BF16)
    rotation = sylvester(HBLOCK) * flip_signs[:, None]
    input_grad = dot(picker, returned.reshape(experts * padded, width), 0, 0).astype(BF16)

    gate_new, up_new, down_new = call(
        grads_kernel,
        "weight_grads",
        [(width, ff), (width, ff), (ff, width)],
        (core_arg, mine, theirs, mate_rows, rotation),
        1,
        scratch=[pltpu.VMEM((n, rows), BF16) for n in (width, width, half, half, half)],
    )
    return gate_new[None], up_new[None], down_new[None], input_grad


def solution(mesh):
    n_dp = mesh.shape["dp"]
    split = Mesh(mesh.devices.reshape((n_dp // 2, 2) + (2,) * len(BITS)), ("y", "core") + BITS)
    dp = ("y", "core")
    return jax.shard_map(
        shards,
        mesh=split,
        in_specs=(
            P(BITS, dp),
            P(BITS, dp),
            P(BITS, None),
            P(BITS, None),
            P(BITS, dp, None),
            P(BITS, dp, None),
            P(BITS, None, dp),
            P(),
            P(),
        ),
        out_specs=(
            P(BITS, dp, None),
            P(BITS, dp, None),
            P(BITS, None, dp),
            P(BITS, dp),
        ),
        check_vma=False,
    )
```

```python
import functools

import jax
import jax.numpy as jnp
from jax import lax
from jax.experimental import pallas as pl
from jax.experimental.pallas import tpu as pltpu
from jax.sharding import Mesh
from jax.sharding import PartitionSpec as P

HBLOCK = 128
EPS = 1e-06
QSTEP = 2.0
SINE = (
    0.9999995827674866,
    -6.579691410064697,
    12.986429214477539,
    -12.18803596496582,
    6.557779312133789,
    -1.952649712562561,
)
BF16 = jnp.bfloat16
F32 = jnp.float32
BITS = ("b4", "b3", "b2", "b1", "b0")
GROUP = 8
VMEM_BYTES = 16 * 2**20
ALL_VMEM = 60 * 2**20


def dot(left, right, left_dim, right_dim):
    return lax.dot_general(
        left, right, (((left_dim,), (right_dim,)), ((), ())), preferred_element_type=F32
    )


def sylvester(block_len):
    positions = jnp.arange(block_len, dtype=jnp.int32)
    common_bits = positions[:, None] & positions[None, :]
    parity = jnp.zeros((block_len, block_len), jnp.int32)
    for bit_pos in range(block_len.bit_length() - 1):
        parity = parity ^ common_bits >> bit_pos & 1
    return (1 - 2 * parity).astype(BF16)


def pick_kernel(
    capacity, routes_in, weights_in, tok_in, grad_in, out_ref, routes_ref, weights_ref, both_ref, sems
):
    choices, tok_count = routes_ref.shape
    loads = [
        pltpu.make_async_copy(src, dst, sems.at[k])
        for k, (src, dst) in enumerate(
            (
                (routes_in, routes_ref),
                (weights_in, weights_ref),
                (tok_in, both_ref.at[:tok_count]),
                (grad_in, both_ref.at[tok_count : 2 * tok_count]),
                (grad_in, both_ref.at[2 * tok_count :]),
            )
        )
    ]
    for load in loads:
        load.start()
    block = 2 * capacity
    out_rows = out_ref.shape[0]
    experts = out_rows // block

    row = lax.broadcasted_iota(jnp.int32, (out_rows, experts), 0)
    start = lax.broadcasted_iota(jnp.int32, (out_rows, experts), 1) * block
    owns = (row >= start) & (row < start + block)
    spread = jnp.where(owns, 1.0, 0.0).astype(BF16)
    place = jnp.sum(jnp.where(owns, row - start, 0).astype(F32), axis=1, keepdims=True)
    is_tok = place < capacity
    tok_place = jnp.where(is_tok, place, -2.0)
    grad_place = jnp.where(is_tok, -2.0, place - capacity)
    lane = lax.broadcasted_iota(jnp.int32, (out_rows, 3 * tok_count), 1)
    place = jnp.where(lane < tok_count, tok_place, grad_place)
    square = (tok_count, tok_count)
    earlier = lax.broadcasted_iota(jnp.int32, square, 0) < lax.broadcasted_iota(jnp.int32, square, 1)
    earlier = jnp.where(earlier, 1.0, 0.0).astype(BF16)
    expert_ids = lax.broadcasted_iota(jnp.int32, (experts, tok_count), 0)

    for load in loads:
        load.wait()
    member = jnp.zeros((experts, tok_count), F32)
    weight = jnp.zeros((experts, tok_count), F32)
    for k in range(choices):
        hit = routes_ref[k : k + 1, :] == expert_ids
        member = member + jnp.where(hit, 1.0, 0.0)
        weight = weight + jnp.where(hit, weights_ref[k : k + 1, :], 0.0)
    rank = dot(member.astype(BF16), earlier, 1, 0)
    rank = jnp.where(member > 0.0, rank, -1.0)
    weight_hi = weight.astype(BF16).astype(F32)
    rank = jnp.concatenate([rank, rank, rank], 1).astype(BF16)
    value = jnp.concatenate([jnp.ones_like(weight), weight_hi, weight - weight_hi], 1).astype(BF16)
    here = dot(spread, rank, 1, 0) == place
    pick = jnp.where(here, dot(spread, value, 1, 0), 0.0).astype(BF16)
    out_ref[...] = dot(pick, both_ref[...], 1, 0).astype(BF16)


def call(kernel, name, out_shapes, operands, scalars=0, in_hbm=False, scratch=(), dtype=BF16):
    smem = pl.BlockSpec(memory_space=pltpu.SMEM)
    rest = pl.BlockSpec(memory_space=pltpu.HBM) if in_hbm else pl.BlockSpec(memory_space=pltpu.VMEM)
    outs = [jax.ShapeDtypeStruct(shape, dtype) for shape in out_shapes]
    flops = 2 * 384 * 768 * 768
    moved = sum(v.size * 2 for v in list(operands) + outs)
    return pl.pallas_call(
        kernel,
        out_shape=outs,
        in_specs=[smem] * scalars + [rest] * (len(operands) - scalars),
        out_specs=[pl.BlockSpec(memory_space=pltpu.VMEM)] * len(outs),
        scratch_shapes=list(scratch),
        compiler_params=pltpu.CompilerParams(vmem_limit_bytes=ALL_VMEM if in_hbm else VMEM_BYTES),
        cost_estimate=pl.CostEstimate(flops=flops, bytes_accessed=moved, transcendentals=0),
        name=name,
    )(*operands)


def pick_rows(routes, weights, tokens, out_grad, experts, capacity):
    operands = (routes.T, weights.T, tokens, out_grad)
    out = call(
        functools.partial(pick_kernel, capacity),
        "pick_rows",
        [(2 * capacity * experts, tokens.shape[1])],
        operands,
        in_hbm=True,
        scratch=[
            pltpu.VMEM(routes.T.shape, routes.dtype),
            pltpu.VMEM(weights.T.shape, weights.dtype),
            pltpu.VMEM((3 * tokens.shape[0], tokens.shape[1]), BF16),
            pltpu.SemaphoreType.DMA((5,)),
        ],
    )[0]
    return out.reshape(experts, 2 * capacity, tokens.shape[1])


def copies_kernel(in_ref, out_ref, sems):
    stores = [pltpu.make_async_copy(in_ref, out_ref.at[k], sems.at[k]) for k in range(out_ref.shape[0])]
    for store in stores:
        store.start()
    for store in stores:
        store.wait()


def copies(x, count):
    return pl.pallas_call(
        copies_kernel,
        out_shape=jax.ShapeDtypeStruct((count,) + x.shape, x.dtype),
        in_specs=[pl.BlockSpec(memory_space=pltpu.VMEM)],
        out_specs=pl.BlockSpec(memory_space=pl.ANY),
        scratch_shapes=[pltpu.SemaphoreType.DMA((count,))],
        compiler_params=pltpu.CompilerParams(vmem_limit_bytes=VMEM_BYTES),
        name="copies",
    )(x)


def side(which, size):
    return pl.ds(pl.multiple_of(which * size, size), size)


def away_kernel(capacity, core_ref, gate_ref, up_ref, down_ref, recv_ref, out_ref, rows_ref):
    rows = rows_ref.shape[0] // 2
    size = GROUP * capacity
    row = lax.broadcasted_iota(jnp.int32, (size, GROUP), 0)
    start = lax.broadcasted_iota(jnp.int32, (size, GROUP), 1) * capacity
    inside = (row >= start) & (row < start + capacity)
    source = jnp.sum(jnp.where(inside, row + start, 0).astype(F32), axis=1, keepdims=True)
    column = lax.broadcasted_iota(jnp.int32, (size, 2 * size), 1).astype(F32)
    for k, place in enumerate((source, source + capacity)):
        pick = jnp.where(column == place, 1.0, 0.0).astype(BF16)
        for g in range(rows // size):
            block = recv_ref[2 * g * size : 2 * (g + 1) * size, :]
            rows_ref[k * rows + g * size : k * rows + (g + 1) * size, :] = dot(pick, block, 1, 0).astype(BF16)
    units = out_ref.shape[0]
    cut = side(1 - core_ref[0], units)
    out_ref[:, :rows] = dot(gate_ref[cut, :], rows_ref[:rows, :], 1, 1).astype(BF16)
    out_ref[:, rows : 2 * rows] = dot(up_ref[cut, :], rows_ref[:rows, :], 1, 1).astype(BF16)
    out_ref[:, 2 * rows :] = dot(down_ref[cut, :], rows_ref[rows:, :], 1, 1).astype(BF16)


def keep_kernel(core_ref, gate_ref, up_ref, down_ref, rows_ref, add_ref, out_ref):
    units, rows = out_ref.shape[0], rows_ref.shape[0] // 2
    cut = side(core_ref[0], units)

    def put(k, part):
        lanes = slice(k * rows, (k + 1) * rows)
        out_ref[:, lanes] = (part + add_ref[:, lanes].astype(F32)).astype(BF16)

    put(0, dot(gate_ref[cut, :], rows_ref[:rows, :], 1, 1))
    put(1, dot(up_ref[cut, :], rows_ref[:rows, :], 1, 1))
    put(2, dot(down_ref[cut, :], rows_ref[rows:, :], 1, 1))


def half_back(units_ref, weight_ref, cut, rows):
    width = weight_ref.shape[0] // 2
    part = dot(weight_ref[:width, cut], units_ref[:, :rows], 1, 0)
    return part + dot(weight_ref[width:, cut], units_ref[:, rows : 2 * rows], 1, 0)


def mine_back_kernel(capacity, core_ref, mine_ref, weight_ref, out_ref, place_ref):
    units, rows = mine_ref.shape[0], out_ref.shape[1]
    out_ref[...] = half_back(mine_ref, weight_ref, side(core_ref[0], units), rows)
    out_rows = place_ref.shape[0]
    groups = rows // capacity
    padded = out_rows // groups
    row = lax.broadcasted_iota(jnp.int32, (out_rows, groups), 0)
    group = lax.broadcasted_iota(jnp.int32, (out_rows, groups), 1)
    inside = (row >= group * padded) & (row < group * padded + capacity)
    source = jnp.where(inside, row - group * (padded - capacity) + 1, 0).astype(F32)
    source = jnp.sum(source, axis=1, keepdims=True) - 1.0
    column = lax.broadcasted_iota(jnp.int32, (out_rows, rows), 1).astype(F32)
    place_ref[...] = jnp.where(column == source, 1.0, 0.0)


def back_kernel(core_ref, theirs_ref, weight_ref, total_ref, place_ref, out_ref):
    units, rows = theirs_ref.shape[0], total_ref.shape[1]
    total = total_ref[...] + half_back(theirs_ref, weight_ref, side(1 - core_ref[0], units), rows)
    out_ref[...] = dot(place_ref[...].astype(BF16), total.astype(BF16), 1, 1).astype(BF16)


def soft_rotate(block, rotation):
    rotated = dot(block, rotation, 1, 0)
    meansq = jnp.sum(rotated * rotated, axis=1, keepdims=True) * (1.0 / HBLOCK) + EPS
    steps = rotated * (QSTEP * lax.rsqrt(meansq))
    near = steps - jnp.round(steps)
    square = near * near
    series = square * SINE[-1] + SINE[-2]
    for term in SINE[-3::-1]:
        series = series * square + term
    return ((steps - near * series) * (jnp.sqrt(meansq) / QSTEP)).astype(BF16)


def grads_kernel(
    core_ref, mine_ref, theirs_ref, rows_ref, rotation_ref, gate_ref, up_ref, down_ref, in_q, grad_q, gate_q, up_q, hid_q
):
    units, rows = mine_ref.shape[0], mine_ref.shape[1] // 3
    width = in_q.shape[0]
    rotation = rotation_ref[...]
    core = core_ref[0]
    scale = 1.0 / HBLOCK
    for b in range(rows // HBLOCK):
        cut = slice(b * HBLOCK, (b + 1) * HBLOCK)
        in_q[:, cut] = soft_rotate(rows_ref[:width, cut], rotation)
        grad_q[:, cut] = soft_rotate(rows_ref[width:, cut], rotation)
    for ref, which in ((mine_ref, core), (theirs_ref, 1 - core)):
        place = side(which, units)
        for k, dst in enumerate((gate_q, up_q, hid_q)):
            for b in range(rows // HBLOCK):
                cut = slice(b * HBLOCK, (b + 1) * HBLOCK)
                lanes = slice(k * rows + b * HBLOCK, k * rows + (b + 1) * HBLOCK)
                dst[:, cut] = soft_rotate(ref[:, lanes], rotation)
        gate_ref[:, place] = (dot(in_q[...], gate_q[...], 1, 1) * scale).astype(BF16)
        up_ref[:, place] = (dot(in_q[...], up_q[...], 1, 1) * scale).astype(BF16)
        down_ref[place, :] = (dot(hid_q[...], grad_q[...], 1, 1) * scale).astype(BF16)


def slot_picker(routes, expert_count, capacity):
    experts_iota = jnp.arange(expert_count, dtype=jnp.int32)
    member = jnp.sum((routes[:, :, None] == experts_iota[None, None, :]).astype(jnp.int32), axis=1)
    rank_table = jnp.cumsum(member, axis=0) - member
    cap_iota = jnp.arange(capacity, dtype=jnp.int32)
    placed = (rank_table[:, :, None] == cap_iota[None, None, :]) & (member[:, :, None] == 1)
    return jnp.transpose(placed.astype(BF16), (1, 2, 0))


def pair_permute(x, axis):
    return lax.ppermute(x, axis, [(0, 1), (1, 0)])


def by_pair(which, alone, paired, *operands):
    branches = [alone] + [functools.partial(paired, axis) for axis in BITS[::-1]]
    return lax.switch(which, branches, *operands)


def swap(which, x):
    def paired(axis, v):
        return jax.tree.map(lambda leaf: pair_permute(leaf, axis), v)

    return by_pair(which, lambda v: v, paired, x)


def shards(
    tokens, out_grad, routes, route_weights, gate_weight, up_weight, down_weight, sign_bits, partner
):
    experts = lax.axis_size(BITS)
    n_y = lax.axis_size("y")
    core = lax.axis_index("core")
    me = lax.axis_index(BITS)
    mate = partner[me]
    apart = me ^ mate
    which = sum((apart == 1 << k).astype(jnp.int32) * (k + 1) for k in range(len(BITS)))
    tok_count, width = tokens.shape
    capacity = min(tok_count, tok_count * routes.shape[1] * 3 // (2 * experts))
    rows = experts * capacity
    ff = gate_weight.shape[2]
    half = ff // 2
    core_arg = core.astype(jnp.int32)[None]

    gate_w, up_w, down_w = gate_weight[0], up_weight[0], down_weight[0]
    send = pick_rows(routes, route_weights, tokens, out_grad, experts, capacity)
    recv = lax.all_to_all(send, BITS, 0, 0, tiled=True)
    gate_t, up_t = gate_w.T, up_w.T
    cut_1, cut_2 = width // 4, width * 5 // 8
    weight_2 = gate_w[cut_1:cut_2]
    weight_3 = jnp.concatenate([gate_w[cut_2:], up_w], 0)
    weight_1 = swap(which, gate_w[:cut_1])
    recv, weight_1, weight_2, weight_3, gate_t, up_t = lax.optimization_barrier(
        (recv, weight_1, weight_2, weight_3, gate_t, up_t)
    )
    recv = recv.reshape(2 * rows, width)

    feeds = (core_arg, gate_t, up_t, down_w)
    wide = (half, 3 * rows)
    away, routed = call(
        functools.partial(away_kernel, capacity), "away_partials", [wide, recv.shape], feeds + (recv,), 1
    )
    arrived = pair_permute(away, "core")
    chip_sum = call(keep_kernel, "keep_partials", [wide], feeds + (routed, arrived), 1)[0]

    chip_sum, routed, weight_2 = lax.optimization_barrier((chip_sum, routed, weight_2))

    piece = (half // n_y, 3 * rows)
    blocks = lax.all_to_all(chip_sum.reshape((n_y,) + piece), "y", 0, 0, tiled=True)
    mate_routed, weight_2 = swap(which, (routed, weight_2))
    padded = -(-capacity // 16) * 16
    blocks, mate_routed, weight_2 = lax.optimization_barrier((blocks, mate_routed, weight_2))
    sums = jnp.sum(blocks.astype(F32), axis=0)
    gate_sum, up_sum, hid_grad = sums[:, :rows], sums[:, rows : 2 * rows], sums[:, 2 * rows :]
    sig = jax.nn.sigmoid(gate_sum)
    silu = gate_sum * sig
    gate_rows = hid_grad * up_sum * sig * (1.0 + gate_sum * (1.0 - sig))
    acts = jnp.concatenate([gate_rows, hid_grad * silu, silu * up_sum], 1).astype(BF16)

    acts, weight_3 = lax.optimization_barrier((swap(which, acts), weight_3))
    mine = lax.all_to_all(copies(acts, n_y), "y", 0, 0, tiled=True).reshape(wide)
    weight_3 = swap(which, weight_3)
    mate_rows = jnp.concatenate([mate_routed[:rows].T, mate_routed[rows:].T], 0)
    weights = jnp.concatenate([weight_1, weight_2, weight_3], 0)
    mine, weights, mate_rows = lax.optimization_barrier((mine, weights, mate_rows))
    theirs = pair_permute(mine, "core")

    mine_back, place = call(
        functools.partial(mine_back_kernel, capacity),
        "mine_back",
        [(width, rows), (experts * padded, rows)],
        (core_arg, mine, weights),
        1,
        dtype=F32,
    )
    slot_back = call(
        back_kernel,
        "slot_back",
        [(experts * padded, width)],
        (core_arg, theirs, weights, mine_back, place),
        1,
    )[0]
    slot_back, routes, sign_bits = lax.optimization_barrier((slot_back, routes, sign_bits))
    returned = lax.all_to_all(slot_back.reshape(experts, padded, width), BITS, 0, 0, tiled=True)
    picker = jnp.take(slot_picker(routes, experts, capacity), partner, axis=0)
    picker = jnp.pad(picker, ((0, 0), (0, padded - capacity), (0, 0))).reshape(experts * padded, tok_count)
    flip_signs = (1 - 2 * lax.dynamic_index_in_dim(sign_bits, mate, 0, keepdims=False)).astype(BF16)
    rotation = sylvester(HBLOCK) * flip_signs[:, None]
    input_grad = dot(picker, returned.reshape(experts * padded, width), 0, 0).astype(BF16)

    gate_new, up_new, down_new = call(
        grads_kernel,
        "weight_grads",
        [(width, ff), (width, ff), (ff, width)],
        (core_arg, mine, theirs, mate_rows, rotation),
        1,
        scratch=[pltpu.VMEM((n, rows), BF16) for n in (width, width, half, half, half)],
    )
    return gate_new[None], up_new[None], down_new[None], input_grad


def solution(mesh):
    n_dp = mesh.shape["dp"]
    split = Mesh(mesh.devices.reshape((n_dp // 2, 2) + (2,) * len(BITS)), ("y", "core") + BITS)
    dp = ("y", "core")
    return jax.shard_map(
        shards,
        mesh=split,
        in_specs=(
            P(BITS, dp),
            P(BITS, dp),
            P(BITS, None),
            P(BITS, None),
            P(BITS, dp, None),
            P(BITS, dp, None),
            P(BITS, None, dp),
            P(),
            P(),
        ),
        out_specs=(
            P(BITS, dp, None),
            P(BITS, dp, None),
            P(BITS, None, dp),
            P(BITS, dp),
        ),
        check_vma=False,
    )
```

```python
import functools

import jax
import jax.numpy as jnp
from jax import lax
from jax.experimental import pallas as pl
from jax.experimental.pallas import tpu as pltpu
from jax.sharding import Mesh
from jax.sharding import PartitionSpec as P

HBLOCK = 128
EPS = 1e-06
QSTEP = 2.0
SINE = (
    0.9999995827674866,
    -6.579691410064697,
    12.986429214477539,
    -12.18803596496582,
    6.557779312133789,
    -1.952649712562561,
)
BF16 = jnp.bfloat16
F32 = jnp.float32
BITS = ("b4", "b3", "b2", "b1", "b0")
GROUP = 8
VMEM_BYTES = 16 * 2**20
ALL_VMEM = 60 * 2**20


def dot(left, right, left_dim, right_dim):
    return lax.dot_general(
        left, right, (((left_dim,), (right_dim,)), ((), ())), preferred_element_type=F32
    )


def sylvester(block_len):
    positions = jnp.arange(block_len, dtype=jnp.int32)
    common_bits = positions[:, None] & positions[None, :]
    parity = jnp.zeros((block_len, block_len), jnp.int32)
    for bit_pos in range(block_len.bit_length() - 1):
        parity = parity ^ common_bits >> bit_pos & 1
    return (1 - 2 * parity).astype(BF16)


def pick_kernel(
    capacity, routes_in, weights_in, tok_in, grad_in, out_ref, routes_ref, weights_ref, both_ref, sems
):
    choices, tok_count = routes_ref.shape
    loads = [
        pltpu.make_async_copy(src, dst, sems.at[k])
        for k, (src, dst) in enumerate(
            (
                (routes_in, routes_ref),
                (weights_in, weights_ref),
                (tok_in, both_ref.at[:tok_count]),
                (grad_in, both_ref.at[tok_count : 2 * tok_count]),
                (grad_in, both_ref.at[2 * tok_count :]),
            )
        )
    ]
    for load in loads:
        load.start()
    block = 2 * capacity
    out_rows = out_ref.shape[0]
    experts = out_rows // block

    row = lax.broadcasted_iota(jnp.int32, (out_rows, experts), 0)
    start = lax.broadcasted_iota(jnp.int32, (out_rows, experts), 1) * block
    owns = (row >= start) & (row < start + block)
    spread = jnp.where(owns, 1.0, 0.0).astype(BF16)
    place = jnp.sum(jnp.where(owns, row - start, 0).astype(F32), axis=1, keepdims=True)
    is_tok = place < capacity
    tok_place = jnp.where(is_tok, place, -2.0)
    grad_place = jnp.where(is_tok, -2.0, place - capacity)
    lane = lax.broadcasted_iota(jnp.int32, (out_rows, 3 * tok_count), 1)
    place = jnp.where(lane < tok_count, tok_place, grad_place)
    square = (tok_count, tok_count)
    earlier = lax.broadcasted_iota(jnp.int32, square, 0) < lax.broadcasted_iota(jnp.int32, square, 1)
    earlier = jnp.where(earlier, 1.0, 0.0).astype(BF16)
    expert_ids = lax.broadcasted_iota(jnp.int32, (experts, tok_count), 0)

    for load in loads:
        load.wait()
    member = jnp.zeros((experts, tok_count), F32)
    weight = jnp.zeros((experts, tok_count), F32)
    for k in range(choices):
        hit = routes_ref[k : k + 1, :] == expert_ids
        member = member + jnp.where(hit, 1.0, 0.0)
        weight = weight + jnp.where(hit, weights_ref[k : k + 1, :], 0.0)
    rank = dot(member.astype(BF16), earlier, 1, 0)
    rank = jnp.where(member > 0.0, rank, -1.0)
    weight_hi = weight.astype(BF16).astype(F32)
    rank = jnp.concatenate([rank, rank, rank], 1).astype(BF16)
    value = jnp.concatenate([jnp.ones_like(weight), weight_hi, weight - weight_hi], 1).astype(BF16)
    here = dot(spread, rank, 1, 0) == place
    pick = jnp.where(here, dot(spread, value, 1, 0), 0.0).astype(BF16)
    out_ref[...] = dot(pick, both_ref[...], 1, 0).astype(BF16)


def call(kernel, name, out_shapes, operands, scalars=0, in_hbm=False, scratch=(), dtype=BF16):
    smem = pl.BlockSpec(memory_space=pltpu.SMEM)
    rest = pl.BlockSpec(memory_space=pltpu.HBM) if in_hbm else pl.BlockSpec(memory_space=pltpu.VMEM)
    kinds = dtype if isinstance(dtype, tuple) else (dtype,) * len(out_shapes)
    outs = [jax.ShapeDtypeStruct(shape, kind) for shape, kind in zip(out_shapes, kinds)]
    flops = 2 * 384 * 768 * 768
    moved = sum(v.size * 2 for v in list(operands) + outs)
    return pl.pallas_call(
        kernel,
        out_shape=outs,
        in_specs=[smem] * scalars + [rest] * (len(operands) - scalars),
        out_specs=[pl.BlockSpec(memory_space=pltpu.VMEM)] * len(outs),
        scratch_shapes=list(scratch),
        compiler_params=pltpu.CompilerParams(vmem_limit_bytes=ALL_VMEM if in_hbm else VMEM_BYTES),
        cost_estimate=pl.CostEstimate(flops=flops, bytes_accessed=moved, transcendentals=0),
        name=name,
    )(*operands)


def pick_rows(routes, weights, tokens, out_grad, experts, capacity):
    operands = (routes.T, weights.T, tokens, out_grad)
    out = call(
        functools.partial(pick_kernel, capacity),
        "pick_rows",
        [(2 * capacity * experts, tokens.shape[1])],
        operands,
        in_hbm=True,
        scratch=[
            pltpu.VMEM(routes.T.shape, routes.dtype),
            pltpu.VMEM(weights.T.shape, weights.dtype),
            pltpu.VMEM((3 * tokens.shape[0], tokens.shape[1]), BF16),
            pltpu.SemaphoreType.DMA((5,)),
        ],
    )[0]
    return out.reshape(experts, 2 * capacity, tokens.shape[1])


def copies_kernel(in_ref, out_ref, sems):
    stores = [pltpu.make_async_copy(in_ref, out_ref.at[k], sems.at[k]) for k in range(out_ref.shape[0])]
    for store in stores:
        store.start()
    for store in stores:
        store.wait()


def copies(x, count):
    return pl.pallas_call(
        copies_kernel,
        out_shape=jax.ShapeDtypeStruct((count,) + x.shape, x.dtype),
        in_specs=[pl.BlockSpec(memory_space=pltpu.VMEM)],
        out_specs=pl.BlockSpec(memory_space=pl.ANY),
        scratch_shapes=[pltpu.SemaphoreType.DMA((count,))],
        compiler_params=pltpu.CompilerParams(vmem_limit_bytes=VMEM_BYTES),
        name="copies",
    )(x)


def side(which, size):
    return pl.ds(pl.multiple_of(which * size, size), size)


def away_kernel(capacity, core_ref, gate_ref, up_ref, down_ref, recv_ref, out_ref, rows_ref):
    rows = rows_ref.shape[0] // 2
    size = GROUP * capacity
    row = lax.broadcasted_iota(jnp.int32, (size, GROUP), 0)
    start = lax.broadcasted_iota(jnp.int32, (size, GROUP), 1) * capacity
    inside = (row >= start) & (row < start + capacity)
    source = jnp.sum(jnp.where(inside, row + start, 0).astype(F32), axis=1, keepdims=True)
    column = lax.broadcasted_iota(jnp.int32, (size, 2 * size), 1).astype(F32)
    for k, place in enumerate((source, source + capacity)):
        pick = jnp.where(column == place, 1.0, 0.0).astype(BF16)
        for g in range(rows // size):
            block = recv_ref[2 * g * size : 2 * (g + 1) * size, :]
            rows_ref[k * rows + g * size : k * rows + (g + 1) * size, :] = dot(pick, block, 1, 0).astype(BF16)
    units = out_ref.shape[0]
    cut = side(1 - core_ref[0], units)
    out_ref[:, :rows] = dot(gate_ref[cut, :], rows_ref[:rows, :], 1, 1).astype(BF16)
    out_ref[:, rows : 2 * rows] = dot(up_ref[cut, :], rows_ref[:rows, :], 1, 1).astype(BF16)
    out_ref[:, 2 * rows :] = dot(down_ref[cut, :], rows_ref[rows:, :], 1, 1).astype(BF16)


def keep_kernel(core_ref, gate_ref, up_ref, down_ref, rows_ref, add_ref, out_ref):
    units, rows = out_ref.shape[0], rows_ref.shape[0] // 2
    cut = side(core_ref[0], units)

    def put(k, part):
        lanes = slice(k * rows, (k + 1) * rows)
        out_ref[:, lanes] = (part + add_ref[:, lanes].astype(F32)).astype(BF16)

    put(0, dot(gate_ref[cut, :], rows_ref[:rows, :], 1, 1))
    put(1, dot(up_ref[cut, :], rows_ref[:rows, :], 1, 1))
    put(2, dot(down_ref[cut, :], rows_ref[rows:, :], 1, 1))


def half_back(units_ref, weight_ref, cut, rows):
    width = weight_ref.shape[0] // 2
    part = dot(weight_ref[:width, cut], units_ref[:, :rows], 1, 0)
    return part + dot(weight_ref[width:, cut], units_ref[:, rows : 2 * rows], 1, 0)


def mine_back_kernel(capacity, core_ref, mine_ref, weight_ref, out_ref, place_ref):
    units, rows = mine_ref.shape[0], out_ref.shape[1]
    out_ref[...] = half_back(mine_ref, weight_ref, side(core_ref[0], units), rows)
    out_rows = place_ref.shape[0]
    groups = rows // capacity
    padded = out_rows // groups
    row = lax.broadcasted_iota(jnp.int32, (out_rows, groups), 0)
    group = lax.broadcasted_iota(jnp.int32, (out_rows, groups), 1)
    inside = (row >= group * padded) & (row < group * padded + capacity)
    source = jnp.where(inside, row - group * (padded - capacity) + 1, 0).astype(F32)
    source = jnp.sum(source, axis=1, keepdims=True) - 1.0
    column = lax.broadcasted_iota(jnp.int32, (out_rows, rows), 1).astype(F32)
    place_ref[...] = jnp.where(column == source, 1.0, 0.0).astype(BF16)


def back_kernel(core_ref, theirs_ref, weight_ref, total_ref, place_ref, out_ref):
    units, rows = theirs_ref.shape[0], total_ref.shape[1]
    total = total_ref[...] + half_back(theirs_ref, weight_ref, side(1 - core_ref[0], units), rows)
    out_ref[...] = dot(place_ref[...], total.astype(BF16), 1, 1).astype(BF16)


def soft_rotate(block, rotation):
    rotated = dot(block, rotation, 1, 0)
    meansq = jnp.sum(rotated * rotated, axis=1, keepdims=True) * (1.0 / HBLOCK) + EPS
    steps = rotated * (QSTEP * lax.rsqrt(meansq))
    near = steps - jnp.round(steps)
    square = near * near
    series = square * SINE[-1] + SINE[-2]
    for term in SINE[-3::-1]:
        series = series * square + term
    return ((steps - near * series) * (jnp.sqrt(meansq) / QSTEP)).astype(BF16)


def grads_kernel(
    core_ref, mine_ref, theirs_ref, rows_ref, rotation_ref, gate_ref, up_ref, down_ref, in_q, grad_q, gate_q, up_q, hid_q
):
    units, rows = mine_ref.shape[0], mine_ref.shape[1] // 3
    width = in_q.shape[0]
    rotation = rotation_ref[...]
    core = core_ref[0]
    scale = 1.0 / HBLOCK
    for b in range(rows // HBLOCK):
        cut = slice(b * HBLOCK, (b + 1) * HBLOCK)
        in_q[:, cut] = soft_rotate(rows_ref[:width, cut], rotation)
        grad_q[:, cut] = soft_rotate(rows_ref[width:, cut], rotation)
    for ref, which in ((mine_ref, core), (theirs_ref, 1 - core)):
        place = side(which, units)
        for k, dst in enumerate((gate_q, up_q, hid_q)):
            for b in range(rows // HBLOCK):
                cut = slice(b * HBLOCK, (b + 1) * HBLOCK)
                lanes = slice(k * rows + b * HBLOCK, k * rows + (b + 1) * HBLOCK)
                dst[:, cut] = soft_rotate(ref[:, lanes], rotation)
        gate_ref[:, place] = (dot(in_q[...], gate_q[...], 1, 1) * scale).astype(BF16)
        up_ref[:, place] = (dot(in_q[...], up_q[...], 1, 1) * scale).astype(BF16)
        down_ref[place, :] = (dot(hid_q[...], grad_q[...], 1, 1) * scale).astype(BF16)


def slot_picker(routes, expert_count, capacity):
    experts_iota = jnp.arange(expert_count, dtype=jnp.int32)
    member = jnp.sum((routes[:, :, None] == experts_iota[None, None, :]).astype(jnp.int32), axis=1)
    rank_table = jnp.cumsum(member, axis=0) - member
    cap_iota = jnp.arange(capacity, dtype=jnp.int32)
    placed = (rank_table[:, :, None] == cap_iota[None, None, :]) & (member[:, :, None] == 1)
    return jnp.transpose(placed.astype(BF16), (1, 2, 0))


def pair_permute(x, axis):
    return lax.ppermute(x, axis, [(0, 1), (1, 0)])


def by_pair(which, alone, paired, *operands):
    branches = [alone] + [functools.partial(paired, axis) for axis in BITS[::-1]]
    return lax.switch(which, branches, *operands)


def swap(which, x):
    def paired(axis, v):
        return jax.tree.map(lambda leaf: pair_permute(leaf, axis), v)

    return by_pair(which, lambda v: v, paired, x)


def shards(
    tokens, out_grad, routes, route_weights, gate_weight, up_weight, down_weight, sign_bits, partner
):
    experts = lax.axis_size(BITS)
    n_y = lax.axis_size("y")
    core = lax.axis_index("core")
    me = lax.axis_index(BITS)
    mate = partner[me]
    apart = me ^ mate
    which = sum((apart == 1 << k).astype(jnp.int32) * (k + 1) for k in range(len(BITS)))
    tok_count, width = tokens.shape
    capacity = min(tok_count, tok_count * routes.shape[1] * 3 // (2 * experts))
    rows = experts * capacity
    ff = gate_weight.shape[2]
    half = ff // 2
    core_arg = core.astype(jnp.int32)[None]

    gate_w, up_w, down_w = gate_weight[0], up_weight[0], down_weight[0]
    send = pick_rows(routes, route_weights, tokens, out_grad, experts, capacity)
    recv = lax.all_to_all(send, BITS, 0, 0, tiled=True)
    gate_t, up_t = gate_w.T, up_w.T
    cut_1, cut_2 = width // 4, width * 5 // 8
    weight_2 = gate_w[cut_1:cut_2]
    weight_3 = jnp.concatenate([gate_w[cut_2:], up_w], 0)
    weight_1 = swap(which, gate_w[:cut_1])
    recv, weight_1, weight_2, weight_3, gate_t, up_t = lax.optimization_barrier(
        (recv, weight_1, weight_2, weight_3, gate_t, up_t)
    )
    recv = recv.reshape(2 * rows, width)

    feeds = (core_arg, gate_t, up_t, down_w)
    wide = (half, 3 * rows)
    away, routed = call(
        functools.partial(away_kernel, capacity), "away_partials", [wide, recv.shape], feeds + (recv,), 1
    )
    arrived = pair_permute(away, "core")
    chip_sum = call(keep_kernel, "keep_partials", [wide], feeds + (routed, arrived), 1)[0]

    chip_sum, routed, weight_2 = lax.optimization_barrier((chip_sum, routed, weight_2))

    piece = (half // n_y, 3 * rows)
    blocks = lax.all_to_all(chip_sum.reshape((n_y,) + piece), "y", 0, 0, tiled=True)
    mate_routed, weight_2 = swap(which, (routed, weight_2))
    padded = -(-capacity // 16) * 16
    blocks, mate_routed, weight_2 = lax.optimization_barrier((blocks, mate_routed, weight_2))
    sums = jnp.sum(blocks.astype(F32), axis=0)
    gate_sum, up_sum, hid_grad = sums[:, :rows], sums[:, rows : 2 * rows], sums[:, 2 * rows :]
    sig = jax.nn.sigmoid(gate_sum)
    silu = gate_sum * sig
    gate_rows = hid_grad * up_sum * sig * (1.0 + gate_sum * (1.0 - sig))
    acts = jnp.concatenate([gate_rows, hid_grad * silu, silu * up_sum], 1).astype(BF16)

    acts, weight_3 = lax.optimization_barrier((swap(which, acts), weight_3))
    mine = lax.all_to_all(copies(acts, n_y), "y", 0, 0, tiled=True).reshape(wide)
    weight_3 = swap(which, weight_3)
    mate_rows = jnp.concatenate([mate_routed[:rows].T, mate_routed[rows:].T], 0)
    weights = jnp.concatenate([weight_1, weight_2, weight_3], 0)
    mine, weights, mate_rows = lax.optimization_barrier((mine, weights, mate_rows))
    theirs = pair_permute(mine, "core")

    mine_back, place = call(
        functools.partial(mine_back_kernel, capacity),
        "mine_back",
        [(width, rows), (experts * padded, rows)],
        (core_arg, mine, weights),
        1,
        dtype=(F32, BF16),
    )
    slot_back = call(
        back_kernel,
        "slot_back",
        [(experts * padded, width)],
        (core_arg, theirs, weights, mine_back, place),
        1,
    )[0]
    slot_back, routes, sign_bits = lax.optimization_barrier((slot_back, routes, sign_bits))
    returned = lax.all_to_all(slot_back.reshape(experts, padded, width), BITS, 0, 0, tiled=True)
    picker = jnp.take(slot_picker(routes, experts, capacity), partner, axis=0)
    picker = jnp.pad(picker, ((0, 0), (0, padded - capacity), (0, 0))).reshape(experts * padded, tok_count)
    flip_signs = (1 - 2 * lax.dynamic_index_in_dim(sign_bits, mate, 0, keepdims=False)).astype(BF16)
    rotation = sylvester(HBLOCK) * flip_signs[:, None]
    input_grad = dot(picker, returned.reshape(experts * padded, width), 0, 0).astype(BF16)

    gate_new, up_new, down_new = call(
        grads_kernel,
        "weight_grads",
        [(width, ff), (width, ff), (ff, width)],
        (core_arg, mine, theirs, mate_rows, rotation),
        1,
        scratch=[pltpu.VMEM((n, rows), BF16) for n in (width, width, half, half, half)],
    )
    return gate_new[None], up_new[None], down_new[None], input_grad


def solution(mesh):
    n_dp = mesh.shape["dp"]
    split = Mesh(mesh.devices.reshape((n_dp // 2, 2) + (2,) * len(BITS)), ("y", "core") + BITS)
    dp = ("y", "core")
    return jax.shard_map(
        shards,
        mesh=split,
        in_specs=(
            P(BITS, dp),
            P(BITS, dp),
            P(BITS, None),
            P(BITS, None),
            P(BITS, dp, None),
            P(BITS, dp, None),
            P(BITS, None, dp),
            P(),
            P(),
        ),
        out_specs=(
            P(BITS, dp, None),
            P(BITS, dp, None),
            P(BITS, None, dp),
            P(BITS, dp),
        ),
        check_vma=False,
    )
```

```python
import functools

import jax
import jax.numpy as jnp
from jax import lax
from jax.experimental import pallas as pl
from jax.experimental.pallas import tpu as pltpu
from jax.sharding import Mesh
from jax.sharding import PartitionSpec as P

HBLOCK = 128
EPS = 1e-06
QSTEP = 2.0
SINE = (
    0.9999995827674866,
    -6.579691410064697,
    12.986429214477539,
    -12.18803596496582,
    6.557779312133789,
    -1.952649712562561,
)
BF16 = jnp.bfloat16
F32 = jnp.float32
BITS = ("b4", "b3", "b2", "b1", "b0")
GROUP = 8
VMEM_BYTES = 16 * 2**20
ALL_VMEM = 60 * 2**20


def dot(left, right, left_dim, right_dim):
    return lax.dot_general(
        left, right, (((left_dim,), (right_dim,)), ((), ())), preferred_element_type=F32
    )


def sylvester(block_len):
    positions = jnp.arange(block_len, dtype=jnp.int32)
    common_bits = positions[:, None] & positions[None, :]
    parity = jnp.zeros((block_len, block_len), jnp.int32)
    for bit_pos in range(block_len.bit_length() - 1):
        parity = parity ^ common_bits >> bit_pos & 1
    return (1 - 2 * parity).astype(BF16)


def pick_kernel(
    capacity, routes_in, weights_in, tok_in, grad_in, out_ref, routes_ref, weights_ref, both_ref, sems
):
    choices, tok_count = routes_ref.shape
    loads = [
        pltpu.make_async_copy(src, dst, sems.at[k])
        for k, (src, dst) in enumerate(
            (
                (routes_in, routes_ref),
                (weights_in, weights_ref),
                (tok_in, both_ref.at[:tok_count]),
                (grad_in, both_ref.at[tok_count : 2 * tok_count]),
                (grad_in, both_ref.at[2 * tok_count :]),
            )
        )
    ]
    for load in loads:
        load.start()
    block = 2 * capacity
    out_rows = out_ref.shape[0]
    experts = out_rows // block

    row = lax.broadcasted_iota(jnp.int32, (out_rows, experts), 0)
    start = lax.broadcasted_iota(jnp.int32, (out_rows, experts), 1) * block
    owns = (row >= start) & (row < start + block)
    spread = jnp.where(owns, 1.0, 0.0).astype(BF16)
    place = jnp.sum(jnp.where(owns, row - start, 0).astype(F32), axis=1, keepdims=True)
    is_tok = place < capacity
    tok_place = jnp.where(is_tok, place, -2.0)
    grad_place = jnp.where(is_tok, -2.0, place - capacity)
    lane = lax.broadcasted_iota(jnp.int32, (out_rows, 3 * tok_count), 1)
    place = jnp.where(lane < tok_count, tok_place, grad_place)
    square = (tok_count, tok_count)
    earlier = lax.broadcasted_iota(jnp.int32, square, 0) < lax.broadcasted_iota(jnp.int32, square, 1)
    earlier = jnp.where(earlier, 1.0, 0.0).astype(BF16)
    expert_ids = lax.broadcasted_iota(jnp.int32, (experts, tok_count), 0)

    for load in loads:
        load.wait()
    member = jnp.zeros((experts, tok_count), F32)
    weight = jnp.zeros((experts, tok_count), F32)
    for k in range(choices):
        hit = routes_ref[k : k + 1, :] == expert_ids
        member = member + jnp.where(hit, 1.0, 0.0)
        weight = weight + jnp.where(hit, weights_ref[k : k + 1, :], 0.0)
    rank = dot(member.astype(BF16), earlier, 1, 0)
    rank = jnp.where(member > 0.0, rank, -1.0)
    weight_hi = weight.astype(BF16).astype(F32)
    rank = jnp.concatenate([rank, rank, rank], 1).astype(BF16)
    value = jnp.concatenate([jnp.ones_like(weight), weight_hi, weight - weight_hi], 1).astype(BF16)
    here = dot(spread, rank, 1, 0) == place
    pick = jnp.where(here, dot(spread, value, 1, 0), 0.0).astype(BF16)
    out_ref[...] = dot(pick, both_ref[...], 1, 0).astype(BF16)


def call(kernel, name, out_shapes, operands, scalars=0, in_hbm=False, scratch=(), dtype=BF16):
    smem = pl.BlockSpec(memory_space=pltpu.SMEM)
    rest = pl.BlockSpec(memory_space=pltpu.HBM) if in_hbm else pl.BlockSpec(memory_space=pltpu.VMEM)
    kinds = dtype if isinstance(dtype, tuple) else (dtype,) * len(out_shapes)
    outs = [jax.ShapeDtypeStruct(shape, kind) for shape, kind in zip(out_shapes, kinds)]
    flops = 2 * 384 * 768 * 768
    moved = sum(v.size * 2 for v in list(operands) + outs)
    return pl.pallas_call(
        kernel,
        out_shape=outs,
        in_specs=[smem] * scalars + [rest] * (len(operands) - scalars),
        out_specs=[pl.BlockSpec(memory_space=pltpu.VMEM)] * len(outs),
        scratch_shapes=list(scratch),
        compiler_params=pltpu.CompilerParams(vmem_limit_bytes=ALL_VMEM if in_hbm else VMEM_BYTES),
        cost_estimate=pl.CostEstimate(flops=flops, bytes_accessed=moved, transcendentals=0),
        name=name,
    )(*operands)


def pick_rows(routes, weights, tokens, out_grad, experts, capacity):
    operands = (routes.T, weights.T, tokens, out_grad)
    out = call(
        functools.partial(pick_kernel, capacity),
        "pick_rows",
        [(2 * capacity * experts, tokens.shape[1])],
        operands,
        in_hbm=True,
        scratch=[
            pltpu.VMEM(routes.T.shape, routes.dtype),
            pltpu.VMEM(weights.T.shape, weights.dtype),
            pltpu.VMEM((3 * tokens.shape[0], tokens.shape[1]), BF16),
            pltpu.SemaphoreType.DMA((5,)),
        ],
    )[0]
    return out.reshape(experts, 2 * capacity, tokens.shape[1])


def copies_kernel(in_ref, out_ref, sems):
    stores = [pltpu.make_async_copy(in_ref, out_ref.at[k], sems.at[k]) for k in range(out_ref.shape[0])]
    for store in stores:
        store.start()
    for store in stores:
        store.wait()


def copies(x, count):
    return pl.pallas_call(
        copies_kernel,
        out_shape=jax.ShapeDtypeStruct((count,) + x.shape, x.dtype),
        in_specs=[pl.BlockSpec(memory_space=pltpu.VMEM)],
        out_specs=pl.BlockSpec(memory_space=pl.ANY),
        scratch_shapes=[pltpu.SemaphoreType.DMA((count,))],
        compiler_params=pltpu.CompilerParams(vmem_limit_bytes=VMEM_BYTES),
        name="copies",
    )(x)


def side(which, size):
    return pl.ds(pl.multiple_of(which * size, size), size)


def away_kernel(capacity, core_ref, gate_ref, up_ref, down_ref, recv_ref, out_ref, rows_ref):
    rows = rows_ref.shape[0] // 2
    size = GROUP * capacity
    row = lax.broadcasted_iota(jnp.int32, (size, GROUP), 0)
    start = lax.broadcasted_iota(jnp.int32, (size, GROUP), 1) * capacity
    inside = (row >= start) & (row < start + capacity)
    source = jnp.sum(jnp.where(inside, row + start, 0).astype(F32), axis=1, keepdims=True)
    column = lax.broadcasted_iota(jnp.int32, (size, 2 * size), 1).astype(F32)
    for k, place in enumerate((source, source + capacity)):
        pick = jnp.where(column == place, 1.0, 0.0).astype(BF16)
        for g in range(rows // size):
            block = recv_ref[2 * g * size : 2 * (g + 1) * size, :]
            rows_ref[k * rows + g * size : k * rows + (g + 1) * size, :] = dot(pick, block, 1, 0).astype(BF16)
    units = out_ref.shape[0]
    cut = side(1 - core_ref[0], units)
    out_ref[:, :rows] = dot(gate_ref[cut, :], rows_ref[:rows, :], 1, 1).astype(BF16)
    out_ref[:, rows : 2 * rows] = dot(up_ref[cut, :], rows_ref[:rows, :], 1, 1).astype(BF16)
    out_ref[:, 2 * rows :] = dot(down_ref[cut, :], rows_ref[rows:, :], 1, 1).astype(BF16)


def keep_kernel(core_ref, gate_ref, up_ref, down_ref, rows_ref, add_ref, out_ref):
    units, rows = out_ref.shape[0], rows_ref.shape[0] // 2
    cut = side(core_ref[0], units)

    def put(k, part):
        lanes = slice(k * rows, (k + 1) * rows)
        out_ref[:, lanes] = (part + add_ref[:, lanes].astype(F32)).astype(BF16)

    put(0, dot(gate_ref[cut, :], rows_ref[:rows, :], 1, 1))
    put(1, dot(up_ref[cut, :], rows_ref[:rows, :], 1, 1))
    put(2, dot(down_ref[cut, :], rows_ref[rows:, :], 1, 1))


def half_back(units_ref, weight_ref, cut, rows):
    width = weight_ref.shape[0] // 2
    part = dot(weight_ref[:width, cut], units_ref[:, :rows], 1, 0)
    return part + dot(weight_ref[width:, cut], units_ref[:, rows : 2 * rows], 1, 0)


def mine_back_kernel(capacity, core_ref, mine_ref, weight_ref, out_ref, place_ref):
    units, rows = mine_ref.shape[0], out_ref.shape[1]
    out_ref[...] = half_back(mine_ref, weight_ref, side(core_ref[0], units), rows)
    out_rows = place_ref.shape[0]
    groups = rows // capacity
    padded = out_rows // groups
    row = lax.broadcasted_iota(jnp.int32, (out_rows, groups), 0)
    group = lax.broadcasted_iota(jnp.int32, (out_rows, groups), 1)
    inside = (row >= group * padded) & (row < group * padded + capacity)
    source = jnp.where(inside, row - group * (padded - capacity) + 1, 0).astype(F32)
    source = jnp.sum(source, axis=1, keepdims=True) - 1.0
    column = lax.broadcasted_iota(jnp.int32, (out_rows, rows), 1).astype(F32)
    place_ref[...] = jnp.where(column == source, 1.0, 0.0).astype(BF16)


def back_kernel(core_ref, theirs_ref, weight_ref, total_ref, place_ref, out_ref):
    units, rows = theirs_ref.shape[0], total_ref.shape[1]
    total = total_ref[...] + half_back(theirs_ref, weight_ref, side(1 - core_ref[0], units), rows)
    out_ref[...] = dot(place_ref[...], total.astype(BF16), 1, 1).astype(BF16)


def token_kernel(picker_ref, rows_ref, out_ref):
    out_ref[...] = dot(picker_ref[...], rows_ref[...], 1, 0).astype(BF16)


def soft_rotate(block, rotation):
    rotated = dot(block, rotation, 1, 0)
    meansq = jnp.sum(rotated * rotated, axis=1, keepdims=True) * (1.0 / HBLOCK) + EPS
    steps = rotated * (QSTEP * lax.rsqrt(meansq))
    near = steps - jnp.round(steps)
    square = near * near
    series = square * SINE[-1] + SINE[-2]
    for term in SINE[-3::-1]:
        series = series * square + term
    return ((steps - near * series) * (jnp.sqrt(meansq) / QSTEP)).astype(BF16)


def grads_kernel(
    core_ref, mine_ref, theirs_ref, rows_ref, rotation_ref, gate_ref, up_ref, down_ref, in_q, grad_q, gate_q, up_q, hid_q
):
    units, rows = mine_ref.shape[0], mine_ref.shape[1] // 3
    width = in_q.shape[0]
    rotation = rotation_ref[...]
    core = core_ref[0]
    scale = 1.0 / HBLOCK
    for b in range(rows // HBLOCK):
        cut = slice(b * HBLOCK, (b + 1) * HBLOCK)
        in_q[:, cut] = soft_rotate(rows_ref[:width, cut], rotation)
        grad_q[:, cut] = soft_rotate(rows_ref[width:, cut], rotation)
    for ref, which in ((mine_ref, core), (theirs_ref, 1 - core)):
        place = side(which, units)
        for k, dst in enumerate((gate_q, up_q, hid_q)):
            for b in range(rows // HBLOCK):
                cut = slice(b * HBLOCK, (b + 1) * HBLOCK)
                lanes = slice(k * rows + b * HBLOCK, k * rows + (b + 1) * HBLOCK)
                dst[:, cut] = soft_rotate(ref[:, lanes], rotation)
        gate_ref[:, place] = (dot(in_q[...], gate_q[...], 1, 1) * scale).astype(BF16)
        up_ref[:, place] = (dot(in_q[...], up_q[...], 1, 1) * scale).astype(BF16)
        down_ref[place, :] = (dot(hid_q[...], grad_q[...], 1, 1) * scale).astype(BF16)


def slot_picker(routes, expert_count, capacity):
    experts_iota = jnp.arange(expert_count, dtype=jnp.int32)
    member = jnp.sum((routes[:, :, None] == experts_iota[None, None, :]).astype(jnp.int32), axis=1)
    rank_table = jnp.cumsum(member, axis=0) - member
    cap_iota = jnp.arange(capacity, dtype=jnp.int32)
    placed = (rank_table[:, :, None] == cap_iota[None, None, :]) & (member[:, :, None] == 1)
    return jnp.transpose(placed.astype(BF16), (1, 2, 0))


def pair_permute(x, axis):
    return lax.ppermute(x, axis, [(0, 1), (1, 0)])


def by_pair(which, alone, paired, *operands):
    branches = [alone] + [functools.partial(paired, axis) for axis in BITS[::-1]]
    return lax.switch(which, branches, *operands)


def swap(which, x):
    def paired(axis, v):
        return jax.tree.map(lambda leaf: pair_permute(leaf, axis), v)

    return by_pair(which, lambda v: v, paired, x)


def shards(
    tokens, out_grad, routes, route_weights, gate_weight, up_weight, down_weight, sign_bits, partner
):
    experts = lax.axis_size(BITS)
    n_y = lax.axis_size("y")
    core = lax.axis_index("core")
    me = lax.axis_index(BITS)
    mate = partner[me]
    apart = me ^ mate
    which = sum((apart == 1 << k).astype(jnp.int32) * (k + 1) for k in range(len(BITS)))
    tok_count, width = tokens.shape
    capacity = min(tok_count, tok_count * routes.shape[1] * 3 // (2 * experts))
    rows = experts * capacity
    ff = gate_weight.shape[2]
    half = ff // 2
    core_arg = core.astype(jnp.int32)[None]

    gate_w, up_w, down_w = gate_weight[0], up_weight[0], down_weight[0]
    send = pick_rows(routes, route_weights, tokens, out_grad, experts, capacity)
    recv = lax.all_to_all(send, BITS, 0, 0, tiled=True)
    gate_t, up_t = gate_w.T, up_w.T
    cut_1, cut_2 = width // 4, width * 5 // 8
    weight_2 = gate_w[cut_1:cut_2]
    weight_3 = jnp.concatenate([gate_w[cut_2:], up_w], 0)
    weight_1 = swap(which, gate_w[:cut_1])
    recv, weight_1, weight_2, weight_3, gate_t, up_t = lax.optimization_barrier(
        (recv, weight_1, weight_2, weight_3, gate_t, up_t)
    )
    recv = recv.reshape(2 * rows, width)

    feeds = (core_arg, gate_t, up_t, down_w)
    wide = (half, 3 * rows)
    away, routed = call(
        functools.partial(away_kernel, capacity), "away_partials", [wide, recv.shape], feeds + (recv,), 1
    )
    arrived = pair_permute(away, "core")
    chip_sum = call(keep_kernel, "keep_partials", [wide], feeds + (routed, arrived), 1)[0]

    chip_sum, routed, weight_2 = lax.optimization_barrier((chip_sum, routed, weight_2))

    piece = (half // n_y, 3 * rows)
    blocks = lax.all_to_all(chip_sum.reshape((n_y,) + piece), "y", 0, 0, tiled=True)
    mate_routed, weight_2 = swap(which, (routed, weight_2))
    padded = -(-capacity // 16) * 16
    blocks, mate_routed, weight_2 = lax.optimization_barrier((blocks, mate_routed, weight_2))
    sums = jnp.sum(blocks.astype(F32), axis=0)
    gate_sum, up_sum, hid_grad = sums[:, :rows], sums[:, rows : 2 * rows], sums[:, 2 * rows :]
    sig = jax.nn.sigmoid(gate_sum)
    silu = gate_sum * sig
    gate_rows = hid_grad * up_sum * sig * (1.0 + gate_sum * (1.0 - sig))
    acts = jnp.concatenate([gate_rows, hid_grad * silu, silu * up_sum], 1).astype(BF16)

    acts, weight_3 = lax.optimization_barrier((swap(which, acts), weight_3))
    mine = lax.all_to_all(copies(acts, n_y), "y", 0, 0, tiled=True).reshape(wide)
    weight_3 = swap(which, weight_3)
    mate_rows = jnp.concatenate([mate_routed[:rows].T, mate_routed[rows:].T], 0)
    weights = jnp.concatenate([weight_1, weight_2, weight_3], 0)
    mine, weights, mate_rows = lax.optimization_barrier((mine, weights, mate_rows))
    theirs = pair_permute(mine, "core")

    mine_back, place = call(
        functools.partial(mine_back_kernel, capacity),
        "mine_back",
        [(width, rows), (experts * padded, rows)],
        (core_arg, mine, weights),
        1,
        dtype=(F32, BF16),
    )
    slot_back = call(
        back_kernel,
        "slot_back",
        [(experts * padded, width)],
        (core_arg, theirs, weights, mine_back, place),
        1,
    )[0]
    slot_back, routes, sign_bits = lax.optimization_barrier((slot_back, routes, sign_bits))
    returned = lax.all_to_all(slot_back.reshape(experts, padded, width), BITS, 0, 0, tiled=True)
    picker = jnp.take(slot_picker(routes, experts, capacity), partner, axis=0)
    picker = jnp.pad(picker, ((0, 0), (0, padded - capacity), (0, 0))).reshape(experts * padded, tok_count)
    flip_signs = (1 - 2 * lax.dynamic_index_in_dim(sign_bits, mate, 0, keepdims=False)).astype(BF16)
    rotation = sylvester(HBLOCK) * flip_signs[:, None]
    input_grad = call(
        token_kernel,
        "input_grad",
        [(tok_count, width)],
        (picker.T, returned.reshape(experts * padded, width)),
    )[0]

    gate_new, up_new, down_new = call(
        grads_kernel,
        "weight_grads",
        [(width, ff), (width, ff), (ff, width)],
        (core_arg, mine, theirs, mate_rows, rotation),
        1,
        scratch=[pltpu.VMEM((n, rows), BF16) for n in (width, width, half, half, half)],
    )
    return gate_new[None], up_new[None], down_new[None], input_grad


def solution(mesh):
    n_dp = mesh.shape["dp"]
    split = Mesh(mesh.devices.reshape((n_dp // 2, 2) + (2,) * len(BITS)), ("y", "core") + BITS)
    dp = ("y", "core")
    return jax.shard_map(
        shards,
        mesh=split,
        in_specs=(
            P(BITS, dp),
            P(BITS, dp),
            P(BITS, None),
            P(BITS, None),
            P(BITS, dp, None),
            P(BITS, dp, None),
            P(BITS, None, dp),
            P(),
            P(),
        ),
        out_specs=(
            P(BITS, dp, None),
            P(BITS, dp, None),
            P(BITS, None, dp),
            P(BITS, dp),
        ),
        check_vma=False,
    )
```
